128 devices in a mesh: dp: 32 (over x, z_lo, y), tensor: 4 (over z_hi, core).
Axes of the slice: x: 4, y: 4, z: 4 (z_hi: 2, z_lo: 2; z = z_hi * 2 + z_lo), core: 2. Of those that a mesh axis runs over, the one named last changes fastest.
Arguments:
- tokens: bfloat16 [8192, 1536], P(('dp', 'tensor')), may hold values from -6 to 6
- cotangent: bfloat16 [8192, 1536], P(('dp', 'tensor')), may hold values from -6 to 6
- segments: int32 [8192], P('dp'), may hold values from 0 to 7, as said below
- routes: int32 [8192, 6], P('dp'), may hold values from 0 to 7, all different within a row; in each aligned block of 256 rows (0 to 255, 256 to 511, ...) at most 256 rows name the same one
- gate_weights: float32 [8192, 6], P('dp'), may hold values from 0.1 to 0.3
- norm_gain: float32 [1536], replicated, may hold values from 0.5 to 1.5
- w_zx: bfloat16 [1536, 2, 3072], P('dp', None, 'tensor'), may hold values from -0.15625 to 0.15625
- w_bc: bfloat16 [1536, 2, 128], P('dp'), may hold values from -0.15625 to 0.15625
- w_dt: bfloat16 [1536, 48], P('dp', 'tensor'), may hold values from -0.15625 to 0.15625
- conv_x: float32 [4, 3072], replicated, may hold values from -3 to 3
- conv_bc: float32 [4, 2, 128], replicated, may hold values from -3 to 3
- dt_bias: float32 [48], replicated, may hold values from -4 to -1
- a_log: float32 [48], replicated, may hold values from -12 to 1
- d_skip: float32 [48], replicated, may hold values from 0.5 to 1.5
- mix_gain: float32 [3072], replicated, may hold values from 0.5 to 1.5
- w_out: bfloat16 [3072, 1536], P('tensor', 'dp'), may hold values from -0.109375 to 0.109375
- post_gain: float32 [1536], replicated, may hold values from 0.5 to 1.5
- exp_gate: bfloat16 [8, 1536, 512], P(None, 'dp', 'tensor'), may hold values from -0.15625 to 0.15625
- exp_up: bfloat16 [8, 1536, 512], P(None, 'dp', 'tensor'), may hold values from -0.15625 to 0.15625
- exp_down: bfloat16 [8, 512, 1536], P(None, 'tensor', 'dp'), may hold values from -0.25 to 0.25
- sh_gate: bfloat16 [1536, 1024], P('dp', 'tensor'), may hold values from -0.15625 to 0.15625
- sh_up: bfloat16 [1536, 1024], P('dp', 'tensor'), may hold values from -0.15625 to 0.15625
- sh_down: bfloat16 [1024, 1536], P('tensor', 'dp'), may hold values from -0.1875 to 0.1875
Outputs:
- block_out: float32 [8192, 1536], P(('dp', 'tensor'))
- grad_tokens: float32 [8192, 1536], P(('dp', 'tensor'))
- grad_norm_gain: float32 [1536], replicated
- grad_w_zx: float32 [1536, 2, 3072], P('dp', None, 'tensor')
- grad_w_bc: float32 [1536, 2, 128], P('dp')
- grad_w_dt: float32 [1536, 48], P('dp', 'tensor')
- grad_conv_x: float32 [4, 3072], replicated
- grad_conv_bc: float32 [4, 2, 128], replicated
- grad_dt_bias: float32 [48], replicated
- grad_a_log: float32 [48], replicated
- grad_d_skip: float32 [48], replicated
- grad_mix_gain: float32 [3072], replicated
- grad_w_out: float32 [3072, 1536], P('tensor', 'dp')
- grad_post_gain: float32 [1536], replicated
- grad_exp_gate: float32 [8, 1536, 512], P(None, 'dp', 'tensor')
- grad_exp_up: float32 [8, 1536, 512], P(None, 'dp', 'tensor')
- grad_exp_down: float32 [8, 512, 1536], P(None, 'tensor', 'dp')
- grad_sh_gate: float32 [1536, 1024], P('dp', 'tensor')
- grad_sh_up: float32 [1536, 1024], P('dp', 'tensor')
- grad_sh_down: float32 [1024, 1536], P('tensor', 'dp')
The draws below stay inside these ranges and needn't reach their ends.
Inputs may be any that keep to these rules, and one draw needn't show every extreme that they name: `routes`: within the rows of one index of dp (aligned blocks of 256 rows) no expert is named by more than 256 rows, a bound that some block reaches; a row names 6 different experts. `segments`: document numbers never fall along the rows; every number from 0 to 7 has at least one row.
All inputs are finite; a program needn't handle non-finite values.
Results may differ from the reference program's by a relative error of at most 0.018.
Values may be sent and summed in bfloat16 or wider, within the bound.
No kernel may reach another device: no remote copies, remote signals or barrier semaphores. Data moves between devices by JAX's collectives and lax.ppermute only.
A program may use at most 192 MiB of HBM per device.

```python
import math
import jax
import jax.numpy as jnp
import numpy as np
from jax import lax

D = 1536
H = 48
P_SIZE = 64
N = 128
K = 4
FFE = 512
FFS = 1024
E = 8
TOP = 6
TOK_DEV = 256
SCAN_BLOCK = 256
DI = 3072
TOKENS = 8192
LEN = 8192
CAP = 256


def draw_segments(key, part):
    key = jax.random.fold_in(key, 11)
    front_key, back_key = jax.random.split(key)
    spread = TOK_DEV // 2 - 1
    front_cuts = jnp.sort(jax.random.permutation(front_key, spread)[:4] + 1)
    back_cuts = jnp.sort(jax.random.permutation(back_key, spread)[:3] + 1)
    bounds = jnp.concatenate([front_cuts, TOKENS - back_cuts]).astype(jnp.int32)
    positions = jnp.arange(TOKENS, dtype=jnp.int32)
    return jnp.sum((positions[:, None] >= bounds[None, :]).astype(jnp.int32), 1).astype(jnp.int32)


def level_of(stream_key, shape, cuts, low, largest):
    def one(axis_at, shards_of):
        draws = jax.random.uniform(jax.random.fold_in(jax.random.fold_in(stream_key, 6), axis_at), (shards_of,), jnp.float32, low / len(cuts), largest / len(cuts))
        return jnp.repeat(jnp.exp(draws), shape[axis_at] // shards_of).reshape((-1,) + (1,) * (len(shape) - axis_at - 1))

    gain = one(*cuts[0])
    for cut in cuts[1:]:
        gain = gain * one(*cut)
    return gain


def routed_block(own_key, own, number, rows, amount, top, bound, slope):
    order = jax.random.permutation(own_key, amount)
    heavy_load, common = portions_of(amount, rows * top, bound, slope, True), portions_of(amount, rows * top, bound, slope, False)
    places = jnp.arange(amount)

    def named(sizes, offset_by):
        used = int((sizes > 0).sum())
        fixed = max(1, used // 4)
        shifted = fixed + (places - fixed + offset_by * (used - fixed)) % max(1, amount - fixed)
        return jnp.zeros((amount,), jnp.int32).at[order[jnp.where(places < fixed, places, shifted)]].set(jnp.asarray(sizes, jnp.int32))

    sizes = jnp.where(number % 4 == 0, named(heavy_load, number // 4), named(common, number - number // 4 - 1))
    mixed = jax.random.permutation(jax.random.fold_in(own, 3), amount)
    source_of, taker = mixed[0:amount // 2 * 2:2], mixed[1:amount // 2 * 2:2]
    room = jnp.minimum(sizes[source_of] - 1, bound - sizes[taker]) // 2
    room = jnp.where((source_of == order[0]) | (taker == order[0]) | (sizes[taker] == 0), 0, jnp.maximum(room, 0))
    shifted = jax.random.randint(jax.random.fold_in(own, 4), (amount // 2,), 0, 1 << 20) % (room + 1)
    sizes = sizes.at[source_of].add(-shifted).at[taker].add(shifted)
    members = jnp.searchsorted(jnp.cumsum(sizes), jnp.arange(rows * top), side="right").astype(jnp.int32)
    grid = members.reshape(top, rows).T
    grid = grid[jax.random.permutation(jax.random.fold_in(own, 1), rows)]
    offset_by = jax.random.randint(jax.random.fold_in(own, 2), (rows, 1), 0, top)
    return jnp.take_along_axis(grid, (jnp.arange(top)[None, :] + offset_by) % top, axis=1)


def portions_of(amount, total, reach, lean, full):
    loads = [(1 << 20) // math.isqrt(rank ** lean) + 1 for rank in range(1, amount + 1)]
    largest = reach if full else min(reach, max(-(-total // amount), total * loads[0] // sum(loads)))
    least = 1 if total - largest >= amount - 1 else 0
    given, rest = [largest] + [least] * (amount - 1), total - largest - least * (amount - 1)
    while rest > 0:
        movable = [i for i in range(1, amount) if given[i] < largest] or [i for i in range(1, amount) if given[i] < reach]
        whole, left = sum([loads[i] for i in movable]), rest
        for i in movable:
            more = min(reach - given[i], max(1, left * loads[i] // whole), rest)
            given[i] = given[i] + more
            rest = rest - more
    return np.array(given)


def gaussian(key, shape, deviation, bound, cuts=(), kind=jnp.bfloat16):
    entries = jax.random.normal(key, shape, jnp.float32) * deviation
    if len(cuts) > 0:
        entries = level_of(key, shape, cuts, -0.22, 0.18) * entries
    return jnp.clip(entries, min=-bound, max=bound).astype(kind)


def setup_inputs(seed: int = 0) -> dict:
    seeds = jax.random.split(jax.random.key(seed), 24)
    tokens = gaussian(seeds[0], (TOKENS, D), 1.0, 6.0, ((0, 128),))
    cotangent = gaussian(seeds[1], (TOKENS, D), 1.0, 6.0, ((0, 128),))
    segments = draw_segments(jax.random.fold_in(seeds[23], 71), 0)
    routes_keys = jax.random.split(jax.random.fold_in(seeds[3], 1), TOKENS // TOK_DEV)
    routes_turns = jax.random.permutation(jax.random.fold_in(seeds[3], 3), TOKENS // TOK_DEV)
    routes = jax.vmap(lambda own, number: routed_block(jax.random.fold_in(seeds[3], 2), own, number, TOK_DEV, E, TOP, CAP, 1))(routes_keys, routes_turns).reshape((TOKENS, TOP))
    gate_weights = jnp.clip(0.1 + 0.20000001043081284 * jax.random.uniform(seeds[4], (TOKENS, TOP), jnp.float32) ** level_of(seeds[4], (TOKENS, TOP), ((0, 32),), -0.2, 0.2), 0.1, 0.3)
    norm_gain = jnp.clip(1.0 + 0.1 * jax.random.normal(seeds[5], (D,), jnp.float32), 0.5, 1.5)
    w_zx = gaussian(seeds[6], (D, 2, DI), D ** -0.5, 0.15625, ((0, 32), (2, 4)))
    w_bc = gaussian(seeds[7], (D, 2, N), D ** -0.5, 0.15625, ((0, 32),))
    w_dt = gaussian(seeds[8], (D, H), D ** -0.5, 0.15625, ((0, 32), (1, 4)))
    conv_x = gaussian(seeds[9], (K, DI), K ** -0.5, 3.0, (), jnp.float32)
    conv_bc = gaussian(seeds[10], (K, 2, N), K ** -0.5, 3.0, (), jnp.float32)
    dt_bias = jnp.clip(jax.random.uniform(seeds[11], (H,), jnp.float32, -4.0, -1.0), -4.0, -1.0)
    a_log = jnp.clip(jax.random.uniform(seeds[12], (H,), jnp.float32, -12.0, 1.0), -12.0, 1.0)
    d_skip = jnp.clip(jax.random.uniform(seeds[13], (H,), jnp.float32, 0.5, 1.5), 0.5, 1.5)
    mix_gain = jnp.clip(1.0 + 0.1 * jax.random.normal(seeds[14], (DI,), jnp.float32), 0.5, 1.5)
    w_out = gaussian(seeds[15], (DI, D), DI ** -0.5, 0.109375, ((0, 4), (1, 32)))
    post_gain = jnp.clip(1.0 + 0.1 * jax.random.normal(seeds[16], (D,), jnp.float32), 0.5, 1.5)
    exp_gate = gaussian(seeds[17], (E, D, FFE), D ** -0.5, 0.15625, ((1, 32), (2, 4)))
    exp_up = gaussian(seeds[18], (E, D, FFE), D ** -0.5, 0.15625, ((1, 32), (2, 4)))
    exp_down = gaussian(seeds[19], (E, FFE, D), FFE ** -0.5, 0.25, ((1, 4), (2, 32)))
    sh_gate = gaussian(seeds[20], (D, FFS), D ** -0.5, 0.15625, ((0, 32), (1, 4)))
    sh_up = gaussian(seeds[21], (D, FFS), D ** -0.5, 0.15625, ((0, 32), (1, 4)))
    sh_down = gaussian(seeds[22], (FFS, D), FFS ** -0.5, 0.1875, ((0, 4), (1, 32)))
    return dict(tokens=tokens, cotangent=cotangent, segments=segments, routes=routes, gate_weights=gate_weights, norm_gain=norm_gain, w_zx=w_zx, w_bc=w_bc, w_dt=w_dt, conv_x=conv_x, conv_bc=conv_bc, dt_bias=dt_bias, a_log=a_log, d_skip=d_skip, mix_gain=mix_gain, w_out=w_out, post_gain=post_gain, exp_gate=exp_gate, exp_up=exp_up, exp_down=exp_down, sh_gate=sh_gate, sh_up=sh_up, sh_down=sh_down)


eps = 1e-05
highest = lax.Precision.HIGHEST

@jax.custom_vjp
def low(v):
    return lax.optimization_barrier(v.astype(jnp.bfloat16)).astype(jnp.float32)

@jax.custom_vjp
def low_back(v):
    return v

def low_keep(v):
    return (low(v), None)

def low_pass(kept, grad):
    return (grad,)

def back_keep(v):
    return (v, None)

def back_low(kept, grad):
    return (low(grad),)
low.defvjp(low_keep, low_pass)
low_back.defvjp(back_keep, back_low)

def product(left, right):
    return jnp.dot(left, right, precision=highest, preferred_element_type=jnp.float32)

def block_scan(values, b_rows, c_rows, steps_dt, log_decay, resets, skip_gain, carry_start):
    total_rows = values.shape[0]
    head_count = values.shape[1]
    head_dim = values.shape[2]
    state_dim = b_rows.shape[1]
    block_count = total_rows // SCAN_BLOCK

    def block_step(carried, pieces):
        x_blk, b_blk, c_blk, dt_blk, ld_blk, rs_blk = pieces
        cum_log = jnp.cumsum(ld_blk, 0)
        run_ids = jnp.cumsum(rs_blk)
        row_ids = lax.broadcasted_iota(jnp.int32, (SCAN_BLOCK, SCAN_BLOCK), 0)
        col_ids = lax.broadcasted_iota(jnp.int32, (SCAN_BLOCK, SCAN_BLOCK), 1)
        keep_mask = (row_ids >= col_ids) & (run_ids[:, None] == run_ids[None, :])
        gaps = cum_log[:, None, :] - cum_log[None, :, :]
        decays = jnp.exp(jnp.where(keep_mask[:, :, None], gaps, -jnp.inf))
        inner_cb = jnp.dot(c_blk, b_blk.T, precision=highest)
        weights = decays * inner_cb[:, :, None] * dt_blk[None, :, :]
        y_blk = jnp.einsum('ijh,jhp->ihp', weights, x_blk, precision=highest)
        opening = jnp.exp(cum_log) * (run_ids == 0).astype(jnp.float32)[:, None]
        y_blk = y_blk + opening[:, :, None] * jnp.einsum('in,hpn->ihp', c_blk, carried, precision=highest)
        y_blk = y_blk + skip_gain[None, :, None] * x_blk
        last_run = run_ids[SCAN_BLOCK - 1]
        closing = jnp.where((run_ids == last_run)[:, None], jnp.exp(cum_log[SCAN_BLOCK - 1][None, :] - cum_log), 0.0) * dt_blk
        keep_old = jnp.exp(cum_log[SCAN_BLOCK - 1]) * (last_run == 0).astype(jnp.float32)
        updated = carried * keep_old[:, None, None] + jnp.einsum('jh,jhp,jn->hpn', closing, x_blk, b_blk, precision=highest)
        return (updated, y_blk)
    pieces = (values.reshape(block_count, SCAN_BLOCK, head_count, head_dim), b_rows.reshape(block_count, SCAN_BLOCK, state_dim), c_rows.reshape(block_count, SCAN_BLOCK, state_dim), steps_dt.reshape(block_count, SCAN_BLOCK, head_count), log_decay.reshape(block_count, SCAN_BLOCK, head_count), resets.reshape(block_count, SCAN_BLOCK))
    final_state, y_blocks = lax.scan(jax.checkpoint(block_step), carry_start, pieces)
    return (y_blocks.reshape(total_rows, head_count, head_dim), final_state)

def layer(params, rows_in, seg_ids, route_ids, gate_vals):
    norm_gain, w_zx, w_bc, w_dt, conv_x, conv_bc, dt_bias, a_log, d_skip, mix_gain, w_out, post_gain, exp_gate, exp_up, exp_down, sh_gate, sh_up, sh_down = params
    count_rows = rows_in.shape[0]
    scale_in = lax.rsqrt(lax.optimization_barrier(jnp.mean(rows_in * rows_in, -1, keepdims=True)) + eps)
    normed_in = low(rows_in * scale_in * norm_gain)
    proj_zx = low_back(product(normed_in, w_zx.reshape(D, 2 * DI)))
    proj_bc = low_back(product(normed_in, w_bc.reshape(D, 2 * N)))
    proj_dt = low_back(product(normed_in, w_dt))
    gate_z = proj_zx[:, :DI]
    pre_conv = jnp.concatenate([proj_zx[:, DI:], proj_bc], 1)
    pre_ext = jnp.concatenate([jnp.zeros((K - 1, DI + 2 * N), jnp.float32), pre_conv], 0)
    ids_ext = jnp.concatenate([jnp.full((K - 1,), -1, jnp.int32), seg_ids.astype(jnp.int32)])
    conv_all = jnp.concatenate([conv_x, conv_bc.reshape(K, 2 * N)], 1)
    conv_sum = jnp.zeros_like(pre_conv)
    lag_masks = []
    for shift_back in range(K):
        start_row = K - 1 - shift_back
        same_doc = (ids_ext[start_row:start_row + count_rows] == seg_ids.astype(jnp.int32)).astype(jnp.float32)
        lag_masks.append(same_doc)
        conv_sum = conv_sum + conv_all[K - 1 - shift_back][None, :] * pre_ext[start_row:start_row + count_rows] * same_doc[:, None]
    conv_act = jax.nn.silu(conv_sum)
    x_heads = conv_act[:, :DI].reshape(count_rows, H, P_SIZE)
    b_rows = conv_act[:, DI:DI + N]
    c_rows = conv_act[:, DI + N:]
    steps_dt = jax.nn.softplus(proj_dt + dt_bias)
    log_decay = -steps_dt * jnp.exp(a_log)
    doc_resets = 1.0 - lag_masks[1]
    y_heads, final_state = block_scan(x_heads, b_rows, c_rows, steps_dt, log_decay, doc_resets, d_skip, jnp.zeros((H, P_SIZE, N), jnp.float32))
    gated = y_heads.reshape(count_rows, DI) * jax.nn.silu(gate_z)
    scale_mix = lax.rsqrt(lax.optimization_barrier(jnp.mean(gated * gated, -1)) + eps)
    mixer_in = low(gated * mix_gain)
    projected = low_back(product(mixer_in, w_out))
    mixer_out = low_back(scale_mix[:, None] * projected)
    middle = rows_in + mixer_out
    scale_post = lax.rsqrt(lax.optimization_barrier(jnp.mean(middle * middle, -1, keepdims=True)) + eps)
    normed_post = low(middle * scale_post * post_gain)
    sh_pre_g = low_back(product(normed_post, sh_gate))
    sh_pre_u = low_back(product(normed_post, sh_up))
    sh_act = low(jax.nn.silu(sh_pre_g) * sh_pre_u)
    shared_out = product(sh_act, sh_down)
    expert_hot = (route_ids[:, :, None] == jnp.arange(E, dtype=jnp.int32)[None, None, :]).astype(jnp.float32)
    expert_share = lax.optimization_barrier(jnp.sum(gate_vals[:, :, None] * expert_hot, 1))

    def expert_step(running, pieces):
        weight_g, weight_u, weight_d, share_col = pieces
        pre_gate = low_back(product(normed_post, weight_g))
        pre_up = low_back(product(normed_post, weight_u))
        expert_act = low(jax.nn.silu(pre_gate) * pre_up)
        expert_out = low_back(product(expert_act, weight_d))
        return (running + share_col[:, None] * expert_out, None)
    routed, ignored = lax.scan(jax.checkpoint(expert_step), jnp.zeros((count_rows, D), jnp.float32), (exp_gate, exp_up, exp_down, expert_share.T))
    return middle + routed + shared_out

def reference(tokens, cotangent, segments, routes, gate_weights, norm_gain, w_zx, w_bc, w_dt, conv_x, conv_bc, dt_bias, a_log, d_skip, mix_gain, w_out, post_gain, exp_gate, exp_up, exp_down, sh_gate, sh_up, sh_down):
    params = tuple((value.astype(jnp.float32) for value in (norm_gain, w_zx, w_bc, w_dt, conv_x, conv_bc, dt_bias, a_log, d_skip, mix_gain, w_out, post_gain, exp_gate, exp_up, exp_down, sh_gate, sh_up, sh_down)))
    seq_count = TOKENS // LEN

    def per_sequence(totals, pieces):
        rows_in, grads_out, seg_ids, route_ids, gate_vals = pieces
        result, pull = jax.vjp(lambda weights, inputs: layer(weights, inputs, seg_ids, route_ids, gate_vals), params, rows_in)
        grad_params, grad_rows = pull(grads_out)
        return (jax.tree.map(jnp.add, totals, grad_params), (result, grad_rows))
    totals, outputs = lax.scan(per_sequence, jax.tree.map(jnp.zeros_like, params), (tokens.astype(jnp.float32).reshape(seq_count, LEN, D), cotangent.astype(jnp.float32).reshape(seq_count, LEN, D), segments.reshape(seq_count, LEN), routes.reshape(seq_count, LEN, TOP), gate_weights.reshape(seq_count, LEN, TOP)))
    results, grad_rows = outputs
    return (results.reshape(TOKENS, D), grad_rows.reshape(TOKENS, D), totals[0], totals[1], totals[2], totals[3], totals[4], totals[5], totals[6], totals[7], totals[8], totals[9], totals[10], totals[11], totals[12], totals[13], totals[14], totals[15], totals[16], totals[17])
```

```python
import math

import jax
import jax.numpy as jnp
from jax import lax
from jax.experimental import pallas as pl
from jax.experimental.pallas import tpu as pltpu
from jax.sharding import PartitionSpec as P

f32 = jnp.float32
bf16 = jnp.bfloat16
eps = 1e-05
highest = lax.Precision.HIGHEST
LANES = 128
DP_SHAPE = (4, 2, 4)
EDGE = 16
SUB = 8
RAW_LIMIT = 48 * 1024 * 1024
VMEM_SPARE = 12 * 1024 * 1024

NN = (((1,), (0,)), ((), ()))
NT = (((1,), (1,)), ((), ()))
TN = (((0,), (0,)), ((), ()))


def dot(a, b, dims=NN):
    return lax.dot_general(a.astype(bf16), b.astype(bf16), dims, preferred_element_type=f32)


def dot_exact(a, b, dims=NN):
    return lax.dot_general(a, b, dims, precision=highest, preferred_element_type=f32)


def halves(value):
    high = value.astype(bf16)
    return high, (value - high.astype(f32)).astype(bf16)


def dot_left(a, b, dims=NN):
    high, low = halves(a)
    return dot(high, b, dims) + dot(low, b, dims)


def dot_both(a, b, dims=NN):
    a_high, a_low = halves(a)
    b_high, b_low = halves(b)
    return dot(a_high, b_high, dims) + (dot(a_low, b_high, dims) + dot(a_high, b_low, dims))


def from_behind(value, axis, steps):
    count = lax.axis_size(axis)
    leading, last = (max(0, -steps), min(count, count - steps))
    return lax.ppermute(value, axis, [(source, source + steps) for source in range(leading, last)])


def kernel_call(kernel, out_shapes, *args, flops=0, scratch=(), small=(), raw=()):
    moved = sum(a.size * a.dtype.itemsize for a in args)
    moved += sum(s.size * s.dtype.itemsize for s in out_shapes)
    kept = [a for i, a in enumerate(args) if i not in raw and i not in small] + list(out_shapes)
    kept += [s for s in scratch if s.dtype in (f32, bf16)]
    held = sum(math.prod(a.shape) * (4 if a.dtype == f32 else 2) for a in kept)
    spaces = [
        pltpu.SMEM if i in small else pl.ANY if i in raw else pltpu.VMEM for i in range(len(args))
    ]
    return pl.pallas_call(
        kernel,
        out_shape=out_shapes,
        in_specs=[pl.BlockSpec(memory_space=space) for space in spaces],
        scratch_shapes=scratch,
        compiler_params=pltpu.CompilerParams(vmem_limit_bytes=max(held + VMEM_SPARE, RAW_LIMIT if len(raw) > 1 else 0)),
        cost_estimate=pl.CostEstimate(flops=flops, bytes_accessed=moved, transcendentals=0),
    )(*args)


def shape_of(shape, dtype=f32):
    return jax.ShapeDtypeStruct(shape, dtype)


def ids(shape, dim):
    return lax.broadcasted_iota(jnp.int32, shape, dim)


def per_head(columns, pair, rows):
    left = ids((rows, LANES), 1) < LANES // 2
    return jnp.where(left, columns[:, 2 * pair : 2 * pair + 1], columns[:, 2 * pair + 1 : 2 * pair + 2])


def run_info(cum, heads):
    rows = cum.shape[0]
    turned = cum.T
    run_col = cum[:, heads : heads + 1]
    run_row = turned[heads : heads + 1, :]
    keep = (ids((rows, rows), 0) >= ids((rows, rows), 1)) & (run_col == run_row)
    return turned, run_col, run_col[rows - 1 : rows, :], keep


PIECES = 10


def load_blocks(pieces, target, done, here, ranges, shard):
    x_size, z_size, y_size = DP_SHAPE
    x, z, y = here[0], here[1], here[2]
    copies = []
    for half, start, at, width in ranges:
        for index, far in enumerate((0, -1, 1, 2, 2)):
            for block in range(4 if far == 2 else 8):
                place_in = block + 4 * (index == 4)
                near = RING[place_in // 2]
                to_x, to_y = (far, near) if half == 0 else (near, far)
                to_x = lax.rem(x + (to_x + x_size), x_size)
                to_y = lax.rem(y + (to_y + y_size), y_size)
                to_z = lax.rem(z + place_in % 2, z_size)
                row = pl.multiple_of(((to_x * z_size + to_z) * y_size + to_y) * shard, 16)
                copy = pltpu.make_async_copy(
                    pieces[half * 5 + index].at[block, :, pl.ds(start, width)],
                    target.at[pl.ds(row, shard), pl.ds(at, width)],
                    done.at[len(copies)],
                )
                copy.start()
                copies.append(copy)
    return copies


def wait_all(copies):
    for copy in copies:
        copy.wait()


def column_ranges(split, first, last):
    ranges = []
    if first < split:
        ranges.append((0, first, 0, min(last, split) - first))
    if last > split:
        begin = max(first, split)
        ranges.append((1, begin - split, begin - first, last - begin))
    return ranges


def rows_at(index, quarter):
    return pl.ds(pl.multiple_of(index * quarter, quarter), quarter)


def silu_slope(value, sigma):
    return sigma * (1.0 + value * (1.0 - sigma))


def input_rows(quarter, width):
    def kernel(here, own, across, core_own, core_across, gain, rows_out, normed_out, own_out):
        core, pair = here[3], here[4]
        places = (pair * 2 + core, (1 - pair) * 2 + core, pair * 2 + 1 - core, (1 - pair) * 2 + 1 - core)
        for ref, place_at in zip((own, across, core_own, core_across), places, strict=True):
            rows = ref[0:quarter, :]
            value = rows.astype(f32)
            scale = lax.rsqrt(jnp.mean(value * value, -1, keepdims=True) + eps)
            rows_out[rows_at(place_at, quarter), :] = rows
            normed = (value * scale * gain[...]).astype(bf16)
            normed_out[rows_at(place_at, quarter), :] = normed
            if ref is own:
                own_out[...] = normed

    return kernel


def scan_front(heads, inner, state, shard, ranges):
    pairs = heads // 2
    tiles = (inner + 2 * state) // LANES

    def kernel(here, normed, tail, taps, lags, bias, alog, skip, *refs):
        pieces, refs = refs[:PIECES], refs[PIECES:]
        weights_in, proj, y_out, conv_out, cum_out, steps_out, state_out, act, sums, done = refs
        copies = load_blocks(pieces, weights_in, done, here, ranges, shard)
        wait_all(copies)
        columns = weights_in.shape[1]
        wide = 3 * LANES
        for at in range(0, columns, wide):
            part = weights_in[:, at : at + wide]
            proj[0:EDGE, at : at + wide] = dot(tail[...], part)
            proj[EDGE:, at : at + wide] = dot(normed[...], part)
        rows = y_out.shape[0]
        count = taps.shape[0] // 2
        for tile in range(tiles):
            at = tile * LANES
            total = jnp.zeros((rows, LANES), f32)
            for back in range(count):
                source = proj[EDGE - back : EDGE - back + rows, inner + at : inner + at + LANES]
                weight = taps[count - 1 - back : count - back, at : at + LANES]
                total = total + weight * source * lags[:, back : back + 1]
            conv_out[:, at : at + LANES] = total
            act[:, at : at + LANES] = total * jax.nn.sigmoid(total)
        b_rows = act[:, inner : inner + state]
        c_rows = act[:, inner + state : inner + 2 * state]
        raw = proj[EDGE : EDGE + rows, 2 * inner + 2 * state :] + bias[...]
        steps = jnp.maximum(raw, 0.0) + jnp.log1p(jnp.exp(-jnp.abs(raw)))
        lane = ids((rows, LANES), 1)
        reset = 1.0 - lags[:, 1:2]
        logs = jnp.where(lane < heads, -steps * jnp.exp(alog[...]), jnp.where(lane == heads, reset, 0.0))
        lower = (ids((rows, rows), 0) >= ids((rows, rows), 1)).astype(f32)
        cum = dot_exact(lower, logs)
        steps_out[...] = steps
        cum_out[...] = cum
        turned, run_col, last_run, keep = run_info(cum, heads)
        inner_cb = dot_exact(c_rows, b_rows, NT)
        closing = jnp.where(run_col == last_run, jnp.exp(cum[rows - 1 : rows, :] - cum), 0.0)
        left = ids((rows, LANES), 1) < LANES // 2
        for pair in range(pairs):
            at = pair * LANES
            x_pair = act[:, at : at + LANES]
            scaled = x_pair * per_head(steps, pair, rows)
            parts = []
            for head in (2 * pair, 2 * pair + 1):
                gaps = cum[:, head : head + 1] - turned[head : head + 1, :]
                weights = jnp.exp(jnp.where(keep, gaps, -jnp.inf)) * inner_cb
                parts.append(dot_both(weights, scaled))
            y_out[:, at : at + LANES] = (
                jnp.where(left, parts[0], parts[1]) + skip[:, at : at + LANES] * x_pair
            )
            sums[at : at + LANES, :] = dot_both(scaled * per_head(closing, pair, rows), b_rows, TN)
        last = cum[rows - 1 : rows, :]
        fill_states(state_out, sums, jnp.where(last_run == 0.0, jnp.exp(last), 0.0), heads)

    return kernel


def fill_states(out, sums, keep, heads):
    blocks, size = out.shape[0], sums.shape[0] // out.shape[0]
    head_rows = sums.shape[0] // heads
    row_head = (ids((blocks, LANES), 0) * size + ids((blocks, LANES), 1)) // head_rows
    table = jnp.zeros((blocks, LANES), f32)
    for head in range(heads):
        table = jnp.where(row_head == head, keep[:, head : head + 1], table)
    for block in range(blocks):
        out[block, 0:size, :] = sums[block * size : (block + 1) * size, :]
        out[block, size : size + SUB, :] = jnp.broadcast_to(table[block : block + 1, :], (SUB, LANES))


def gate_front(heads, inner, state, shard, ranges):
    pairs = heads // 2

    def kernel(here, y_in, proj, conv, cum_in, entering, gain, *refs):
        pieces, refs = refs[:PIECES], refs[PIECES:]
        w_back, y_out, mixed_out, mine_out, theirs_out, mixed_low, partial, done = refs
        copies = load_blocks(pieces, w_back, done, here, ranges, shard)
        rows = y_in.shape[0]
        quarter = rows // 4
        width = partial.shape[1] - LANES
        core = here[3]
        cum = cum_in[...]
        opening = jnp.where(cum[:, heads : heads + 1] == 0.0, jnp.exp(cum), 0.0)
        c_conv = conv[:, inner + state : inner + 2 * state]
        c_rows = c_conv * jax.nn.sigmoid(c_conv)
        squares = jnp.zeros((rows, LANES), f32)
        for pair in range(pairs):
            at = pair * LANES
            y_pair = y_in[:, at : at + LANES] + per_head(opening, pair, rows) * dot_both(
                c_rows, entering[at : at + LANES, :], NT
            )
            z_pair = proj[EDGE : EDGE + rows, at : at + LANES]
            gated = y_pair * z_pair * jax.nn.sigmoid(z_pair)
            y_out[:, at : at + LANES] = y_pair
            high, low = halves(gated * gain[:, at : at + LANES])
            mixed_out[:, at : at + LANES] = high
            mixed_low[:, at : at + LANES] = low
            squares = squares + gated * gated
        total = jnp.sum(squares, 1, keepdims=True)
        partial[:, width:] = jnp.broadcast_to(total, (rows, LANES))
        wait_all(copies)
        wide = 2 * LANES
        for at in range(0, width, wide):
            part = w_back[at : at + wide, :]
            partial[:, at : at + wide] = dot(mixed_out[...], part, NT) + dot(mixed_low[...], part, NT)
        for half in range(2):
            to = slice(half * quarter, (half + 1) * quarter)
            mine_out[to, :] = partial[rows_at(2 * half + core, quarter), :]
            theirs_out[to, :] = partial[rows_at(2 * half + 1 - core, quarter), :]

    return kernel


def core_sum(width):
    def kernel(mine, theirs, sum_out, sent_out):
        total = mine[...] + theirs[...]
        sum_out[...] = total[:, :width]
        sent_out[:, :width] = total[:, :width].astype(bf16)
        squares = total[:, width : width + 1]
        high = squares.astype(bf16).astype(f32)
        lane = ids((total.shape[0], LANES), 1)
        sent_out[:, width:] = jnp.where(lane == 0, high, jnp.where(lane == 1, squares - high, 0.0)).astype(bf16)

    return kernel


def middle_rows(quarter, width, inner_total):
    def kernel(here, sent, got, own, across, gain, middle_out, post_out, scales_out):
        pair = here[4]
        total = sent[...].astype(f32) + got[...].astype(f32)
        squares = total[:, width : width + 1] + total[:, width + 1 : width + 2]
        scale_mix = lax.rsqrt(squares / inner_total + eps)
        middle_out[rows_at(pair, quarter), :] = own[0:quarter, :].astype(f32)
        middle_out[rows_at(1 - pair, quarter), :] = across[0:quarter, :].astype(f32)
        middle = middle_out[...] + scale_mix * total[:, :width]
        middle_out[...] = middle
        scale = lax.rsqrt(jnp.mean(middle * middle, -1, keepdims=True) + eps)
        post_out[...] = (middle * scale * gain[...]).astype(bf16)
        lane = ids((2 * quarter, LANES), 1)
        scales_out[...] = jnp.where(lane == 0, scale_mix, scale)

    return kernel


def experts_both(quarter, hidden, ffe, experts, shard, ranges):
    def kernel(here, post_mine, post_theirs, own, across, core_own, core_across, share, *refs):
        pieces, refs = refs[:PIECES], refs[PIECES:]
        (
            post, cot, act_out, dpre_out, out_mine, out_theirs, dpost_mine, dpost_theirs,
            weights, shares, done,
        ) = refs
        copies = load_blocks(pieces, weights, done, here, ranges, shard)
        core, pair = here[3], here[4]
        half = 2 * quarter
        width = post.shape[1]
        post[0:half, :] = post_mine[...]
        post[half:, :] = post_theirs[...]
        cot[rows_at(pair, quarter), :] = own[quarter:, :]
        cot[rows_at(1 - pair, quarter), :] = across[quarter:, :]
        cot[rows_at(2 + pair, quarter), :] = core_own[quarter:, :]
        cot[rows_at(3 - pair, quarter), :] = core_across[quarter:, :]
        for index in range(2):
            shares[index * quarter : (index + 1) * quarter, :] = share[rows_at(2 * index + core, quarter), :]
            shares[half + index * quarter : half + (index + 1) * quarter, :] = share[
                rows_at(2 * index + 1 - core, quarter), :
            ]
        wait_all(copies)
        wide = 2 * LANES
        left = ids((2 * half, wide), 1) < ffe
        for at in range(0, hidden, wide):
            gate = dot(post[...], weights[:, at : at + wide])
            up = dot(post[...], weights[:, hidden + at : hidden + at + wide])
            d_act = dot(cot[...], weights[:, 2 * hidden + at : 2 * hidden + at + wide])
            sigma = jax.nn.sigmoid(gate)
            silu = gate * sigma
            act = silu * up
            expert = at // ffe
            if expert < experts:
                by = jnp.where(left, shares[:, expert : expert + 1], shares[:, expert + 1 : expert + 2])
                act = act * by
                d_act = d_act * by
            act_out[:, at : at + wide] = act.astype(bf16)
            dpre_out[:, at : at + wide] = (d_act * up * silu_slope(gate, sigma)).astype(bf16)
            dpre_out[:, hidden + at : hidden + at + wide] = (d_act * silu).astype(bf16)
        for at in range(0, width, wide):
            d_post = dot(dpre_out[...], weights[at : at + wide, : 2 * hidden], NT)
            dpost_mine[:, at : at + wide] = d_post[:half]
            dpost_theirs[:, at : at + wide] = d_post[half:].astype(bf16)
        for at in range(0, width, wide):
            out = dot(act_out[...], weights[at : at + wide, 2 * hidden :], NT)
            out_mine[:, at : at + wide] = out[:half]
            out_theirs[:, at : at + wide] = out[half:].astype(bf16)

    return kernel


def add_round():
    def kernel(mine, theirs, sent_out):
        sent_out[...] = (mine[...] + theirs[...].astype(f32)).astype(bf16)

    return kernel


def add_split(quarter):
    def kernel(here, mine, theirs, own_out, sent_out):
        pair = here[4]
        own = rows_at(pair, quarter)
        away = rows_at(1 - pair, quarter)
        own_out[...] = mine[own, :] + theirs[own, :].astype(f32)
        sent_out[...] = (mine[away, :] + theirs[away, :].astype(f32)).astype(sent_out.dtype)

    return kernel


def middle_back(quarter, width, inner_total):
    def kernel(
        here, sent, got, own, across, middle_in, scales, core_total, pair_sent, gain,
        dmiddle_out, back_out, gain_out,
    ):
        pair = here[4]
        d_post = sent[...].astype(f32) + got[...].astype(f32)
        middle = middle_in[...]
        scale_mix, scale = scales[:, 0:1], scales[:, 1:2]
        gain_out[...] = 0.5 * jnp.sum(d_post * middle * scale, 0, keepdims=True)
        scaled = d_post * gain[...]
        dmiddle_out[rows_at(pair, quarter), :] = own[quarter:, :].astype(f32)
        dmiddle_out[rows_at(1 - pair, quarter), :] = across[quarter:, :].astype(f32)
        d_middle = (
            dmiddle_out[...]
            + scale * scaled
            - middle * (scale * scale * scale) * jnp.mean(scaled * middle, -1, keepdims=True)
        )
        dmiddle_out[...] = d_middle
        d_proj = (scale_mix * d_middle.astype(bf16).astype(f32)).astype(bf16)
        back_out[:, :width] = d_proj
        projected = core_total[...] + pair_sent[:, :width].astype(f32)
        d_scale = jnp.sum(d_proj.astype(f32) * projected, -1, keepdims=True)
        coeff = -d_scale * scale_mix * scale_mix / inner_total
        high = coeff.astype(bf16).astype(f32)
        lane = ids((2 * quarter, LANES), 1)
        back_out[:, width:] = jnp.where(lane == 0, high, jnp.where(lane == 1, coeff - high, 0.0)).astype(bf16)

    return kernel


def gate_back(heads, inner, state):
    pairs = heads // 2

    def kernel(
        here, back_mine, back_theirs, w_back, y_in, proj, conv, cum_in, gain,
        dproj_out, dy_out, dz_out, gain_out, enter_out, sums, factors, d_mixed,
    ):
        rows = y_in.shape[0]
        quarter = rows // 4
        width = dproj_out.shape[1]
        core = here[3]
        for index in range(2):
            part = slice(index * quarter, (index + 1) * quarter)
            for ref, at in ((back_mine, 2 * index + core), (back_theirs, 2 * index + 1 - core)):
                dproj_out[rows_at(at, quarter), :] = ref[part, :width]
                factors[rows_at(at, quarter), :] = ref[part, width:].astype(f32)
        d_mixed[...] = dot(dproj_out[...], w_back[...])
        cum = cum_in[...]
        opening = jnp.where(cum[:, heads : heads + 1] == 0.0, jnp.exp(cum), 0.0)
        c_conv = conv[:, inner + state : inner + 2 * state]
        c_rows = c_conv * jax.nn.sigmoid(c_conv)
        factor = factors[:, 0:1] + factors[:, 1:2]
        for pair in range(pairs):
            at = pair * LANES
            y_pair = y_in[:, at : at + LANES]
            z_pair = proj[EDGE : EDGE + rows, at : at + LANES]
            sigma = jax.nn.sigmoid(z_pair)
            silu = z_pair * sigma
            gated = y_pair * silu
            d_mix = d_mixed[:, at : at + LANES]
            gain_out[:, at : at + LANES] = jnp.sum(d_mix * gated, 0, keepdims=True)
            d_gated = d_mix * gain[:, at : at + LANES] + factor * gated
            dz_out[:, at : at + LANES] = (d_gated * y_pair * silu_slope(z_pair, sigma)).astype(bf16)
            d_y = d_gated * silu
            dy_out[:, at : at + LANES] = d_y
            sums[at : at + LANES, :] = dot_both(d_y * per_head(opening, pair, rows), c_rows, TN)
        last = cum[rows - 1 : rows, :]
        last_run = last[:, heads : heads + 1]
        fill_states(enter_out, sums, jnp.where(last_run == 0.0, jnp.exp(last), 0.0), heads)

    return kernel


def bc_split(quarter, inner):
    def kernel(here, d_bc, tail, mine_out, theirs_out, whole):
        core = here[3]
        last = d_bc.shape[0] - EDGE
        whole[0:last, :] = d_bc[0:last, :]
        whole[last:, :] = d_bc[last:, :] + tail[:, inner:]
        for index in range(2):
            part = slice(index * quarter, (index + 1) * quarter)
            mine_out[part, :] = whole[rows_at(2 * index + core, quarter), :]
            theirs_out[part, :] = whole[rows_at(2 * index + 1 - core, quarter), :]

    return kernel


def bc_back(first, state):
    def kernel(own_sum, got, tokens, win, own_out, rows_out, gain_out, weights, done):
        copy = pltpu.make_async_copy(win.at[:, pl.ds(first, 2 * state)], weights, done)
        copy.start()
        total = (own_sum[...] + got[...]).astype(bf16)
        own_out[...] = total
        value = tokens[...].astype(f32)
        scale = lax.rsqrt(jnp.mean(value * value, -1, keepdims=True) + eps)
        copy.wait()
        rows = dot(total, weights[...], NT)
        rows_out[...] = rows
        gain_out[...] = jnp.sum(rows * value * scale, 0, keepdims=True)

    return kernel


def input_back(quarter, inner, state):
    def kernel(here, d_z, d_x, tail, d_dt, win, rows_in, dall_out, mine_out, theirs_out, gain_out, d_in):
        core = here[3]
        rows, width = rows_in.shape
        dall_out[:, :inner] = d_z[...]
        dall_out[:, inner : 2 * inner] = d_x[...].astype(bf16)
        dall_out[rows - EDGE :, inner : 2 * inner] = (d_x[rows - EDGE :, :] + tail[:, :inner]).astype(bf16)
        dall_out[:, 2 * inner :] = d_dt[...]
        wide = 2 * LANES
        for at in range(0, width, wide):
            d_in[:, at : at + wide] = dot(dall_out[:, : 2 * inner], win[at : at + wide, : 2 * inner], NT) + dot(
                d_dt[...], win[at : at + wide, 2 * inner + 2 * state :], NT
            )
        value = rows_in[...].astype(f32)
        scale = lax.rsqrt(jnp.mean(value * value, -1, keepdims=True) + eps)
        gain_out[...] = jnp.sum(d_in[...] * value * scale, 0, keepdims=True)
        for index in range(2):
            part = slice(index * quarter, (index + 1) * quarter)
            mine_out[part, :] = d_in[rows_at(2 * index + core, quarter), :]
            theirs_out[part, :] = d_in[rows_at(2 * index + 1 - core, quarter), :].astype(bf16)

    return kernel


def input_grad(quarter):
    def kernel(here, own_sum, got, bc_part, tokens, d_middle, gain, grad_out):
        pair = here[4]
        value = tokens[...].astype(f32)
        scale = lax.rsqrt(jnp.mean(value * value, -1, keepdims=True) + eps)
        scaled = (own_sum[...] + got[...].astype(f32) + bc_part[...]) * gain[...]
        grad_out[...] = (
            d_middle[rows_at(pair, quarter), :]
            + scale * scaled
            - value * (scale * scale * scale) * jnp.mean(scaled * value, -1, keepdims=True)
        )

    return kernel


def layer_out(quarter):
    def kernel(here, own_sum, got, middle, out):
        out[...] = middle[rows_at(here[4], quarter), :] + own_sum[...] + got[...].astype(f32)

    return kernel


def scan_back(heads, inner, state):
    pairs = heads // 2
    tiles = (inner + 2 * state) // LANES

    def kernel(
        proj, taps, lags, bias, alog, skip, conv, cum_in, steps_in, dy_in, entering, leaving,
        dx_out, dbc_out, tail_out, ddt_out, conv_grad, head_grad, skip_grad, dact, rowsums, dpre_out,
    ):
        rows = dy_in.shape[0]
        count = taps.shape[0] // 2
        cum = cum_in[...]
        steps = steps_in[...]
        lane = ids((rows, LANES), 1)
        left = lane < LANES // 2
        turned, run_col, last_run, keep = run_info(cum, heads)
        b_conv = conv[:, inner : inner + state]
        c_conv = conv[:, inner + state : inner + 2 * state]
        b_rows = b_conv * jax.nn.sigmoid(b_conv)
        c_rows = c_conv * jax.nn.sigmoid(c_conv)
        inner_cb = dot_exact(c_rows, b_rows, NT)
        last_cum = cum[rows - 1 : rows, :]
        closing = jnp.where(run_col == last_run, jnp.exp(last_cum - cum), 0.0)
        opening = jnp.where(run_col == 0.0, jnp.exp(cum), 0.0)
        keep_old = jnp.where(last_run == 0.0, jnp.exp(last_cum), 0.0)
        d_cb = jnp.zeros((rows, rows), f32)
        d_b = jnp.zeros((rows, state), f32)
        d_c = jnp.zeros((rows, state), f32)
        d_cum = jnp.zeros((rows, LANES), f32)
        d_steps = jnp.zeros((rows, LANES), f32)
        d_open = jnp.zeros((rows, LANES), f32)
        d_close = jnp.zeros((rows, LANES), f32)
        d_keep = jnp.zeros((1, LANES), f32)
        lane_row = ids((1, LANES), 1)
        rowsums[...] = jnp.zeros_like(rowsums)
        for pair in range(pairs):
            at = pair * LANES
            x_conv = conv[:, at : at + LANES]
            x_pair = x_conv * jax.nn.sigmoid(x_conv)
            d_y = dy_in[:, at : at + LANES]
            step_pair = per_head(steps, pair, rows)
            scaled = x_pair * step_pair
            enter_pair = entering[at : at + LANES, :]
            leave_pair = leaving[at : at + LANES, :]
            close_pair = per_head(closing, pair, rows)
            b_leave = dot(b_rows, leave_pair, NT)
            c_enter = dot(c_rows, enter_pair, NT)
            d_b = d_b + dot_both(scaled * close_pair, leave_pair)
            d_c = d_c + dot_both(d_y * per_head(opening, pair, rows), enter_pair)
            close_prod = b_leave * scaled
            open_prod = d_y * c_enter
            keep_prod = enter_pair * leave_pair
            parts = []
            for side, head in ((0, 2 * pair), (1, 2 * pair + 1)):
                mine = left if side == 0 else ~left
                gaps = cum[:, head : head + 1] - turned[head : head + 1, :]
                decay = jnp.exp(jnp.where(keep, gaps, -jnp.inf))
                weights = decay * inner_cb
                d_weights = dot_both(jnp.where(mine, d_y, 0.0), scaled, NT)
                d_cb = d_cb + d_weights * decay
                flow = d_weights * weights
                d_cum = d_cum + jnp.where(lane == head, jnp.sum(flow, 1, keepdims=True), 0.0)
                rowsums[head : head + 1, :] = jnp.sum(flow, 0, keepdims=True)
                parts.append(dot(weights, d_y, TN))
                half = LANES // 2
                kept = jnp.sum(
                    jnp.sum(keep_prod[side * half : side * half + half, :], 0, keepdims=True), 1, keepdims=True
                )
                d_keep = d_keep + jnp.where(lane_row == head, kept, 0.0)
                d_open = d_open + jnp.where(
                    lane == head, jnp.sum(jnp.where(mine, open_prod, 0.0), 1, keepdims=True), 0.0
                )
                d_close = d_close + jnp.where(
                    lane == head, jnp.sum(jnp.where(mine, close_prod, 0.0), 1, keepdims=True), 0.0
                )
            d_scaled = jnp.where(left, parts[0], parts[1]) + close_pair * b_leave
            skip_grad[:, at : at + LANES] = jnp.sum(d_y * x_pair, 0, keepdims=True)
            dact[:, at : at + LANES] = step_pair * d_scaled + skip[:, at : at + LANES] * d_y
            step_prod = d_scaled * x_pair
            for side, head in ((0, 2 * pair), (1, 2 * pair + 1)):
                mine = left if side == 0 else ~left
                d_steps = d_steps + jnp.where(
                    lane == head, jnp.sum(jnp.where(mine, step_prod, 0.0), 1, keepdims=True), 0.0
                )
        dact[:, inner : inner + state] = d_b + dot_both(d_cb, c_rows, TN)
        dact[:, inner + state : inner + 2 * state] = d_c + dot_both(d_cb, b_rows)
        ended = closing * d_close
        d_last = jnp.sum(ended, 0, keepdims=True) + keep_old * d_keep
        d_cum = d_cum - rowsums[...].T + opening * d_open - ended
        d_cum = d_cum + jnp.where(ids((rows, LANES), 0) == rows - 1, d_last, 0.0)
        upper = (ids((rows, rows), 0) <= ids((rows, rows), 1)).astype(f32)
        d_logs = jnp.where(lane < heads, dot_exact(upper, d_cum), 0.0)
        rate = jnp.exp(alog[...])
        raw = proj[EDGE : EDGE + rows, 2 * inner + 2 * state :] + bias[...]
        d_raw = (d_steps - rate * d_logs) * jax.nn.sigmoid(raw)
        ddt_out[...] = d_raw.astype(bf16)
        head_grad[...] = jnp.zeros_like(head_grad)
        head_grad[0:1, :] = jnp.sum(d_raw, 0, keepdims=True)
        head_grad[1:2, :] = -jnp.sum(d_logs * steps, 0, keepdims=True) * rate
        dpre_out[...] = jnp.zeros_like(dpre_out)
        conv_grad[...] = jnp.zeros_like(conv_grad)
        for tile in range(tiles):
            at = tile * LANES
            value = conv[:, at : at + LANES]
            sigma = jax.nn.sigmoid(value)
            d_conv = dact[:, at : at + LANES] * (sigma * (1.0 + value * (1.0 - sigma)))
            for back in range(count):
                tap = count - 1 - back
                masked = d_conv * lags[:, back : back + 1]
                source = proj[EDGE - back : EDGE - back + rows, inner + at : inner + at + LANES]
                conv_grad[tap : tap + 1, at : at + LANES] = jnp.sum(masked * source, 0, keepdims=True)
                dpre_out[EDGE - back : EDGE - back + rows, at : at + LANES] += (
                    taps[tap : tap + 1, at : at + LANES] * masked
                )
        dx_out[...] = dpre_out[EDGE:, :inner]
        dbc_out[...] = dpre_out[EDGE:, inner:]
        tail_out[...] = dpre_out[0:EDGE, :]

    return kernel


def chain_states(reverse, blocks, size):
    def kernel(parts, carried_out):
        factors = parts[:, size, :].T
        carried = jnp.zeros((size, LANES), f32)
        for turn in range(blocks):
            k = blocks - 1 - turn if reverse else turn
            carried_out[k] = carried
            carried = factors[0:size, k : k + 1] * carried + parts[k, 0:size, :]

    return kernel


def exchange_states(sent, size, axis, reverse, wait=()):
    blocks = lax.axis_size(axis)
    parts = after(wait, lax.all_to_all(sent, axis, 0, 0, tiled=True))
    carried = kernel_call(
        chain_states(reverse, blocks, size), [shape_of((blocks, size, LANES))], parts
    )[0]
    back = lax.all_to_all(carried, axis, 0, 0, tiled=True)
    return back.reshape(blocks * size, LANES), carried


def other(value, bit):
    count = lax.axis_size("tensor")
    return lax.ppermute(value, "tensor", [(rank, rank ^ bit) for rank in range(count)])


def after(first, value):
    return lax.optimization_barrier((first, value))[1]


def place():
    x_size, z_size, y_size = DP_SHAPE
    index = lax.axis_index("dp")
    return index // (z_size * y_size), index // y_size % z_size, index % y_size


def shift(value, axis, step):
    x_size, z_size, y_size = DP_SHAPE
    pairs = []
    for x in range(x_size):
        for z in range(z_size):
            for y in range(y_size):
                to_x = (x + step) % x_size if axis == "x" else x
                to_z = (z + step) % z_size if axis == "z" else z
                to_y = (y + step) % y_size if axis == "y" else y
                pairs.append(((x * z_size + z) * y_size + y, (to_x * z_size + to_z) * y_size + to_y))
    return lax.ppermute(value, "dp", pairs)


RING = (0, -1, 1, 2)


def spread(pack, near, split):
    mids = []
    for columns, axis in ((slice(0, split), "y"), (slice(split, None), "x")):
        own = jnp.stack([pack[:, columns], near[:, columns]])
        back, ahead = shift(own, axis, 1), shift(own, axis, -1)
        far = [shift(back[:1], axis, 1), shift(ahead[1:], axis, -1)]
        mids.append((own, back, ahead, *far))
    return mids


def finish(mids):
    return [(mid, shift(mid, axis, 1), shift(mid, axis, -1)) for mid, axis in zip(mids, "xy", strict=True)]


def finish_far(rings):
    pieces = []
    for (mid, back, ahead), axis in zip(rings, "xy", strict=True):
        pieces += [mid, back, ahead, shift(back[:4], axis, 1), shift(ahead[4:], axis, -1)]
    return pieces


SENT = 5


def cut_chunks(outs, rows_of, part):
    own, to_ahead, to_back, ahead_first, back_second = outs
    own[0:part, :] = rows_of(0, 0)
    own[part:, :] = rows_of(0, 1)
    to_ahead[0:part, :] = rows_of(2, 0)
    to_ahead[part:, :] = rows_of(1, 1)
    to_back[0:part, :] = rows_of(2, 1)
    to_back[part:, :] = rows_of(-1, 0)
    ahead_first[...] = rows_of(1, 0)
    back_second[...] = rows_of(-1, 1)


def chunk_shapes(part, widths):
    shapes = []
    for width in widths:
        shapes += [shape_of((2 * part, width), bf16)] * 3 + [shape_of((part, width), bf16)] * 2
    return shapes


def wrapped(index, step):
    return lax.rem(index + (step + 4), 4)


def term_products(plan, shard):
    x_size, z_size, y_size = DP_SHAPE
    part = 4 * shard

    def kernel(here, *refs):
        count = 1 + max(max(lhs, rhs) for terms in plan for lhs, rhs, _, _ in terms)
        arrays, outs, scratch = refs[:count], refs[count : count + 2 * SENT], refs[count + 2 * SENT :]
        x, y = here[0], here[2]
        for half, terms in enumerate(plan):
            product = scratch[half]
            at = 0
            for lhs, rhs, first, last in terms:
                for start in range(first, last, 2 * LANES):
                    stop = min(start + 2 * LANES, last)
                    product[:, at : at + stop - start] = dot(
                        arrays[lhs][...], arrays[rhs][:, start:stop], TN
                    ).astype(bf16)
                    at += stop - start

            def along_x(step, side, product=product):
                row = (wrapped(x, step) * 2 + side) * part
                return product[pl.ds(pl.multiple_of(row, part), part), :]

            def along_y(step, side, product=product):
                groups = range(side * 4, side * 4 + 4)
                rows = [(group * y_size + wrapped(y, step)) * shard for group in groups]
                return jnp.concatenate([product[pl.ds(pl.multiple_of(row, 16), shard), :] for row in rows], 0)

            cut_chunks(outs[half * SENT : (half + 1) * SENT], along_x if half == 0 else along_y, part)

    return kernel


def ring_add(part):
    def kernel(*refs):
        for half in range(2):
            from_back, from_ahead, ahead_first, back_second = refs[4 * half : 4 * half + 4]
            ahead_out, back_out = refs[8 + 2 * half : 10 + 2 * half]
            ahead_out[...] = (ahead_first[...].astype(f32) + from_back[0:part, :].astype(f32)).astype(bf16)
            back_out[...] = (back_second[...].astype(f32) + from_ahead[0:part, :].astype(f32)).astype(bf16)

    return kernel


def ring_totals(refs, part):
    own, from_back, from_ahead, from_back_last, from_ahead_last = refs
    first = own[0:part, :].astype(f32) + from_ahead[part:, :].astype(f32) + from_back_last[...].astype(f32)
    second = own[part:, :].astype(f32) + from_back[part:, :].astype(f32) + from_ahead_last[...].astype(f32)
    return first, second


def ring_fold(shard):
    part = 4 * shard

    def kernel(here, *refs):
        x, y = here[0], here[2]
        outs, scratch = refs[2 * SENT : 4 * SENT], refs[4 * SENT :]
        for half in range(2):
            total = scratch[half]
            total[0:part, :], total[part:, :] = ring_totals(refs[half * SENT : (half + 1) * SENT], part)

            def along_y(step, side, total=total):
                row = side * part + wrapped(y, step) * shard
                return total[pl.ds(pl.multiple_of(row, 16), shard), :].astype(bf16)

            def along_x(step, side, total=total):
                row = (wrapped(x, step) * 2 + side) * shard
                return total[pl.ds(pl.multiple_of(row, 16), shard), :].astype(bf16)

            cut_chunks(outs[half * SENT : (half + 1) * SENT], along_y if half == 0 else along_x, shard)

    return kernel


def ring_end(shard, widths):
    def kernel(here, *refs):
        z = here[1]
        mine_out, sent_out = refs[2 * SENT :]
        at = 0
        for half in range(2):
            first, second = ring_totals(refs[half * SENT : (half + 1) * SENT], shard)
            columns = slice(at, at + widths[half])
            mine_out[:, columns] = jnp.where(z == 0, first, second)
            sent_out[:, columns] = jnp.where(z == 0, second, first).astype(bf16)
            at += widths[half]

    return kernel


def ring_send(chunks, axes):
    arrived, stays = [], []
    for half, axis in enumerate(axes):
        own, to_ahead, to_back, ahead_first, back_second = chunks[half * SENT : (half + 1) * SENT]
        arrived += [shift(to_ahead, axis, 1), shift(to_back, axis, -1)]
        stays.append((own, ahead_first, back_second))
    return arrived, stays


def ring_pass(arrived, stays, plan, axes, part, wait=None):
    terms = []
    for half in range(2):
        terms += [*arrived[2 * half : 2 * half + 2], *stays[half][1:]]
    if wait is not None:
        terms = after(wait, terms)
    shapes = [shape_of((part, width), bf16) for width in widths_of(plan) for _ in range(2)]
    sent = kernel_call(ring_add(part), shapes, *terms)
    results = []
    for half, axis in enumerate(axes):
        last = [shift(sent[2 * half], axis, 1), shift(sent[2 * half + 1], axis, -1)]
        results += [stays[half][0], *arrived[2 * half : 2 * half + 2], *last]
    return results


def widths_of(plan):
    return [sum(last - first for _, _, first, last in terms) for terms in plan]


def scatter_begin(here, plan, arrays, shard):
    part = 4 * shard
    widths = widths_of(plan)
    return kernel_call(
        term_products(plan, shard), chunk_shapes(part, widths), here, *arrays,
        flops=sum(2 * arrays[0].shape[0] * 8 * part * width for width in widths),
        small=(0,),
        scratch=[pltpu.VMEM((8 * part, width), bf16) for width in widths],
    )


def scatter_fold(here, results, plan, shard):
    widths = widths_of(plan)
    return kernel_call(
        ring_fold(shard), chunk_shapes(shard, widths), here, *results,
        small=(0,),
        scratch=[pltpu.VMEM((8 * shard, width), f32) for width in widths],
    )


def scatter_last(here, results, plan, shard):
    widths = widths_of(plan)
    shape = (shard, sum(widths))
    mine, sent = kernel_call(
        ring_end(shard, widths), [shape_of(shape), shape_of(shape, bf16)], here, *results,
        small=(0,),
    )
    return mine + shift(sent, "z", 1).astype(f32)


EACH = 6


def small_rows(model_dim, inner, state, taps, ranks):
    wide, share = model_dim // LANES, inner // LANES
    sizes = {
        "norm": wide,
        "post": wide,
        "taps": taps * ranks * share,
        "bc": taps * 2 * state // LANES,
        "gain": ranks * share,
        "skip": ranks * share,
        "heads": 2 * ranks,
    }
    rows, at = {}, 0
    for name, size in sizes.items():
        rows[name] = at
        at += size
    return rows


def small_table(layout, inner, state, taps, heads):
    share = inner // LANES

    def kernel(here, norm, norm_bc, post, conv, gain, head, skip, out, table):
        rank = here[4] * 2 + here[3]
        ranks = (layout["skip"] - layout["gain"]) // share

        def lanes(i):
            return slice(i * LANES, (i + 1) * LANES)

        table[...] = jnp.zeros_like(table)
        for i in range(layout["post"] - layout["norm"]):
            table[layout["norm"] + i : layout["norm"] + i + 1, :] = norm[:, lanes(i)] + norm_bc[:, lanes(i)]
            table[layout["post"] + i : layout["post"] + i + 1, :] = post[:, lanes(i)]
        for i in range(share):
            for tap in range(taps):
                row = layout["taps"] + tap * ranks * share + rank * share + i
                table[pl.ds(row, 1), :] = conv[tap : tap + 1, lanes(i)]
            table[pl.ds(layout["gain"] + rank * share + i, 1), :] = gain[:, lanes(i)]
            table[pl.ds(layout["skip"] + rank * share + i, 1), :] = skip[:, lanes(i)]
        wide = 2 * state // LANES
        for tap in range(taps):
            for i in range(wide):
                row = layout["bc"] + tap * wide + i
                table[row : row + 1, :] = conv[tap : tap + 1, lanes(share + i)]
        for i in range(2):
            table[pl.ds(layout["heads"] + i * ranks + rank, 1), :] = head[i : i + 1, :]
        out[...] = jnp.zeros_like(out)
        for block in range(out.shape[0]):
            out[block, 0:EACH, :] = table[block * EACH : (block + 1) * EACH, :]

    return kernel


def small_sum():
    def kernel(parts, out):
        out[...] = jnp.broadcast_to(jnp.sum(parts[...], 0, keepdims=True), out.shape)

    return kernel


def small_out(layout, ranks, inner, state, taps):
    def kernel(parts, norm, post, conv_x, conv_bc, gain, skip, head, table):
        for block in range(parts.shape[0] // ranks):
            total = jnp.sum(parts[block * ranks : (block + 1) * ranks], 0)
            table[block * EACH : (block + 1) * EACH, :] = total[0:EACH, :]

        def spread_out(ref, line, first):
            for i in range(ref.shape[1] // LANES):
                ref[line : line + 1, i * LANES : (i + 1) * LANES] = table[first + i : first + i + 1, :]

        spread_out(norm, 0, layout["norm"])
        spread_out(post, 0, layout["post"])
        spread_out(gain, 0, layout["gain"])
        spread_out(skip, 0, layout["skip"])
        for tap in range(taps):
            spread_out(conv_x, tap, layout["taps"] + tap * (conv_x.shape[1] // LANES))
            spread_out(conv_bc, tap, layout["bc"] + tap * (conv_bc.shape[1] // LANES))
        head[...] = table[layout["heads"] : layout["heads"] + 2 * ranks, :]

    return kernel


def body(
    tokens,
    cotangent,
    segments,
    routes,
    gate_weights,
    norm_gain,
    w_zx,
    w_bc,
    w_dt,
    conv_x,
    conv_bc,
    dt_bias,
    a_log,
    d_skip,
    mix_gain,
    w_out,
    post_gain,
    exp_gate,
    exp_up,
    exp_down,
    sh_gate,
    sh_up,
    sh_down,
):
    tensor_count = lax.axis_size("tensor")
    tensor_rank = lax.axis_index("tensor")
    pair, core = tensor_rank // 2, tensor_rank % 2
    dp_count = lax.axis_size("dp")
    here = jnp.stack([*place(), core, pair]).astype(jnp.int32)
    quarter = tokens.shape[0]
    block_rows = segments.shape[0]
    model_dim = tokens.shape[1]
    shard = w_zx.shape[0]
    inner = w_zx.shape[2]
    heads = w_dt.shape[1]
    head_dim = inner // heads
    state = w_bc.shape[2]
    conv_taps = conv_x.shape[0]
    inner_total = inner * tensor_count
    head_total = heads * tensor_count
    experts = exp_gate.shape[0]
    ffe = exp_gate.shape[2]
    ffs = sh_gate.shape[1]
    hidden = experts * ffe + ffs
    wide_in = 2 * inner + 2 * state + LANES

    own_rows = jnp.concatenate([tokens, cotangent], 0)
    pack_in = jnp.concatenate(
        [
            w_zx.reshape(shard, 2 * inner),
            w_bc.reshape(shard, 2 * state),
            jnp.pad(w_dt, ((0, 0), (0, LANES - heads))),
            w_out.T,
        ],
        1,
    )
    pack_rest = jnp.concatenate(
        [
            exp_gate.transpose(1, 0, 2).reshape(shard, experts * ffe),
            sh_gate,
            exp_up.transpose(1, 0, 2).reshape(shard, experts * ffe),
            sh_up,
            exp_down.transpose(2, 0, 1).reshape(shard, experts * ffe),
            sh_down.T,
        ],
        1,
    )
    in_columns, rest_columns = wide_in, pack_rest.shape[1]
    in_split, rest_split = pack_in.shape[1] // 256 * LANES, rest_columns // 256 * LANES
    in_near, rest_near = shift(pack_in, "z", 1), shift(pack_rest, "z", 1)
    both_splits = zip((pack_in, pack_rest), (in_split, rest_split), strict=True)
    pack = [[part[:, :split], part[:, split:]] for part, split in both_splits]
    both_splits = zip((in_near, rest_near), (in_split, rest_split), strict=True)
    near = [[part[:, :split], part[:, split:]] for part, split in both_splits]
    mids = spread(
        jnp.concatenate([pack[0][0], pack[1][0], pack[0][1], pack[1][1]], 1),
        jnp.concatenate([near[0][0], near[1][0], near[0][1], near[1][1]], 1),
        in_split + rest_split,
    )
    cuts = (in_split, pack_in.shape[1] - in_split)
    in_mids = [
        jnp.concatenate([part[:, :, :cut] for part in parts], 0) for parts, cut in zip(mids, cuts, strict=True)
    ]
    rest_mids = [
        jnp.concatenate([part[:, :, cut:] for part in parts], 0) for parts, cut in zip(mids, cuts, strict=True)
    ]
    in_rings = finish(in_mids)
    core_rows = other(own_rows, 1)
    pair_rows = other(own_rows, 2)
    far_rows = other(pair_rows, 1)
    rows_all, normed_in, normed_own = kernel_call(
        input_rows(quarter, model_dim),
        [shape_of((block_rows, model_dim), bf16)] * 2 + [shape_of((quarter, model_dim), bf16)],
        here, own_rows, pair_rows, core_rows, far_rows, norm_gain[None, :],
        small=(0,),
    )
    tail_rows = from_behind(normed_in[block_rows - EDGE :], "dp", 1)
    in_pieces = finish_far(after(tail_rows, in_rings))
    rest_rings = finish(after(in_pieces, rest_mids))

    head_start = tensor_rank * heads
    chan_start = tensor_rank * inner
    bias_local = lax.dynamic_slice_in_dim(dt_bias, head_start, heads)
    alog_local = lax.dynamic_slice_in_dim(a_log, head_start, heads)
    skip_local = lax.dynamic_slice_in_dim(d_skip, head_start, heads)
    gain_row = lax.dynamic_slice_in_dim(mix_gain, chan_start, inner)[None, :]
    convx_local = lax.dynamic_slice_in_dim(conv_x, chan_start, inner, 1)
    taps = jnp.concatenate([convx_local, conv_bc.reshape(conv_taps, 2 * state)], 1)
    taps = jnp.pad(taps, ((0, conv_taps), (0, 0)))
    bias_row = jnp.pad(bias_local, (0, LANES - heads))[None, :]
    alog_row = jnp.pad(alog_local, (0, LANES - heads))[None, :]
    skip_row = jnp.repeat(skip_local, head_dim)[None, :]

    seg_float = segments.astype(f32)
    tail_ids = from_behind(seg_float[block_rows - EDGE :], "dp", 1)
    ids_ext = jnp.concatenate([tail_ids, seg_float])
    global_rows = lax.axis_index("dp") * block_rows + jnp.arange(block_rows, dtype=jnp.int32)
    lags = [
        (
            (ids_ext[EDGE - back : EDGE - back + block_rows] == seg_float) & (global_rows >= back)
        ).astype(f32)
        for back in range(conv_taps)
    ]
    lags = jnp.pad(jnp.stack(lags, 1), ((0, 0), (0, LANES - conv_taps)))

    scan_flops = 2 * block_rows * block_rows * inner * 2
    size = inner // dp_count
    state_shape = shape_of((dp_count, size + SUB, state))
    win, proj, y_first, conv, cum, steps, state_sum = kernel_call(
        scan_front(heads, inner, state, shard, column_ranges(in_split, 0, in_columns)),
        [
            shape_of((model_dim, in_columns), bf16),
            shape_of((block_rows + EDGE, in_columns)),
            shape_of((block_rows, inner)),
            shape_of((block_rows, inner + 2 * state)),
            shape_of((block_rows, LANES)),
            shape_of((block_rows, LANES)),
            state_shape,
        ],
        here, normed_in, tail_rows, taps, lags, bias_row, alog_row, skip_row, *in_pieces,
        flops=scan_flops + 2 * block_rows * model_dim * in_columns,
        small=(0,),
        raw=range(8, 8 + PIECES),
        scratch=[
            pltpu.VMEM((block_rows, inner + 2 * state), f32),
            pltpu.VMEM((inner, state), f32),
            pltpu.SemaphoreType.DMA((64,)),
        ],
    )
    entering, carried = exchange_states(state_sum, size, "dp", False, [ring[1:] for ring in rest_rings])
    rest_pieces = finish_far(after(carried, rest_rings))
    entering = after(rest_pieces, entering)
    w_back, y_all, mixer_in, mine, theirs = kernel_call(
        gate_front(heads, inner, state, shard, column_ranges(in_split, in_columns, in_columns + inner)),
        [
            shape_of((model_dim, inner), bf16),
            shape_of((block_rows, inner)),
            shape_of((block_rows, inner), bf16),
            shape_of((2 * quarter, model_dim + LANES)),
            shape_of((2 * quarter, model_dim + LANES)),
        ],
        here, y_first, proj, conv, cum, entering, gain_row, *in_pieces,
        flops=scan_flops,
        small=(0,),
        raw=range(7, 7 + PIECES),
        scratch=[
            pltpu.VMEM((block_rows, inner), bf16),
            pltpu.VMEM((block_rows, model_dim + LANES), f32),
            pltpu.SemaphoreType.DMA((64,)),
        ],
    )
    core_total, sent = kernel_call(
        core_sum(model_dim),
        [shape_of((2 * quarter, model_dim)), shape_of((2 * quarter, model_dim + LANES), bf16)],
        mine, other(theirs, 1),
    )
    from_pair = other(sent, 2)
    middle, post_mine, scales = kernel_call(
        middle_rows(quarter, model_dim, inner_total),
        [
            shape_of((2 * quarter, model_dim)),
            shape_of((2 * quarter, model_dim), bf16),
            shape_of((2 * quarter, LANES)),
        ],
        here, sent, from_pair, own_rows, pair_rows, post_gain[None, :],
        small=(0,),
    )
    post_theirs = other(post_mine, 1)
    hot = routes[:, :, None] == jnp.arange(LANES, dtype=jnp.int32)[None, None, :]
    share = jnp.sum(jnp.where(hot, gate_weights[:, :, None], 0.0), 1)
    half_shape = (2 * quarter, model_dim)
    post, cot, act, d_pre, ffn_mine, ffn_theirs, dpost_mine, dpost_theirs = kernel_call(
        experts_both(quarter, hidden, ffe, experts, shard, column_ranges(rest_split, 0, 3 * hidden)),
        [
            shape_of((block_rows, model_dim), bf16),
            shape_of((block_rows, model_dim), bf16),
            shape_of((block_rows, hidden), bf16),
            shape_of((block_rows, 2 * hidden), bf16),
            shape_of(half_shape),
            shape_of(half_shape, bf16),
            shape_of(half_shape),
            shape_of(half_shape, bf16),
        ],
        here, post_mine, post_theirs, own_rows, pair_rows, core_rows, far_rows, share, *rest_pieces,
        flops=12 * block_rows * model_dim * hidden,
        small=(0,),
        raw=range(8, 8 + PIECES),
        scratch=[
            pltpu.VMEM((model_dim, 3 * hidden), bf16),
            pltpu.VMEM((block_rows, LANES), f32),
            pltpu.SemaphoreType.DMA((128,)),
        ],
    )
    ffn_split = (3 * hidden) // 256 * LANES
    ffn_plan = (((0, 2, 0, ffn_split),), ((0, 2, ffn_split, 2 * hidden), (1, 3, 0, hidden)))
    ffn_chunks = scatter_begin(here, ffn_plan, (post, cot, d_pre, act), shard)
    ffn_sent, ffn_terms = ring_send(ffn_chunks, "xy")
    dpost_theirs = after(ffn_chunks, dpost_theirs)
    sent_post = kernel_call(add_round(), [shape_of(half_shape, bf16)], dpost_mine, other(dpost_theirs, 1))[0]
    d_middle, back_mine, grad_post_gain = kernel_call(
        middle_back(quarter, model_dim, inner_total),
        [
            shape_of(half_shape),
            shape_of((2 * quarter, model_dim + LANES), bf16),
            shape_of((1, model_dim)),
        ],
        here, sent_post, other(sent_post, 2), own_rows, pair_rows, middle, scales, core_total, from_pair,
        post_gain[None, :],
        small=(0,),
    )
    back_theirs = other(back_mine, 1)
    d_proj, d_y, d_z, grad_gain, d_enter = kernel_call(
        gate_back(heads, inner, state),
        [
            shape_of((block_rows, model_dim), bf16),
            shape_of((block_rows, inner)),
            shape_of((block_rows, inner), bf16),
            shape_of((1, inner)),
            state_shape,
        ],
        here, back_mine, back_theirs, w_back, y_all, proj, conv, cum, gain_row,
        flops=scan_flops,
        small=(0,),
        scratch=[
            pltpu.VMEM((inner, state), f32),
            pltpu.VMEM((block_rows, LANES), f32),
            pltpu.VMEM((block_rows, inner), f32),
        ],
    )

    ffn_own, ffn_away = kernel_call(
        add_split(quarter),
        [shape_of((quarter, model_dim)), shape_of((quarter, model_dim), bf16)],
        here, ffn_mine, other(ffn_theirs, 1),
        small=(0,),
    )
    block_out = kernel_call(
        layer_out(quarter),
        [shape_of((quarter, model_dim))],
        here, ffn_own, other(ffn_away, 2), middle,
        small=(0,),
    )[0]

    leaving, carried = exchange_states(d_enter, size, "dp", True, ffn_sent)
    ffn_rings = ring_pass(ffn_sent, ffn_terms, ffn_plan, "xy", 4 * shard, carried)
    leaving = after(ffn_rings, leaving)
    d_x, d_bc, tail, d_dt, grad_taps, grad_heads, grad_skip = kernel_call(
        scan_back(heads, inner, state),
        [
            shape_of((block_rows, inner)),
            shape_of((block_rows, 2 * state)),
            shape_of((EDGE, inner + 2 * state)),
            shape_of((block_rows, LANES), bf16),
            shape_of((SUB, inner + 2 * state)),
            shape_of((SUB, LANES)),
            shape_of((1, inner)),
        ],
        proj, taps, lags, bias_row, alog_row, skip_row, conv, cum, steps, d_y, entering, leaving,
        flops=3 * scan_flops,
        scratch=[
            pltpu.VMEM((block_rows, inner + 2 * state), f32),
            pltpu.VMEM((LANES, block_rows), f32),
            pltpu.VMEM((block_rows + EDGE, inner + 2 * state), f32),
        ],
    )
    ffn_chunks = scatter_fold(here, after(d_dt, ffn_rings), ffn_plan, shard)
    tail = after(ffn_chunks, from_behind(tail, "dp", -1))
    ffn_sent, ffn_terms = ring_send(after(tail, ffn_chunks), "yx")
    bc_half = (2 * quarter, 2 * state)
    bc_mine, bc_theirs = kernel_call(
        bc_split(quarter, inner),
        [shape_of(bc_half)] * 2,
        here, d_bc, tail,
        small=(0,),
        scratch=[pltpu.VMEM((block_rows, 2 * state), f32)],
    )
    bc_shape = (quarter, 2 * state)
    bc_sum, bc_sent = kernel_call(
        add_split(quarter), [shape_of(bc_shape)] * 2, here, bc_mine, other(bc_theirs, 1), small=(0,)
    )
    d_all, din_mine, din_theirs, grad_norm = kernel_call(
        input_back(quarter, inner, state),
        [
            shape_of((block_rows, 2 * inner + LANES), bf16),
            shape_of(half_shape),
            shape_of(half_shape, bf16),
            shape_of((1, model_dim)),
        ],
        here, d_z, d_x, tail, d_dt, win, rows_all,
        flops=2 * block_rows * model_dim * in_columns,
        small=(0,),
        scratch=[pltpu.VMEM((block_rows, model_dim), f32)],
    )
    bc_own, din_bc, norm_bc = kernel_call(
        bc_back(2 * inner, state),
        [shape_of(bc_shape, bf16), shape_of((quarter, model_dim)), shape_of((1, model_dim))],
        bc_sum, other(bc_sent, 2), tokens, win,
        raw=(3,),
        scratch=[pltpu.VMEM((model_dim, 2 * state), bf16), pltpu.SemaphoreType.DMA],
    )
    din_own, din_sent = kernel_call(
        add_split(quarter),
        [shape_of((quarter, model_dim)), shape_of((quarter, model_dim), bf16)],
        here, din_mine, other(din_theirs, 1),
        small=(0,),
    )
    grad_tokens = kernel_call(
        input_grad(quarter),
        [shape_of((quarter, model_dim))],
        here, din_own, other(din_sent, 2), din_bc, tokens, d_middle, norm_gain[None, :],
        small=(0,),
    )[0]

    dt_at = 2 * inner
    bc_at = dt_at + LANES
    out_at = bc_at + 2 * state
    mix_split = (out_at + inner) // 256 * LANES
    mix_plan = (
        ((0, 2, 0, mix_split),),
        ((0, 2, mix_split, bc_at), (4, 5, 0, 2 * state), (1, 3, 0, inner)),
    )
    mix_arrays = (normed_in, d_proj, d_all, mixer_in, normed_own, bc_own)
    mix_arrays = after(ffn_sent, (normed_in, d_proj, d_all, mixer_in, normed_own, bc_own))
    mix_chunks = scatter_begin(here, mix_plan, mix_arrays, shard)
    mix_sent, mix_terms = ring_send(mix_chunks, "xy")
    layout = small_rows(model_dim, inner, state, conv_taps, tensor_count)
    table_shape = shape_of((dp_count, SUB, LANES))
    table = kernel_call(
        small_table(layout, inner, state, conv_taps, heads),
        [table_shape],
        here, after(mix_chunks, grad_norm), norm_bc, grad_post_gain, grad_taps, grad_gain, grad_heads, grad_skip,
        small=(0,),
        scratch=[pltpu.VMEM((dp_count * EACH, LANES), f32)],
    )[0]
    table = lax.all_to_all(table, "dp", 0, 0, tiled=True)
    mix_rings = ring_pass(mix_sent, mix_terms, mix_plan, "xy", 4 * shard, table)
    devices = dp_count * tensor_count
    table = kernel_call(small_sum(), [shape_of((devices, SUB, LANES))], after(mix_rings[1], table))[0]
    table = lax.all_to_all(table, ("dp", "tensor"), 0, 0, tiled=True)
    mix_rings = after(table, mix_rings)
    small = kernel_call(
        small_out(layout, tensor_count, inner, state, conv_taps),
        [
            shape_of((1, model_dim)),
            shape_of((1, model_dim)),
            shape_of((conv_taps, inner_total)),
            shape_of((conv_taps, 2 * state)),
            shape_of((1, inner_total)),
            shape_of((1, inner_total)),
            shape_of((2 * tensor_count, LANES)),
        ],
        table,
        scratch=[pltpu.VMEM((dp_count * EACH, LANES), f32)],
    )
    norm_sum, post_sum, taps_x, taps_bc, gain_sum, skip_sum, head_sums = small
    head_sums = head_sums.reshape(2, tensor_count, LANES)[:, :, :heads].reshape(2, -1)
    ffn_rings = ring_pass(ffn_sent, ffn_terms, ffn_plan, "yx", shard, mix_chunks)
    grad_ffn = scatter_last(here, ffn_rings, ffn_plan, shard)
    mix_chunks_last = scatter_fold(here, mix_rings, mix_plan, shard)
    mix_sent, mix_terms = ring_send(mix_chunks_last, "yx")
    mix_rings_last = ring_pass(mix_sent, mix_terms, mix_plan, "yx", shard)
    grad_mix = scatter_last(here, mix_rings_last, mix_plan, shard)
    grad_bc = grad_mix[:, bc_at:out_at]
    grad_bc = grad_bc + other(grad_bc, 1)
    grad_bc = grad_bc + other(grad_bc, 2)
    def experts_of(columns):
        return columns.reshape(shard, experts, ffe)

    wide_e = experts * ffe
    g_gate, g_up, g_down = (
        grad_ffn[:, :hidden],
        grad_ffn[:, hidden : 2 * hidden],
        grad_ffn[:, 2 * hidden :],
    )
    return (
        block_out,
        grad_tokens,
        norm_sum[0],
        grad_mix[:, : 2 * inner].reshape(shard, 2, inner),
        grad_bc.reshape(shard, 2, state),
        grad_mix[:, dt_at : dt_at + heads],
        taps_x,
        taps_bc.reshape(conv_taps, 2, state),
        head_sums[0],
        head_sums[1],
        jnp.sum(skip_sum.reshape(head_total, head_dim), 1),
        gain_sum[0],
        grad_mix[:, out_at:].T,
        post_sum[0],
        experts_of(g_gate[:, :wide_e]).transpose(1, 0, 2),
        experts_of(g_up[:, :wide_e]).transpose(1, 0, 2),
        experts_of(g_down[:, :wide_e]).transpose(1, 2, 0),
        g_gate[:, wide_e:],
        g_up[:, wide_e:],
        g_down[:, wide_e:].T,
    )


def solution(mesh):
    in_specs = (
        P(("dp", "tensor"), None),
        P(("dp", "tensor"), None),
        P("dp"),
        P("dp", None),
        P("dp", None),
        P(),
        P("dp", None, "tensor"),
        P("dp", None, None),
        P("dp", "tensor"),
        P(),
        P(),
        P(),
        P(),
        P(),
        P(),
        P("tensor", "dp"),
        P(),
        P(None, "dp", "tensor"),
        P(None, "dp", "tensor"),
        P(None, "tensor", "dp"),
        P("dp", "tensor"),
        P("dp", "tensor"),
        P("tensor", "dp"),
    )
    out_specs = (
        P(("dp", "tensor"), None),
        P(("dp", "tensor"), None),
        P(),
        P("dp", None, "tensor"),
        P("dp", None, None),
        P("dp", "tensor"),
        P(),
        P(),
        P(),
        P(),
        P(),
        P(),
        P("tensor", "dp"),
        P(),
        P(None, "dp", "tensor"),
        P(None, "dp", "tensor"),
        P(None, "tensor", "dp"),
        P("dp", "tensor"),
        P("dp", "tensor"),
        P("tensor", "dp"),
    )
    return jax.shard_map(body, mesh=mesh, in_specs=in_specs, out_specs=out_specs, check_vma=False)
```

```python
import math

import jax
import jax.numpy as jnp
from jax import lax
from jax.experimental import pallas as pl
from jax.experimental.pallas import tpu as pltpu
from jax.sharding import PartitionSpec as P

f32 = jnp.float32
bf16 = jnp.bfloat16
eps = 1e-05
highest = lax.Precision.HIGHEST
LANES = 128
DP_SHAPE = (4, 2, 4)
EDGE = 16
SUB = 8
RAW_LIMIT = 48 * 1024 * 1024
WHOLE_LIMIT = 62 * 1024 * 1024
RING_SPARE = 4 * 1024 * 1024
VMEM_SPARE = 8 * 1024 * 1024

NN = (((1,), (0,)), ((), ()))
NT = (((1,), (1,)), ((), ()))
TN = (((0,), (0,)), ((), ()))


def dot(a, b, dims=NN):
    return lax.dot_general(a.astype(bf16), b.astype(bf16), dims, preferred_element_type=f32)


def dot_exact(a, b, dims=NN):
    return lax.dot_general(a, b, dims, precision=highest, preferred_element_type=f32)


def halves(value):
    high = value.astype(bf16)
    return high, (value - high.astype(f32)).astype(bf16)


def dot_left(a, b, dims=NN):
    high, low = halves(a)
    return dot(high, b, dims) + dot(low, b, dims)


def dot_both(a, b, dims=NN):
    a_high, a_low = halves(a)
    b_high, b_low = halves(b)
    return dot(a_high, b_high, dims) + (dot(a_low, b_high, dims) + dot(a_high, b_low, dims))


def from_behind(value, axis, steps):
    count = lax.axis_size(axis)
    leading, last = (max(0, -steps), min(count, count - steps))
    return lax.ppermute(value, axis, [(source, source + steps) for source in range(leading, last)])


def kernel_call(kernel, out_shapes, *args, flops=0, scratch=(), small=(), raw=(), whole=False, alone=False, wait=()):
    moved = sum(a.size * a.dtype.itemsize for a in args)
    moved += sum(s.size * s.dtype.itemsize for s in out_shapes)
    kept = [a for i, a in enumerate(args) if i not in raw and i not in small] + list(out_shapes)
    kept += [s for s in scratch if s.dtype in (f32, bf16)]
    held = sum(math.prod(a.shape) * (4 if a.dtype == f32 else 2) for a in kept)
    limit = held + (RING_SPARE if whole else VMEM_SPARE)
    limit = WHOLE_LIMIT if alone else max(limit, RAW_LIMIT if len(raw) > 1 else 0)
    spaces = [
        pltpu.SMEM if i in small else pl.ANY if i in raw else pltpu.VMEM for i in range(len(args))
    ]
    wait = jax.tree.leaves(wait)
    count = len(args)

    def body_of(*refs):
        kernel(*refs[:count], *refs[count + len(wait) :])

    return pl.pallas_call(
        body_of,
        name=kernel.__qualname__.split(".")[0],
        out_shape=out_shapes,
        in_specs=[pl.BlockSpec(memory_space=space) for space in spaces + [pl.ANY] * len(wait)],
        scratch_shapes=scratch,
        compiler_params=pltpu.CompilerParams(vmem_limit_bytes=limit),
        cost_estimate=pl.CostEstimate(flops=flops, bytes_accessed=moved, transcendentals=0),
    )(*args, *wait)


def shape_of(shape, dtype=f32):
    return jax.ShapeDtypeStruct(shape, dtype)


def ids(shape, dim):
    return lax.broadcasted_iota(jnp.int32, shape, dim)


def per_head(columns, pair, rows):
    left = ids((rows, LANES), 1) < LANES // 2
    return jnp.where(left, columns[:, 2 * pair : 2 * pair + 1], columns[:, 2 * pair + 1 : 2 * pair + 2])


def run_info(cum, heads):
    rows = cum.shape[0]
    turned = cum.T
    run_col = cum[:, heads : heads + 1]
    run_row = turned[heads : heads + 1, :]
    keep = (ids((rows, rows), 0) >= ids((rows, rows), 1)) & (run_col == run_row)
    return turned, run_col, run_col[rows - 1 : rows, :], keep


HALVED = ((0, 0, 8), (-1, 0, 8), (1, 0, 8), (2, 0, 4), (2, 4, 4))


def load_blocks(pieces, target, done, here, ranges, shard, form):
    x_size, z_size, y_size = DP_SHAPE
    x, z, y = here[0], here[1], here[2]
    copies = []
    for half, start, at, width in ranges:
        for index, (far, begin, blocks) in enumerate(form):
            for block in range(blocks):
                place_in = begin + block
                near = RING[place_in // 2]
                to_x, to_y = (far, near) if half == 0 else (near, far)
                to_x = lax.rem(x + (to_x + x_size), x_size)
                to_y = lax.rem(y + (to_y + y_size), y_size)
                to_z = lax.rem(z + place_in % 2, z_size)
                row = pl.multiple_of(((to_x * z_size + to_z) * y_size + to_y) * shard, 16)
                copy = pltpu.make_async_copy(
                    pieces[half * len(form) + index].at[block, :, pl.ds(start, width)],
                    target.at[pl.ds(row, shard), pl.ds(at, width)],
                    done.at[len(copies)],
                )
                copy.start()
                copies.append(copy)
    return copies


def wait_all(copies):
    for copy in copies:
        copy.wait()


def column_ranges(split, first, last):
    ranges = []
    if first < split:
        ranges.append((0, first, 0, min(last, split) - first))
    if last > split:
        begin = max(first, split)
        ranges.append((1, begin - split, begin - first, last - begin))
    return ranges


def rows_at(index, quarter):
    return pl.ds(pl.multiple_of(index * quarter, quarter), quarter)


def silu_slope(value, sigma):
    return sigma * (1.0 + value * (1.0 - sigma))


def pack_blocks(plan, width):
    def kernel(*refs):
        ins, out = refs[:-1], refs[-1]
        for arg, lead, first, columns, at in plan:
            if columns % LANES:
                out[:, at : at + LANES] = jnp.zeros((out.shape[0], LANES), bf16)
            ref = ins[arg]
            value = ref[:, first : first + columns] if lead is None else ref[lead, :, first : first + columns]
            out[:, at : at + columns] = value

    return kernel


def pack_plan(args, in_count, in_split, rest_split):
    plan, sizes, at, group = [], [0, 0], 0, 0
    entries = []
    for arg, value in enumerate(args):
        if arg == in_count:
            group, at = 1, 0
        for lead in range(value.shape[0]) if len(value.shape) == 3 else (None,):
            for first in range(0, value.shape[-1], LANES):
                columns = min(LANES, value.shape[-1] - first)
                entries.append((group, at, arg, lead, first, columns))
                at += LANES
        sizes[group] = at
    splits = (in_split, rest_split)
    for group, at, arg, lead, first, columns in entries:
        if at < splits[group]:
            to = at + (in_split if group else 0)
        else:
            to = in_split + rest_split + at - splits[group] + (sizes[0] - in_split if group else 0)
        plan.append((arg, lead, first, columns, to))
    return plan, sum(sizes)


def input_rows(quarter):
    def kernel(here, rows_in, ids_in, gain, normed_out, own_out, tail_out):
        rank = here[4] * 2 + here[3]
        rows, width = rows_in.shape
        value = rows_in[...].astype(f32)
        scale = lax.rsqrt(jnp.mean(value * value, -1, keepdims=True) + eps)
        normed = (value * scale * gain[...]).astype(bf16)
        normed_out[...] = normed
        own_out[...] = normed_out[rows_at(rank, quarter), :]
        tail_out[:, :width] = normed[rows - EDGE :, :]
        tail_out[:, width:] = ids_in[rows - EDGE :, :].astype(bf16)

    return kernel


def scan_front(heads, inner, state, shard, ranges):
    pairs = heads // 2
    tiles = (inner + 2 * state) // LANES

    def kernel(here, normed, tail, taps, ids_in, bias, alog, skip, *refs):
        pieces, refs = refs[: 2 * len(HALVED)], refs[2 * len(HALVED) :]
        proj, lags, y_out, conv_out, cum_out, steps_out, state_out, act, sums, weights_in, ids_ext, done = refs
        copies = load_blocks(pieces, weights_in, done, here, ranges, shard, HALVED)
        columns = weights_in.shape[1]
        wide = 3 * LANES
        rows, depth = normed.shape
        ids_ext[0:EDGE, :] = tail[:, depth:].astype(f32)
        ids_ext[EDGE:, :] = ids_in[...]
        lane = ids((rows, LANES), 1)
        row = ids((rows, LANES), 0)
        no_row_before = here[0] + here[1] + here[2] == 0
        lags[...] = jnp.zeros_like(lags)
        for back in range(taps.shape[0] // 2):
            same = ids_ext[EDGE - back : EDGE - back + rows, :] == ids_in[...]
            same = same & ((row >= back) | jnp.logical_not(no_row_before))
            lags[...] = jnp.where((lane == back) & same, 1.0, lags[...])
        first = len(copies) // 2
        wait_all(copies[:first])
        for at in range(0, columns, wide):
            if at + wide > ranges[0][3] and first:
                wait_all(copies[first:])
                first = 0
            part = weights_in[:, at : at + wide]
            proj[0:EDGE, at : at + wide] = dot(tail[:, :depth], part)
            proj[EDGE:, at : at + wide] = dot(normed[...], part)
        count = taps.shape[0] // 2
        for tile in range(tiles):
            at = tile * LANES
            total = jnp.zeros((rows, LANES), f32)
            for back in range(count):
                source = proj[EDGE - back : EDGE - back + rows, inner + at : inner + at + LANES]
                weight = taps[count - 1 - back : count - back, at : at + LANES]
                total = total + weight * source * lags[:, back : back + 1]
            conv_out[:, at : at + LANES] = total
            act[:, at : at + LANES] = total * jax.nn.sigmoid(total)
        b_rows = act[:, inner : inner + state]
        c_rows = act[:, inner + state : inner + 2 * state]
        raw = proj[EDGE : EDGE + rows, 2 * inner + 2 * state :] + bias[...]
        steps = jnp.maximum(raw, 0.0) + jnp.log1p(jnp.exp(-jnp.abs(raw)))
        reset = 1.0 - lags[:, 1:2]
        logs = jnp.where(lane < heads, -steps * jnp.exp(alog[...]), jnp.where(lane == heads, reset, 0.0))
        lower = (ids((rows, rows), 0) >= ids((rows, rows), 1)).astype(f32)
        cum = dot_exact(lower, logs)
        steps_out[...] = steps
        cum_out[...] = cum
        turned, run_col, last_run, keep = run_info(cum, heads)
        inner_cb = dot_exact(c_rows, b_rows, NT)
        closing = jnp.where(run_col == last_run, jnp.exp(cum[rows - 1 : rows, :] - cum), 0.0)
        left = ids((rows, LANES), 1) < LANES // 2
        for pair in range(pairs):
            at = pair * LANES
            x_pair = act[:, at : at + LANES]
            scaled = x_pair * per_head(steps, pair, rows)
            parts = []
            for head in (2 * pair, 2 * pair + 1):
                gaps = cum[:, head : head + 1] - turned[head : head + 1, :]
                weights = jnp.exp(jnp.where(keep, gaps, -jnp.inf)) * inner_cb
                parts.append(dot_both(weights, scaled))
            y_out[:, at : at + LANES] = (
                jnp.where(left, parts[0], parts[1]) + skip[:, at : at + LANES] * x_pair
            )
            sums[at : at + LANES, :] = dot_both(scaled * per_head(closing, pair, rows), b_rows, TN)
        last = cum[rows - 1 : rows, :]
        fill_states(state_out, sums, jnp.where(last_run == 0.0, jnp.exp(last), 0.0), heads)

    return kernel


def fill_states(out, sums, keep, heads):
    blocks, size = out.shape[0], sums.shape[0] // out.shape[0]
    head_rows = sums.shape[0] // heads
    row_head = (ids((blocks, LANES), 0) * size + ids((blocks, LANES), 1)) // head_rows
    table = jnp.zeros((blocks, LANES), f32)
    for head in range(heads):
        table = jnp.where(row_head == head, keep[:, head : head + 1], table)
    for block in range(blocks):
        out[block, 0:size, :] = sums[block * size : (block + 1) * size, :]
        out[block, size : size + SUB, :] = jnp.broadcast_to(table[block : block + 1, :], (SUB, LANES))


def gate_front(heads, inner, state, shard, ranges):
    pairs = heads // 2

    def kernel(here, y_in, proj, conv, cum_in, entering, gain, *refs):
        pieces, refs = refs[: 2 * len(HALVED)], refs[2 * len(HALVED) :]
        w_back, y_out, mixed_out, mine_out, theirs_out, mixed_low, partial, done = refs
        copies = load_blocks(pieces, w_back, done, here, ranges, shard, HALVED)
        rows = y_in.shape[0]
        quarter = rows // 4
        width = partial.shape[1] - LANES
        core = here[3]
        cum = cum_in[...]
        opening = jnp.where(cum[:, heads : heads + 1] == 0.0, jnp.exp(cum), 0.0)
        c_conv = conv[:, inner + state : inner + 2 * state]
        c_rows = c_conv * jax.nn.sigmoid(c_conv)
        squares = jnp.zeros((rows, LANES), f32)
        for pair in range(pairs):
            at = pair * LANES
            y_pair = y_in[:, at : at + LANES] + per_head(opening, pair, rows) * dot_both(
                c_rows, entering[at : at + LANES, :], NT
            )
            z_pair = proj[EDGE : EDGE + rows, at : at + LANES]
            gated = y_pair * z_pair * jax.nn.sigmoid(z_pair)
            y_out[:, at : at + LANES] = y_pair
            high, low = halves(gated * gain[:, at : at + LANES])
            mixed_out[:, at : at + LANES] = high
            mixed_low[:, at : at + LANES] = low
            squares = squares + gated * gated
        total = jnp.sum(squares, 1, keepdims=True)
        partial[:, width:] = jnp.broadcast_to(total, (rows, LANES))
        wait_all(copies)
        wide = 2 * LANES
        for at in range(0, width, wide):
            part = w_back[at : at + wide, :]
            partial[:, at : at + wide] = dot(mixed_out[...], part, NT) + dot(mixed_low[...], part, NT)
        for half in range(2):
            to = slice(half * quarter, (half + 1) * quarter)
            mine_out[to, :] = partial[rows_at(2 * half + core, quarter), :]
            theirs_out[to, :] = partial[rows_at(2 * half + 1 - core, quarter), :]

    return kernel


def core_sum(width):
    def kernel(mine, theirs, sum_out, sent_out):
        total = mine[...] + theirs[...]
        sum_out[...] = total[:, :width]
        sent_out[:, :width] = total[:, :width].astype(bf16)
        squares = total[:, width : width + 1]
        high = squares.astype(bf16).astype(f32)
        lane = ids((total.shape[0], LANES), 1)
        sent_out[:, width:] = jnp.where(lane == 0, high, jnp.where(lane == 1, squares - high, 0.0)).astype(bf16)

    return kernel


def middle_rows(quarter, width, inner_total):
    def kernel(here, sent, got, rows_in, gain, middle_out, post_out, scales_out):
        core = here[3]
        total = sent[...].astype(f32) + got[...].astype(f32)
        squares = total[:, width : width + 1] + total[:, width + 1 : width + 2]
        scale_mix = lax.rsqrt(squares / inner_total + eps)
        for half in range(2):
            to = slice(half * quarter, (half + 1) * quarter)
            middle_out[to, :] = rows_in[rows_at(2 * half + core, quarter), :].astype(f32)
        middle = middle_out[...] + scale_mix * total[:, :width]
        middle_out[...] = middle
        scale = lax.rsqrt(jnp.mean(middle * middle, -1, keepdims=True) + eps)
        post_out[...] = (middle * scale * gain[...]).astype(bf16)
        lane = ids((2 * quarter, LANES), 1)
        scales_out[...] = jnp.where(lane == 0, scale_mix, scale)

    return kernel


def experts_both(quarter, hidden, ffe, experts, shard, ranges):
    def kernel(here, post_mine, post_theirs, cot_in, share, *refs):
        pieces, refs = refs[: 2 * len(HALVED)], refs[2 * len(HALVED) :]
        (
            post, cot, act_out, dpre_out, out_mine, out_theirs, dpost_mine, dpost_theirs,
            weights, shares, done,
        ) = refs
        copies = load_blocks(pieces, weights, done, here, ranges, shard, HALVED)
        core = here[3]
        half = 2 * quarter
        width = post.shape[1]
        post[0:half, :] = post_mine[...]
        post[half:, :] = post_theirs[...]
        for index in range(2):
            to = slice(index * quarter, (index + 1) * quarter)
            cot[to, :] = cot_in[rows_at(2 * index + core, quarter), :]
            to = slice(half + index * quarter, half + (index + 1) * quarter)
            cot[to, :] = cot_in[rows_at(2 * index + 1 - core, quarter), :]
            shares[index * quarter : (index + 1) * quarter, :] = share[rows_at(2 * index + core, quarter), :]
            shares[half + index * quarter : half + (index + 1) * quarter, :] = share[
                rows_at(2 * index + 1 - core, quarter), :
            ]
        wait_all(copies)
        wide = 2 * LANES
        left = ids((2 * half, wide), 1) < ffe
        for at in range(0, hidden, wide):
            gate = dot(post[...], weights[:, at : at + wide])
            up = dot(post[...], weights[:, hidden + at : hidden + at + wide])
            d_act = dot(cot[...], weights[:, 2 * hidden + at : 2 * hidden + at + wide])
            sigma = jax.nn.sigmoid(gate)
            silu = gate * sigma
            act = silu * up
            expert = at // ffe
            if expert < experts:
                by = jnp.where(left, shares[:, expert : expert + 1], shares[:, expert + 1 : expert + 2])
                act = act * by
                d_act = d_act * by
            act_out[:, at : at + wide] = act.astype(bf16)
            dpre_out[:, at : at + wide] = (d_act * up * silu_slope(gate, sigma)).astype(bf16)
            dpre_out[:, hidden + at : hidden + at + wide] = (d_act * silu).astype(bf16)
        for at in range(0, width, wide):
            d_post = dot(dpre_out[...], weights[at : at + wide, : 2 * hidden], NT)
            dpost_mine[:, at : at + wide] = d_post[:half]
            dpost_theirs[:, at : at + wide] = d_post[half:].astype(bf16)
        for at in range(0, width, wide):
            out = dot(act_out[...], weights[at : at + wide, 2 * hidden :], NT)
            out_mine[:, at : at + wide] = out[:half]
            out_theirs[:, at : at + wide] = out[half:].astype(bf16)

    return kernel


def add_round():
    def kernel(mine, theirs, sent_out):
        sent_out[...] = (mine[...] + theirs[...].astype(f32)).astype(bf16)

    return kernel


def add_split(quarter):
    def kernel(here, mine, theirs, own_out, sent_out):
        pair = here[4]
        own = rows_at(pair, quarter)
        away = rows_at(1 - pair, quarter)
        own_out[...] = mine[own, :] + theirs[own, :].astype(f32)
        sent_out[...] = (mine[away, :] + theirs[away, :].astype(f32)).astype(sent_out.dtype)

    return kernel


def middle_back(quarter, width, inner_total):
    def kernel(
        here, sent, got, cot_in, middle_in, scales, core_total, pair_sent, gain,
        dmiddle_out, back_out, gain_out,
    ):
        core = here[3]
        d_post = sent[...].astype(f32) + got[...].astype(f32)
        middle = middle_in[...]
        scale_mix, scale = scales[:, 0:1], scales[:, 1:2]
        gain_out[...] = 0.5 * jnp.sum(d_post * middle * scale, 0, keepdims=True)
        scaled = d_post * gain[...]
        for half in range(2):
            to = slice(half * quarter, (half + 1) * quarter)
            dmiddle_out[to, :] = cot_in[rows_at(2 * half + core, quarter), :].astype(f32)
        d_middle = (
            dmiddle_out[...]
            + scale * scaled
            - middle * (scale * scale * scale) * jnp.mean(scaled * middle, -1, keepdims=True)
        )
        dmiddle_out[...] = d_middle
        d_proj = (scale_mix * d_middle.astype(bf16).astype(f32)).astype(bf16)
        back_out[:, :width] = d_proj
        projected = core_total[...] + pair_sent[:, :width].astype(f32)
        d_scale = jnp.sum(d_proj.astype(f32) * projected, -1, keepdims=True)
        coeff = -d_scale * scale_mix * scale_mix / inner_total
        high = coeff.astype(bf16).astype(f32)
        lane = ids((2 * quarter, LANES), 1)
        back_out[:, width:] = jnp.where(lane == 0, high, jnp.where(lane == 1, coeff - high, 0.0)).astype(bf16)

    return kernel


def gate_back(heads, inner, state):
    pairs = heads // 2

    def kernel(
        here, back_mine, back_theirs, w_back, y_in, proj, conv, cum_in, gain,
        dproj_out, dy_out, dz_out, gain_out, enter_out, sums, factors, d_mixed,
    ):
        rows = y_in.shape[0]
        quarter = rows // 4
        width = dproj_out.shape[1]
        core = here[3]
        for index in range(2):
            part = slice(index * quarter, (index + 1) * quarter)
            for ref, at in ((back_mine, 2 * index + core), (back_theirs, 2 * index + 1 - core)):
                dproj_out[rows_at(at, quarter), :] = ref[part, :width]
                factors[rows_at(at, quarter), :] = ref[part, width:].astype(f32)
        d_mixed[...] = dot(dproj_out[...], w_back[...])
        cum = cum_in[...]
        opening = jnp.where(cum[:, heads : heads + 1] == 0.0, jnp.exp(cum), 0.0)
        c_conv = conv[:, inner + state : inner + 2 * state]
        c_rows = c_conv * jax.nn.sigmoid(c_conv)
        factor = factors[:, 0:1] + factors[:, 1:2]
        for pair in range(pairs):
            at = pair * LANES
            y_pair = y_in[:, at : at + LANES]
            z_pair = proj[EDGE : EDGE + rows, at : at + LANES]
            sigma = jax.nn.sigmoid(z_pair)
            silu = z_pair * sigma
            gated = y_pair * silu
            d_mix = d_mixed[:, at : at + LANES]
            gain_out[:, at : at + LANES] = jnp.sum(d_mix * gated, 0, keepdims=True)
            d_gated = d_mix * gain[:, at : at + LANES] + factor * gated
            dz_out[:, at : at + LANES] = (d_gated * y_pair * silu_slope(z_pair, sigma)).astype(bf16)
            d_y = d_gated * silu
            dy_out[:, at : at + LANES] = d_y
            sums[at : at + LANES, :] = dot_both(d_y * per_head(opening, pair, rows), c_rows, TN)
        last = cum[rows - 1 : rows, :]
        last_run = last[:, heads : heads + 1]
        fill_states(enter_out, sums, jnp.where(last_run == 0.0, jnp.exp(last), 0.0), heads)

    return kernel


def bc_split(state, inner):
    def kernel(here, d_bc, tail, mine_out, theirs_out, whole):
        core = here[3]
        last = d_bc.shape[0] - EDGE
        whole[0:last, :] = d_bc[0:last, :]
        whole[last:, :] = d_bc[last:, :] + tail[:, inner:]
        first, second = whole[:, :state], whole[:, state:]
        mine_out[...] = jnp.where(core == 0, first, second)
        theirs_out[...] = jnp.where(core == 0, second, first)

    return kernel


def add_exact():
    def kernel(mine, theirs, out):
        out[...] = mine[...] + theirs[...]

    return kernel


def join_grads(inner):
    def prepare(arrays, out):
        d_z, d_x, tail, d_dt, bc_mine, bc_theirs = arrays
        rows = out.shape[0]
        out[:, :inner] = d_z[...]
        out[:, inner : 2 * inner] = d_x[...].astype(bf16)
        out[rows - EDGE :, inner : 2 * inner] = (d_x[rows - EDGE :, :] + tail[:, :inner]).astype(bf16)
        out[:, 2 * inner : 2 * inner + LANES] = d_dt[...]
        out[:, 2 * inner + LANES :] = (bc_mine[...] + bc_theirs[...]).astype(bf16)

    return prepare


def input_back(quarter, inner, state, shard, ranges):
    def kernel(here, d_all, rows_in, *refs):
        pieces, refs = refs[: 2 * len(HALVED)], refs[2 * len(HALVED) :]
        mine_out, theirs_out, gain_out, d_in, win, done = refs
        wait_all(load_blocks(pieces, win, done, here, ranges, shard, HALVED))
        core = here[3]
        rows, width = rows_in.shape
        wide = 2 * LANES
        bc_at = 2 * inner + 2 * state
        d_bc = 0.5 * d_all[:, 2 * inner + LANES :].astype(f32)
        for at in range(0, width, wide):
            part = win[at : at + wide, :]
            w_bc = jnp.where(
                core == 0,
                part[:, 2 * inner : 2 * inner + state].astype(f32),
                part[:, 2 * inner + state : bc_at].astype(f32),
            )
            d_in[:, at : at + wide] = (
                dot(d_all[:, : 2 * inner], part[:, : 2 * inner], NT)
                + dot(d_all[:, 2 * inner : 2 * inner + LANES], part[:, bc_at:], NT)
                + dot(d_bc, w_bc, NT)
            )
        value = rows_in[...].astype(f32)
        scale = lax.rsqrt(jnp.mean(value * value, -1, keepdims=True) + eps)
        gain_out[...] = jnp.sum(d_in[...] * value * scale, 0, keepdims=True)
        for index in range(2):
            part = slice(index * quarter, (index + 1) * quarter)
            mine_out[part, :] = d_in[rows_at(2 * index + core, quarter), :]
            theirs_out[part, :] = d_in[rows_at(2 * index + 1 - core, quarter), :].astype(bf16)

    return kernel


def input_grad(quarter):
    def kernel(here, own_sum, got, tokens, d_middle, gain, grad_out):
        pair = here[4]
        value = tokens[...].astype(f32)
        scale = lax.rsqrt(jnp.mean(value * value, -1, keepdims=True) + eps)
        scaled = (own_sum[...] + got[...].astype(f32)) * gain[...]
        grad_out[...] = (
            d_middle[rows_at(pair, quarter), :]
            + scale * scaled
            - value * (scale * scale * scale) * jnp.mean(scaled * value, -1, keepdims=True)
        )

    return kernel


def layer_out(quarter):
    def kernel(here, own_sum, got, middle, out):
        out[...] = middle[rows_at(here[4], quarter), :] + own_sum[...] + got[...].astype(f32)

    return kernel


def scan_back(heads, inner, state):
    pairs = heads // 2
    tiles = (inner + 2 * state) // LANES

    def kernel(
        proj, taps, lags, bias, alog, skip, conv, cum_in, steps_in, dy_in, entering, leaving,
        dx_out, dbc_out, tail_out, ddt_out, conv_grad, head_grad, skip_grad, dact, rowsums, dpre_out,
    ):
        rows = dy_in.shape[0]
        count = taps.shape[0] // 2
        cum = cum_in[...]
        steps = steps_in[...]
        lane = ids((rows, LANES), 1)
        left = lane < LANES // 2
        turned, run_col, last_run, keep = run_info(cum, heads)
        b_conv = conv[:, inner : inner + state]
        c_conv = conv[:, inner + state : inner + 2 * state]
        b_rows = b_conv * jax.nn.sigmoid(b_conv)
        c_rows = c_conv * jax.nn.sigmoid(c_conv)
        inner_cb = dot_exact(c_rows, b_rows, NT)
        last_cum = cum[rows - 1 : rows, :]
        closing = jnp.where(run_col == last_run, jnp.exp(last_cum - cum), 0.0)
        opening = jnp.where(run_col == 0.0, jnp.exp(cum), 0.0)
        keep_old = jnp.where(last_run == 0.0, jnp.exp(last_cum), 0.0)
        d_cb = jnp.zeros((rows, rows), f32)
        d_b = jnp.zeros((rows, state), f32)
        d_c = jnp.zeros((rows, state), f32)
        d_cum = jnp.zeros((rows, LANES), f32)
        d_steps = jnp.zeros((rows, LANES), f32)
        d_open = jnp.zeros((rows, LANES), f32)
        d_close = jnp.zeros((rows, LANES), f32)
        d_keep = jnp.zeros((1, LANES), f32)
        lane_row = ids((1, LANES), 1)
        rowsums[...] = jnp.zeros_like(rowsums)
        for pair in range(pairs):
            at = pair * LANES
            x_conv = conv[:, at : at + LANES]
            x_pair = x_conv * jax.nn.sigmoid(x_conv)
            d_y = dy_in[:, at : at + LANES]
            step_pair = per_head(steps, pair, rows)
            scaled = x_pair * step_pair
            enter_pair = entering[at : at + LANES, :]
            leave_pair = leaving[at : at + LANES, :]
            close_pair = per_head(closing, pair, rows)
            b_leave = dot(b_rows, leave_pair, NT)
            c_enter = dot(c_rows, enter_pair, NT)
            d_b = d_b + dot_both(scaled * close_pair, leave_pair)
            d_c = d_c + dot_both(d_y * per_head(opening, pair, rows), enter_pair)
            close_prod = b_leave * scaled
            open_prod = d_y * c_enter
            keep_prod = enter_pair * leave_pair
            parts = []
            for side, head in ((0, 2 * pair), (1, 2 * pair + 1)):
                mine = left if side == 0 else ~left
                gaps = cum[:, head : head + 1] - turned[head : head + 1, :]
                decay = jnp.exp(jnp.where(keep, gaps, -jnp.inf))
                weights = decay * inner_cb
                d_weights = dot_both(jnp.where(mine, d_y, 0.0), scaled, NT)
                d_cb = d_cb + d_weights * decay
                flow = d_weights * weights
                d_cum = d_cum + jnp.where(lane == head, jnp.sum(flow, 1, keepdims=True), 0.0)
                rowsums[head : head + 1, :] = jnp.sum(flow, 0, keepdims=True)
                parts.append(dot(weights, d_y, TN))
                half = LANES // 2
                kept = jnp.sum(
                    jnp.sum(keep_prod[side * half : side * half + half, :], 0, keepdims=True), 1, keepdims=True
                )
                d_keep = d_keep + jnp.where(lane_row == head, kept, 0.0)
                d_open = d_open + jnp.where(
                    lane == head, jnp.sum(jnp.where(mine, open_prod, 0.0), 1, keepdims=True), 0.0
                )
                d_close = d_close + jnp.where(
                    lane == head, jnp.sum(jnp.where(mine, close_prod, 0.0), 1, keepdims=True), 0.0
                )
            d_scaled = jnp.where(left, parts[0], parts[1]) + close_pair * b_leave
            skip_grad[:, at : at + LANES] = jnp.sum(d_y * x_pair, 0, keepdims=True)
            dact[:, at : at + LANES] = step_pair * d_scaled + skip[:, at : at + LANES] * d_y
            step_prod = d_scaled * x_pair
            for side, head in ((0, 2 * pair), (1, 2 * pair + 1)):
                mine = left if side == 0 else ~left
                d_steps = d_steps + jnp.where(
                    lane == head, jnp.sum(jnp.where(mine, step_prod, 0.0), 1, keepdims=True), 0.0
                )
        dact[:, inner : inner + state] = d_b + dot_both(d_cb, c_rows, TN)
        dact[:, inner + state : inner + 2 * state] = d_c + dot_both(d_cb, b_rows)
        ended = closing * d_close
        d_last = jnp.sum(ended, 0, keepdims=True) + keep_old * d_keep
        d_cum = d_cum - rowsums[...].T + opening * d_open - ended
        d_cum = d_cum + jnp.where(ids((rows, LANES), 0) == rows - 1, d_last, 0.0)
        upper = (ids((rows, rows), 0) <= ids((rows, rows), 1)).astype(f32)
        d_logs = jnp.where(lane < heads, dot_exact(upper, d_cum), 0.0)
        rate = jnp.exp(alog[...])
        raw = proj[EDGE : EDGE + rows, 2 * inner + 2 * state :] + bias[...]
        d_raw = (d_steps - rate * d_logs) * jax.nn.sigmoid(raw)
        ddt_out[...] = d_raw.astype(bf16)
        head_grad[...] = jnp.zeros_like(head_grad)
        head_grad[0:1, :] = jnp.sum(d_raw, 0, keepdims=True)
        head_grad[1:2, :] = -jnp.sum(d_logs * steps, 0, keepdims=True) * rate
        dpre_out[...] = jnp.zeros_like(dpre_out)
        conv_grad[...] = jnp.zeros_like(conv_grad)
        for tile in range(tiles):
            at = tile * LANES
            value = conv[:, at : at + LANES]
            sigma = jax.nn.sigmoid(value)
            d_conv = dact[:, at : at + LANES] * (sigma * (1.0 + value * (1.0 - sigma)))
            for back in range(count):
                tap = count - 1 - back
                masked = d_conv * lags[:, back : back + 1]
                source = proj[EDGE - back : EDGE - back + rows, inner + at : inner + at + LANES]
                conv_grad[tap : tap + 1, at : at + LANES] = jnp.sum(masked * source, 0, keepdims=True)
                dpre_out[EDGE - back : EDGE - back + rows, at : at + LANES] += (
                    taps[tap : tap + 1, at : at + LANES] * masked
                )
        dx_out[...] = dpre_out[EDGE:, :inner]
        dbc_out[...] = dpre_out[EDGE:, inner:]
        tail_out[...] = dpre_out[0:EDGE, :]

    return kernel


def chain_states(reverse, blocks, size):
    def kernel(parts, carried_out):
        factors = parts[:, size, :].T
        carried = jnp.zeros((size, LANES), f32)
        for turn in range(blocks):
            k = blocks - 1 - turn if reverse else turn
            carried_out[k] = carried
            carried = factors[0:size, k : k + 1] * carried + parts[k, 0:size, :]

    return kernel


def exchange_states(sent, size, axis, reverse, wait=()):
    blocks = lax.axis_size(axis)
    parts = lax.all_to_all(sent, axis, 0, 0, tiled=True)
    carried = kernel_call(
        chain_states(reverse, blocks, size), [shape_of((blocks, size, LANES))], parts, wait=wait
    )[0]
    back = lax.all_to_all(carried, axis, 0, 0, tiled=True)
    return back.reshape(blocks * size, LANES)


def other(value, bit):
    count = lax.axis_size("tensor")
    return lax.ppermute(value, "tensor", [(rank, rank ^ bit) for rank in range(count)])


def place():
    x_size, z_size, y_size = DP_SHAPE
    index = lax.axis_index("dp")
    return index // (z_size * y_size), index // y_size % z_size, index % y_size


def shift(value, axis, step):
    x_size, z_size, y_size = DP_SHAPE
    pairs = []
    for x in range(x_size):
        for z in range(z_size):
            for y in range(y_size):
                to_x = (x + step) % x_size if axis == "x" else x
                to_z = (z + step) % z_size if axis == "z" else z
                to_y = (y + step) % y_size if axis == "y" else y
                pairs.append(((x * z_size + z) * y_size + y, (to_x * z_size + to_z) * y_size + to_y))
    return lax.ppermute(value, "dp", pairs)


RING = (0, -1, 1, 2)


def spread(pack, near, split):
    mids = []
    for columns, axis in ((slice(0, split), "y"), (slice(split, None), "x")):
        own = jnp.stack([pack[:, columns], near[:, columns]])
        back, ahead = shift(own, axis, 1), shift(own, axis, -1)
        far = [shift(back[:1], axis, 1), shift(ahead[1:], axis, -1)]
        mids.append((own, back, ahead, *far))
    return mids


def finish(mids):
    return [(mid, shift(mid, axis, 1), shift(mid, axis, -1)) for mid, axis in zip(mids, "xy", strict=True)]


def join_mids(cuts):
    def kernel(*refs):
        done = refs[-1]
        copies = []
        for half, cut in enumerate(cuts):
            at = 0
            out = refs[10 + half]
            for ref in refs[5 * half : 5 * half + 5]:
                copy = pltpu.make_async_copy(
                    ref.at[:, :, pl.ds(cut, out.shape[2])], out.at[pl.ds(at, ref.shape[0])], done.at[len(copies)]
                )
                copy.start()
                copies.append(copy)
                at += ref.shape[0]
        wait_all(copies)

    return kernel


def cut_far():
    def kernel(*refs):
        done = refs[-1]
        copies = []
        for index in range(4):
            out = refs[4 + index]
            half = out.shape[0]
            copy = pltpu.make_async_copy(refs[index].at[pl.ds((index % 2) * half, half)], out, done.at[index])
            copy.start()
            copies.append(copy)
        wait_all(copies)

    return kernel


def finish_cut(rings, wait):
    arrived = [part for ring in rings for part in ring[1:]]
    return kernel_call(
        cut_far(), [shape_of((part.shape[0] // 2, *part.shape[1:]), bf16) for part in arrived], *arrived,
        raw=range(4),
        scratch=[pltpu.SemaphoreType.DMA((4,))],
        wait=wait,
    )


def finish_far(rings, cut):
    pieces = []
    for half, axis in enumerate("xy"):
        pieces += [*rings[half], shift(cut[2 * half], axis, 1), shift(cut[2 * half + 1], axis, -1)]
    return pieces


SENT = 5


def cut_chunks(outs, rows_of, part):
    own, to_ahead, to_back, ahead_first, back_second = outs
    own[0:part, :] = rows_of(0, 0)
    own[part:, :] = rows_of(0, 1)
    to_ahead[0:part, :] = rows_of(2, 0)
    to_ahead[part:, :] = rows_of(1, 1)
    to_back[0:part, :] = rows_of(2, 1)
    to_back[part:, :] = rows_of(-1, 0)
    ahead_first[...] = rows_of(1, 0)
    back_second[...] = rows_of(-1, 1)


def chunk_shapes(part, widths):
    shapes = []
    for width in widths:
        shapes += [shape_of((2 * part, width), bf16)] * 3 + [shape_of((part, width), bf16)] * 2
    return shapes


def wrapped(index, step):
    return lax.rem(index + (step + 4), 4)


def term_products(plan, shard, prepare=None, joined=0):
    x_size, z_size, y_size = DP_SHAPE
    part = 4 * shard

    def kernel(here, *refs):
        count = len(refs) - 2 * SENT - 2 - (prepare is not None)
        arrays, outs, scratch = list(refs[:count]), refs[count : count + 2 * SENT], refs[-2:]
        if prepare is not None:
            prepare(arrays[count - joined :], refs[-3])
            arrays = [*arrays[: count - joined], refs[-3]]
        x, y = here[0], here[2]
        for half, terms in enumerate(plan):
            product = scratch[half]
            at = 0
            for lhs, rhs, first, last in terms:
                for start in range(first, last, 2 * LANES):
                    stop = min(start + 2 * LANES, last)
                    product[:, at : at + stop - start] = dot(
                        arrays[lhs][...], arrays[rhs][:, start:stop], TN
                    ).astype(bf16)
                    at += stop - start

            def along_x(step, side, product=product):
                row = (wrapped(x, step) * 2 + side) * part
                return product[pl.ds(pl.multiple_of(row, part), part), :]

            def along_y(step, side, product=product):
                groups = range(side * 4, side * 4 + 4)
                rows = [(group * y_size + wrapped(y, step)) * shard for group in groups]
                return jnp.concatenate([product[pl.ds(pl.multiple_of(row, 16), shard), :] for row in rows], 0)

            cut_chunks(outs[half * SENT : (half + 1) * SENT], along_x if half == 0 else along_y, part)

    return kernel


def ring_add(part):
    def kernel(*refs):
        for half in range(2):
            from_back, from_ahead, ahead_first, back_second = refs[4 * half : 4 * half + 4]
            ahead_out, back_out = refs[8 + 2 * half : 10 + 2 * half]
            ahead_out[...] = (ahead_first[...].astype(f32) + from_back[0:part, :].astype(f32)).astype(bf16)
            back_out[...] = (back_second[...].astype(f32) + from_ahead[0:part, :].astype(f32)).astype(bf16)

    return kernel


def ring_totals(refs, part):
    own, from_back, from_ahead, from_back_last, from_ahead_last = refs
    first = own[0:part, :].astype(f32) + from_ahead[part:, :].astype(f32) + from_back_last[...].astype(f32)
    second = own[part:, :].astype(f32) + from_back[part:, :].astype(f32) + from_ahead_last[...].astype(f32)
    return first, second


def ring_total():
    def kernel(*refs):
        for half in range(2):
            out = refs[2 * SENT + half]
            part = out.shape[0] // 2
            first, second = ring_totals(refs[half * SENT : (half + 1) * SENT], part)
            out[0:part, :] = first.astype(bf16)
            out[part:, :] = second.astype(bf16)

    return kernel


def ring_fold(shard):
    part = 4 * shard

    def kernel(here, *refs):
        x, y = here[0], here[2]
        ended, refs = refs[:2], refs[2:]
        outs, scratch = refs[2 * SENT : 4 * SENT], refs[4 * SENT :]
        for half in range(2):
            total = scratch[half]
            wide = ended[half].shape[1]
            total[:, :wide] = ended[half][...].astype(f32)
            total[0:part, wide:], total[part:, wide:] = ring_totals(refs[half * SENT : (half + 1) * SENT], part)

            def along_y(step, side, total=total):
                row = side * part + wrapped(y, step) * shard
                return total[pl.ds(pl.multiple_of(row, 16), shard), :].astype(bf16)

            def along_x(step, side, total=total):
                row = (wrapped(x, step) * 2 + side) * shard
                return total[pl.ds(pl.multiple_of(row, 16), shard), :].astype(bf16)

            cut_chunks(outs[half * SENT : (half + 1) * SENT], along_y if half == 0 else along_x, shard)

    return kernel


def ring_end(shard, widths):
    def kernel(here, *refs):
        z = here[1]
        mine_out, sent_out = refs[2 * SENT :]
        at = 0
        for half in range(2):
            first, second = ring_totals(refs[half * SENT : (half + 1) * SENT], shard)
            columns = slice(at, at + widths[half])
            mine_out[:, columns] = jnp.where(z == 0, first, second)
            sent_out[:, columns] = jnp.where(z == 0, second, first).astype(bf16)
            at += widths[half]

    return kernel


def ring_send(chunks, axes):
    arrived, stays = [], []
    for half, axis in enumerate(axes):
        own, to_ahead, to_back, ahead_first, back_second = chunks[half * SENT : (half + 1) * SENT]
        arrived += [shift(to_ahead, axis, 1), shift(to_back, axis, -1)]
        stays.append((own, ahead_first, back_second))
    return arrived, stays


def ring_added(arrived, stays, widths, part, wait=()):
    terms = []
    for half in range(2):
        terms += [*arrived[2 * half : 2 * half + 2], *stays[half][1:]]
    shapes = [shape_of((part, width), bf16) for width in widths for _ in range(2)]
    return kernel_call(ring_add(part), shapes, *terms, whole=True, wait=wait)


def ring_passed(arrived, stays, sent, axes):
    results = []
    for half, axis in enumerate(axes):
        last = [shift(sent[2 * half], axis, 1), shift(sent[2 * half + 1], axis, -1)]
        results += [stays[half][0], *arrived[2 * half : 2 * half + 2], *last]
    return results


def ring_pass(arrived, stays, widths, axes, part, wait=()):
    return ring_passed(arrived, stays, ring_added(arrived, stays, widths, part, wait), axes)


def widths_of(plan):
    return [sum(last - first for _, _, first, last in terms) for terms in plan]


def scatter_begin(here, plan, arrays, shard, prepare=None, joined=0, columns=0, wait=()):
    part = 4 * shard
    widths = widths_of(plan)
    shapes = chunk_shapes(part, widths)
    if prepare is not None:
        shapes.append(shape_of((arrays[0].shape[0], columns), bf16))
    return kernel_call(
        term_products(plan, shard, prepare, joined), shapes, here, *arrays,
        flops=sum(2 * arrays[0].shape[0] * 8 * part * width for width in widths),
        small=(0,),
        scratch=[pltpu.VMEM((8 * part, width), bf16) for width in widths],
        whole=True,
        wait=wait,
    )


def grad_blocks(plan, shard):
    def kernel(mine, got, *outs):
        for out, entries in zip(outs, plan, strict=True):
            for lead, first, at, columns in entries:
                value = mine[:, at : at + columns] + got[:, at : at + columns].astype(f32)
                if lead is None:
                    out[:, first : first + columns] = value
                else:
                    out[lead, :, first : first + columns] = value

    return kernel


EACH = 6


def small_rows(model_dim, inner, state, taps, ranks):
    wide, share = model_dim // LANES, inner // LANES
    sizes = {
        "norm": wide,
        "post": wide,
        "taps": taps * ranks * share,
        "bc": taps * 2 * state // LANES,
        "gain": ranks * share,
        "skip": ranks * share,
        "heads": 2 * ranks,
    }
    rows, at = {}, 0
    for name, size in sizes.items():
        rows[name] = at
        at += size
    return rows


def small_table(layout, inner, state, taps, heads):
    share = inner // LANES

    def kernel(here, norm, post, conv, gain, head, skip, out, table):
        rank = here[4] * 2 + here[3]
        ranks = (layout["skip"] - layout["gain"]) // share

        def lanes(i):
            return slice(i * LANES, (i + 1) * LANES)

        table[...] = jnp.zeros_like(table)
        for i in range(layout["post"] - layout["norm"]):
            table[layout["norm"] + i : layout["norm"] + i + 1, :] = norm[:, lanes(i)]
            table[layout["post"] + i : layout["post"] + i + 1, :] = post[:, lanes(i)]
        for i in range(share):
            for tap in range(taps):
                row = layout["taps"] + tap * ranks * share + rank * share + i
                table[pl.ds(row, 1), :] = conv[tap : tap + 1, lanes(i)]
            table[pl.ds(layout["gain"] + rank * share + i, 1), :] = gain[:, lanes(i)]
            table[pl.ds(layout["skip"] + rank * share + i, 1), :] = skip[:, lanes(i)]
        wide = 2 * state // LANES
        for tap in range(taps):
            for i in range(wide):
                row = layout["bc"] + tap * wide + i
                table[row : row + 1, :] = conv[tap : tap + 1, lanes(share + i)]
        for i in range(2):
            table[pl.ds(layout["heads"] + i * ranks + rank, 1), :] = head[i : i + 1, :]
        out[...] = jnp.zeros_like(out)
        for block in range(out.shape[0]):
            out[block, 0:EACH, :] = table[block * EACH : (block + 1) * EACH, :]

    return kernel


def small_sum():
    def kernel(parts, out):
        out[...] = jnp.broadcast_to(jnp.sum(parts[...], 0, keepdims=True), out.shape)

    return kernel


def small_out(layout, ranks, inner, state, taps):
    def kernel(parts, norm, post, conv_x, conv_bc, gain, skip, head, table):
        for block in range(parts.shape[0] // ranks):
            total = jnp.sum(parts[block * ranks : (block + 1) * ranks], 0)
            table[block * EACH : (block + 1) * EACH, :] = total[0:EACH, :]

        def spread_out(ref, line, first):
            for i in range(ref.shape[1] // LANES):
                ref[line : line + 1, i * LANES : (i + 1) * LANES] = table[first + i : first + i + 1, :]

        spread_out(norm, 0, layout["norm"])
        spread_out(post, 0, layout["post"])
        spread_out(gain, 0, layout["gain"])
        spread_out(skip, 0, layout["skip"])
        for tap in range(taps):
            spread_out(conv_x, tap, layout["taps"] + tap * (conv_x.shape[1] // LANES))
            spread_out(conv_bc, tap, layout["bc"] + tap * (conv_bc.shape[1] // LANES))
        head[...] = table[layout["heads"] : layout["heads"] + 2 * ranks, :]

    return kernel


def body(
    tokens,
    cotangent,
    segments,
    routes,
    gate_weights,
    norm_gain,
    w_zx,
    w_bc,
    w_dt,
    conv_x,
    conv_bc,
    dt_bias,
    a_log,
    d_skip,
    mix_gain,
    w_out,
    post_gain,
    exp_gate,
    exp_up,
    exp_down,
    sh_gate,
    sh_up,
    sh_down,
):
    tensor_count = lax.axis_size("tensor")
    tensor_rank = lax.axis_index("tensor")
    pair, core = tensor_rank // 2, tensor_rank % 2
    dp_count = lax.axis_size("dp")
    here = jnp.stack([*place(), core, pair]).astype(jnp.int32)
    quarter = tokens.shape[0]
    block_rows = segments.shape[0]
    model_dim = tokens.shape[1]
    shard = w_zx.shape[0]
    inner = w_zx.shape[2]
    heads = w_dt.shape[1]
    head_dim = inner // heads
    state = w_bc.shape[2]
    conv_taps = conv_x.shape[0]
    inner_total = inner * tensor_count
    head_total = heads * tensor_count
    experts = exp_gate.shape[0]
    ffe = exp_gate.shape[2]
    ffs = sh_gate.shape[1]
    hidden = experts * ffe + ffs
    wide_in = 2 * inner + 2 * state + LANES

    shards = [
        w_zx.reshape(shard, 2 * inner),
        w_bc.reshape(shard, 2 * state),
        w_dt,
        w_out.T,
        exp_gate,
        sh_gate,
        exp_up,
        sh_up,
        exp_down.transpose(0, 2, 1),
        sh_down.T,
    ]
    in_columns, mix_columns, rest_columns = wide_in, wide_in + inner, 3 * hidden
    in_split, rest_split = mix_columns // 256 * LANES, rest_columns // 256 * LANES
    plan, pack_columns = pack_plan(shards, 4, in_split, rest_split)
    pack = kernel_call(pack_blocks(plan, pack_columns), [shape_of((shard, pack_columns), bf16)], *shards, alone=True)[0]
    near = shift(pack, "z", 1)
    mids = spread(pack, near, in_split + rest_split)
    cuts = (in_split, mix_columns - in_split)
    in_mids = [
        jnp.concatenate([part[:, :, :cut] for part in parts], 0) for parts, cut in zip(mids, cuts, strict=True)
    ]
    in_rings = finish(in_mids)
    rows_all = lax.all_gather(tokens, "tensor", axis=0, tiled=True)
    cot_all = lax.all_gather(cotangent, "tensor", axis=0, tiled=True)
    seg_lanes = jnp.broadcast_to(segments.astype(f32)[:, None], (block_rows, LANES))
    normed_in, normed_own, tail_sent = kernel_call(
        input_rows(quarter),
        [
            shape_of((block_rows, model_dim), bf16),
            shape_of((quarter, model_dim), bf16),
            shape_of((EDGE, model_dim + LANES), bf16),
        ],
        here, rows_all, seg_lanes, norm_gain[None, :],
        small=(0,),
    )
    tail_rows = from_behind(tail_sent, "dp", 1)
    head_start = tensor_rank * heads
    chan_start = tensor_rank * inner
    bias_local = lax.dynamic_slice_in_dim(dt_bias, head_start, heads)
    alog_local = lax.dynamic_slice_in_dim(a_log, head_start, heads)
    skip_local = lax.dynamic_slice_in_dim(d_skip, head_start, heads)
    gain_row = lax.dynamic_slice_in_dim(mix_gain, chan_start, inner)[None, :]
    convx_local = lax.dynamic_slice_in_dim(conv_x, chan_start, inner, 1)
    taps = jnp.concatenate([convx_local, conv_bc.reshape(conv_taps, 2 * state)], 1)
    taps = jnp.pad(taps, ((0, conv_taps), (0, 0)))
    bias_row = jnp.pad(bias_local, (0, LANES - heads))[None, :]
    alog_row = jnp.pad(alog_local, (0, LANES - heads))[None, :]
    skip_row = jnp.repeat(skip_local, head_dim)[None, :]

    hot = routes[:, :, None] == jnp.arange(LANES, dtype=jnp.int32)[None, None, :]
    share = jnp.sum(jnp.where(hot, gate_weights[:, :, None], 0.0), 1)
    early = (tail_rows, taps, bias_row, alog_row, skip_row, gain_row, share)
    in_pieces = finish_far(in_rings, finish_cut(in_rings, early))
    rest_mids = kernel_call(
        join_mids(cuts),
        [shape_of((8, shard, parts[0].shape[2] - cut), bf16) for parts, cut in zip(mids, cuts, strict=True)],
        *[part for parts in mids for part in parts],
        raw=range(10),
        alone=True,
        scratch=[pltpu.SemaphoreType.DMA((10,))],
        wait=in_pieces,
    )
    rest_rings = finish(rest_mids)
    rest_cut = finish_cut(rest_rings, ())
    rest_pieces = finish_far(rest_rings, rest_cut)

    scan_flops = 2 * block_rows * block_rows * inner * 2
    size = inner // dp_count
    state_shape = shape_of((dp_count, size + SUB, state))
    proj, lags, y_first, conv, cum, steps, state_sum = kernel_call(
        scan_front(heads, inner, state, shard, column_ranges(in_split, 0, in_columns)),
        [
            shape_of((block_rows + EDGE, in_columns)),
            shape_of((block_rows, LANES)),
            shape_of((block_rows, inner)),
            shape_of((block_rows, inner + 2 * state)),
            shape_of((block_rows, LANES)),
            shape_of((block_rows, LANES)),
            state_shape,
        ],
        here, normed_in, tail_rows, taps, seg_lanes, bias_row, alog_row, skip_row, *in_pieces,
        flops=scan_flops + 2 * block_rows * model_dim * in_columns,
        small=(0,),
        raw=range(8, 8 + len(in_pieces)),
        scratch=[
            pltpu.VMEM((block_rows, inner + 2 * state), f32),
            pltpu.VMEM((inner, state), f32),
            pltpu.VMEM((model_dim, in_columns), bf16),
            pltpu.VMEM((block_rows + EDGE, LANES), f32),
            pltpu.SemaphoreType.DMA((64,)),
        ],
    )
    entering = exchange_states(state_sum, size, "dp", False, rest_mids)
    w_back, y_all, mixer_in, mine, theirs = kernel_call(
        gate_front(heads, inner, state, shard, column_ranges(in_split, in_columns, in_columns + inner)),
        [
            shape_of((model_dim, inner), bf16),
            shape_of((block_rows, inner)),
            shape_of((block_rows, inner), bf16),
            shape_of((2 * quarter, model_dim + LANES)),
            shape_of((2 * quarter, model_dim + LANES)),
        ],
        here, y_first, proj, conv, cum, entering, gain_row, *in_pieces,
        flops=scan_flops,
        small=(0,),
        raw=range(7, 7 + len(in_pieces)),
        scratch=[
            pltpu.VMEM((block_rows, inner), bf16),
            pltpu.VMEM((block_rows, model_dim + LANES), f32),
            pltpu.SemaphoreType.DMA((64,)),
        ],
    )
    core_total, sent = kernel_call(
        core_sum(model_dim),
        [shape_of((2 * quarter, model_dim)), shape_of((2 * quarter, model_dim + LANES), bf16)],
        mine, other(theirs, 1),
        wait=[ring[1:] for ring in rest_rings],
    )
    from_pair = other(sent, 2)
    middle, post_mine, scales = kernel_call(
        middle_rows(quarter, model_dim, inner_total),
        [
            shape_of((2 * quarter, model_dim)),
            shape_of((2 * quarter, model_dim), bf16),
            shape_of((2 * quarter, LANES)),
        ],
        here, sent, from_pair, rows_all, post_gain[None, :],
        small=(0,),
    )
    post_theirs = other(post_mine, 1)
    half_shape = (2 * quarter, model_dim)
    post, cot, act, d_pre, ffn_mine, ffn_theirs, dpost_mine, dpost_theirs = kernel_call(
        experts_both(quarter, hidden, ffe, experts, shard, column_ranges(rest_split, 0, 3 * hidden)),
        [
            shape_of((block_rows, model_dim), bf16),
            shape_of((block_rows, model_dim), bf16),
            shape_of((block_rows, hidden), bf16),
            shape_of((block_rows, 2 * hidden), bf16),
            shape_of(half_shape),
            shape_of(half_shape, bf16),
            shape_of(half_shape),
            shape_of(half_shape, bf16),
        ],
        here, post_mine, post_theirs, cot_all, share, *rest_pieces,
        flops=12 * block_rows * model_dim * hidden,
        small=(0,),
        raw=range(5, 5 + len(rest_pieces)),
        scratch=[
            pltpu.VMEM((model_dim, 3 * hidden), bf16),
            pltpu.VMEM((block_rows, LANES), f32),
            pltpu.SemaphoreType.DMA((128,)),
        ],
    )
    ffn_split = (3 * hidden) // 256 * LANES
    ffn_plan = (((0, 2, 0, ffn_split),), ((0, 2, ffn_split, 2 * hidden), (1, 3, 0, hidden)))
    sent_post = kernel_call(add_round(), [shape_of(half_shape, bf16)], dpost_mine, other(dpost_theirs, 1))[0]
    ffn_chunks = scatter_begin(here, ffn_plan, (post, cot, d_pre, act), shard)
    ffn_sent, ffn_terms = ring_send(ffn_chunks, "xy")
    d_middle, back_mine, grad_post_gain = kernel_call(
        middle_back(quarter, model_dim, inner_total),
        [
            shape_of(half_shape),
            shape_of((2 * quarter, model_dim + LANES), bf16),
            shape_of((1, model_dim)),
        ],
        here, sent_post, other(sent_post, 2), cot_all, middle, scales, core_total, from_pair,
        post_gain[None, :],
        small=(0,),
    )
    back_theirs = other(back_mine, 1)
    d_proj, d_y, d_z, grad_gain, d_enter = kernel_call(
        gate_back(heads, inner, state),
        [
            shape_of((block_rows, model_dim), bf16),
            shape_of((block_rows, inner)),
            shape_of((block_rows, inner), bf16),
            shape_of((1, inner)),
            state_shape,
        ],
        here, back_mine, back_theirs, w_back, y_all, proj, conv, cum, gain_row,
        flops=scan_flops,
        small=(0,),
        scratch=[
            pltpu.VMEM((inner, state), f32),
            pltpu.VMEM((block_rows, LANES), f32),
            pltpu.VMEM((block_rows, inner), f32),
        ],
    )

    ffn_own, ffn_away = kernel_call(
        add_split(quarter),
        [shape_of((quarter, model_dim)), shape_of((quarter, model_dim), bf16)],
        here, ffn_mine, other(ffn_theirs, 1),
        small=(0,),
    )
    block_out = kernel_call(
        layer_out(quarter),
        [shape_of((quarter, model_dim))],
        here, ffn_own, other(ffn_away, 2), middle,
        small=(0,),
    )[0]

    leaving = exchange_states(d_enter, size, "dp", True, block_out)
    ffn_widths = widths_of(ffn_plan)
    ffn_added = ring_added(ffn_sent, ffn_terms, ffn_widths, 4 * shard)
    d_x, d_bc, tail, d_dt, grad_taps, grad_heads, grad_skip = kernel_call(
        scan_back(heads, inner, state),
        [
            shape_of((block_rows, inner)),
            shape_of((block_rows, 2 * state)),
            shape_of((EDGE, inner + 2 * state)),
            shape_of((block_rows, LANES), bf16),
            shape_of((SUB, inner + 2 * state)),
            shape_of((SUB, LANES)),
            shape_of((1, inner)),
        ],
        proj, taps, lags, bias_row, alog_row, skip_row, conv, cum, steps, d_y, entering, leaving,
        flops=3 * scan_flops,
        wait=ffn_added,
        scratch=[
            pltpu.VMEM((block_rows, inner + 2 * state), f32),
            pltpu.VMEM((LANES, block_rows), f32),
            pltpu.VMEM((block_rows + EDGE, inner + 2 * state), f32),
        ],
    )
    tail = from_behind(tail, "dp", -1)
    ffn_rings = ring_passed(ffn_sent, ffn_terms, ffn_added, "xy")
    ffn_totals = kernel_call(
        ring_total(), [shape_of((8 * shard, width), bf16) for width in ffn_widths], *ffn_rings, whole=True
    )
    bc_half = shape_of((block_rows, state))
    bc_mine, bc_theirs = kernel_call(
        bc_split(state, inner),
        [bc_half] * 2,
        here, d_bc, tail,
        small=(0,),
        scratch=[pltpu.VMEM((block_rows, 2 * state), f32)],
    )
    bc_sum = kernel_call(add_exact(), [bc_half], bc_mine, other(bc_theirs, 1))[0]
    dt_at = 2 * inner
    bc_at = dt_at + LANES
    out_at = bc_at + state
    mix_split = (out_at + inner) // 256 * LANES
    mix_plan = (((0, 3, 0, mix_split),), ((0, 3, mix_split, out_at), (1, 2, 0, inner)))
    mix_widths = widths_of(mix_plan)
    *mix_chunks, d_all = scatter_begin(
        here, mix_plan,
        (normed_in, d_proj, mixer_in, d_z, d_x, tail, d_dt, bc_sum, other(bc_sum, 2)),
        shard, join_grads(inner), 6, out_at, ffn_totals,
    )
    mix_sent, mix_terms = ring_send(mix_chunks, "xy")
    din_mine, din_theirs, grad_norm = kernel_call(
        input_back(quarter, inner, state, shard, column_ranges(in_split, 0, in_columns)),
        [shape_of(half_shape), shape_of(half_shape, bf16), shape_of((1, model_dim))],
        here, d_all, rows_all, *in_pieces,
        flops=2 * block_rows * model_dim * in_columns,
        small=(0,),
        raw=range(3, 3 + len(in_pieces)),
        scratch=[
            pltpu.VMEM((block_rows, model_dim), f32),
            pltpu.VMEM((model_dim, in_columns), bf16),
            pltpu.SemaphoreType.DMA((64,)),
        ],
    )
    din_own, din_sent = kernel_call(
        add_split(quarter),
        [shape_of((quarter, model_dim)), shape_of((quarter, model_dim), bf16)],
        here, din_mine, other(din_theirs, 1),
        small=(0,),
    )
    grad_tokens = kernel_call(
        input_grad(quarter),
        [shape_of((quarter, model_dim))],
        here, din_own, other(din_sent, 2), tokens, d_middle, norm_gain[None, :],
        small=(0,),
    )[0]
    layout = small_rows(model_dim, inner, state, conv_taps, tensor_count)
    table_shape = shape_of((dp_count, SUB, LANES))
    table = kernel_call(
        small_table(layout, inner, state, conv_taps, heads),
        [table_shape],
        here, grad_norm, grad_post_gain, grad_taps, grad_gain, grad_heads, grad_skip,
        small=(0,),
        scratch=[pltpu.VMEM((dp_count * EACH, LANES), f32)],
    )[0]
    table = lax.all_to_all(table, "dp", 0, 0, tiled=True)
    mix_rings = ring_pass(mix_sent, mix_terms, mix_widths, "xy", 4 * shard, grad_tokens)
    devices = dp_count * tensor_count
    table = kernel_call(small_sum(), [shape_of((devices, SUB, LANES))], table)[0]
    table_end = lax.all_to_all(table, ("dp", "tensor"), 0, 0, tiled=True)
    small = kernel_call(
        small_out(layout, tensor_count, inner, state, conv_taps),
        [
            shape_of((1, model_dim)),
            shape_of((1, model_dim)),
            shape_of((conv_taps, inner_total)),
            shape_of((conv_taps, 2 * state)),
            shape_of((1, inner_total)),
            shape_of((1, inner_total)),
            shape_of((2 * tensor_count, LANES)),
        ],
        table_end,
        scratch=[pltpu.VMEM((dp_count * EACH, LANES), f32)],
    )
    norm_sum, post_sum, taps_x, taps_bc, gain_sum, skip_sum, head_sums = small
    head_sums = head_sums.reshape(2, tensor_count, LANES)[:, :, :heads].reshape(2, -1)
    widths = [one + two for one, two in zip(ffn_widths, mix_widths, strict=True)]
    chunks = kernel_call(
        ring_fold(shard), chunk_shapes(shard, widths), here, *ffn_totals, *mix_rings,
        small=(0,),
        scratch=[pltpu.VMEM((8 * shard, width), f32) for width in widths],
        whole=True,
        wait=table,
    )
    sent, terms = ring_send(chunks, "yx")
    results = ring_pass(sent, terms, widths, "yx", shard, table_end)
    sum_shape = (shard, sum(widths))
    mine, sent = kernel_call(
        ring_end(shard, widths), [shape_of(sum_shape), shape_of(sum_shape, bf16)], here, *results,
        small=(0,),
        whole=True,
    )
    def found(group, first, columns):
        ffn_wide, mix_wide = ffn_widths[0], mix_widths[0]
        entries = []
        for at in range(first, first + columns, LANES):
            half, shift_by = (0, 0) if at < (ffn_wide, mix_wide)[group] else (1, (ffn_wide, mix_wide)[group])
            begin = half * widths[0] + (ffn_widths[half] if group else 0)
            entries.append((at - first, begin + at - shift_by, LANES))
        return entries

    def plain(group, first, columns):
        return [(None, *entry) for entry in found(group, first, columns)]

    def by_expert(first):
        entries = found(0, first, experts * ffe)
        return [(at // ffe, at % ffe, begin, columns) for at, begin, columns in entries]

    wide_e = experts * ffe
    out_plan = [
        plain(1, 0, 2 * inner),
        plain(1, dt_at, LANES),
        plain(1, bc_at, state),
        plain(1, out_at, inner),
        by_expert(0),
        by_expert(hidden),
        by_expert(2 * hidden),
        plain(0, wide_e, ffs),
        plain(0, hidden + wide_e, ffs),
        plain(0, 2 * hidden + wide_e, ffs),
    ]
    grad_zx, grad_dt, bc_half, grad_out, grad_eg, grad_eu, grad_ed, grad_sg, grad_su, grad_sd = kernel_call(
        grad_blocks(out_plan, shard),
        [
            shape_of((shard, 2 * inner)),
            shape_of((shard, LANES)),
            shape_of((shard, state)),
            shape_of((shard, inner)),
            *[shape_of((experts, shard, ffe))] * 3,
            *[shape_of((shard, ffs))] * 3,
        ],
        mine, shift(sent, "z", 1),
    )
    bc_far = other(bc_half, 1)
    grad_bc = jnp.stack([jnp.where(core == 0, bc_half, bc_far), jnp.where(core == 0, bc_far, bc_half)], 1)
    return (
        block_out,
        grad_tokens,
        norm_sum[0],
        grad_zx.reshape(shard, 2, inner),
        grad_bc,
        grad_dt[:, :heads],
        taps_x,
        taps_bc.reshape(conv_taps, 2, state),
        head_sums[0],
        head_sums[1],
        jnp.sum(skip_sum.reshape(head_total, head_dim), 1),
        gain_sum[0],
        grad_out.T,
        post_sum[0],
        grad_eg,
        grad_eu,
        grad_ed.transpose(0, 2, 1),
        grad_sg,
        grad_su,
        grad_sd.T,
    )


def solution(mesh):
    in_specs = (
        P(("dp", "tensor"), None),
        P(("dp", "tensor"), None),
        P("dp"),
        P("dp", None),
        P("dp", None),
        P(),
        P("dp", None, "tensor"),
        P("dp", None, None),
        P("dp", "tensor"),
        P(),
        P(),
        P(),
        P(),
        P(),
        P(),
        P("tensor", "dp"),
        P(),
        P(None, "dp", "tensor"),
        P(None, "dp", "tensor"),
        P(None, "tensor", "dp"),
        P("dp", "tensor"),
        P("dp", "tensor"),
        P("tensor", "dp"),
    )
    out_specs = (
        P(("dp", "tensor"), None),
        P(("dp", "tensor"), None),
        P(),
        P("dp", None, "tensor"),
        P("dp", None, None),
        P("dp", "tensor"),
        P(),
        P(),
        P(),
        P(),
        P(),
        P(),
        P("tensor", "dp"),
        P(),
        P(None, "dp", "tensor"),
        P(None, "dp", "tensor"),
        P(None, "tensor", "dp"),
        P("dp", "tensor"),
        P("dp", "tensor"),
        P("tensor", "dp"),
    )
    return jax.shard_map(body, mesh=mesh, in_specs=in_specs, out_specs=out_specs, check_vma=False)
```

```python
import math

import jax
import jax.numpy as jnp
from jax import lax
from jax.experimental import pallas as pl
from jax.experimental.pallas import tpu as pltpu
from jax.sharding import PartitionSpec as P

f32 = jnp.float32
bf16 = jnp.bfloat16
eps = 1e-05
highest = lax.Precision.HIGHEST
LANES = 128
DP_SHAPE = (4, 2, 4)
EDGE = 16
SUB = 8
RAW_LIMIT = 48 * 1024 * 1024
WHOLE_LIMIT = 62 * 1024 * 1024
RING_SPARE = 4 * 1024 * 1024
VMEM_SPARE = 8 * 1024 * 1024

NN = (((1,), (0,)), ((), ()))
NT = (((1,), (1,)), ((), ()))
TN = (((0,), (0,)), ((), ()))


def dot(a, b, dims=NN):
    return lax.dot_general(a.astype(bf16), b.astype(bf16), dims, preferred_element_type=f32)


def dot_exact(a, b, dims=NN):
    return lax.dot_general(a, b, dims, precision=highest, preferred_element_type=f32)


def halves(value):
    high = value.astype(bf16)
    return high, (value - high.astype(f32)).astype(bf16)


def dot_left(a, b, dims=NN):
    high, low = halves(a)
    return dot(high, b, dims) + dot(low, b, dims)


def dot_both(a, b, dims=NN):
    a_high, a_low = halves(a)
    b_high, b_low = halves(b)
    return dot(a_high, b_high, dims) + (dot(a_low, b_high, dims) + dot(a_high, b_low, dims))


def from_behind(value, axis, steps):
    count = lax.axis_size(axis)
    leading, last = (max(0, -steps), min(count, count - steps))
    return lax.ppermute(value, axis, [(source, source + steps) for source in range(leading, last)])


def kernel_call(kernel, out_shapes, *args, flops=0, scratch=(), small=(), raw=(), whole=False, alone=False, wait=()):
    moved = sum(a.size * a.dtype.itemsize for a in args)
    moved += sum(s.size * s.dtype.itemsize for s in out_shapes)
    kept = [a for i, a in enumerate(args) if i not in raw and i not in small] + list(out_shapes)
    kept += [s for s in scratch if s.dtype in (f32, bf16)]
    held = sum(math.prod(a.shape) * (4 if a.dtype == f32 else 2) for a in kept)
    limit = held + (RING_SPARE if whole else VMEM_SPARE)
    limit = WHOLE_LIMIT if alone else max(limit, RAW_LIMIT if len(raw) > 1 else 0)
    spaces = [
        pltpu.SMEM if i in small else pl.ANY if i in raw else pltpu.VMEM for i in range(len(args))
    ]
    wait = jax.tree.leaves(wait)
    count = len(args)

    def body_of(*refs):
        kernel(*refs[:count], *refs[count + len(wait) :])

    return pl.pallas_call(
        body_of,
        name=kernel.__qualname__.split(".")[0],
        out_shape=out_shapes,
        in_specs=[pl.BlockSpec(memory_space=space) for space in spaces + [pl.ANY] * len(wait)],
        scratch_shapes=scratch,
        compiler_params=pltpu.CompilerParams(vmem_limit_bytes=limit),
        cost_estimate=pl.CostEstimate(flops=flops, bytes_accessed=moved, transcendentals=0),
    )(*args, *wait)


def shape_of(shape, dtype=f32):
    return jax.ShapeDtypeStruct(shape, dtype)


def ids(shape, dim):
    return lax.broadcasted_iota(jnp.int32, shape, dim)


def per_head(columns, pair, rows):
    left = ids((rows, LANES), 1) < LANES // 2
    return jnp.where(left, columns[:, 2 * pair : 2 * pair + 1], columns[:, 2 * pair + 1 : 2 * pair + 2])


def run_info(cum, heads):
    rows = cum.shape[0]
    turned = cum.T
    run_col = cum[:, heads : heads + 1]
    run_row = turned[heads : heads + 1, :]
    keep = (ids((rows, rows), 0) >= ids((rows, rows), 1)) & (run_col == run_row)
    return turned, run_col, run_col[rows - 1 : rows, :], keep


HALVED = ((0, 0, 8), (-1, 0, 8), (1, 0, 8), (2, 0, 4), (2, 4, 4))


def load_blocks(pieces, target, done, here, ranges, shard, form):
    x_size, z_size, y_size = DP_SHAPE
    x, z, y = here[0], here[1], here[2]
    copies = []
    for half, start, at, width in ranges:
        for index, (far, begin, blocks) in enumerate(form):
            for block in range(blocks):
                place_in = begin + block
                near = RING[place_in // 2]
                to_x, to_y = (far, near) if half == 0 else (near, far)
                to_x = lax.rem(x + (to_x + x_size), x_size)
                to_y = lax.rem(y + (to_y + y_size), y_size)
                to_z = lax.rem(z + place_in % 2, z_size)
                row = pl.multiple_of(((to_x * z_size + to_z) * y_size + to_y) * shard, 16)
                copy = pltpu.make_async_copy(
                    pieces[half * len(form) + index].at[block, :, pl.ds(start, width)],
                    target.at[pl.ds(row, shard), pl.ds(at, width)],
                    done.at[len(copies)],
                )
                copy.start()
                copies.append(copy)
    return copies


def wait_all(copies):
    for copy in copies:
        copy.wait()


def column_ranges(split, first, last):
    ranges = []
    if first < split:
        ranges.append((0, first, 0, min(last, split) - first))
    if last > split:
        begin = max(first, split)
        ranges.append((1, begin - split, begin - first, last - begin))
    return ranges


def rows_at(index, quarter):
    return pl.ds(pl.multiple_of(index * quarter, quarter), quarter)


def silu_slope(value, sigma):
    return sigma * (1.0 + value * (1.0 - sigma))


def pack_blocks(plan, width):
    def kernel(*refs):
        ins, out = refs[:-1], refs[-1]
        for arg, lead, first, columns, at in plan:
            if columns % LANES:
                out[:, at : at + LANES] = jnp.zeros((out.shape[0], LANES), bf16)
            ref = ins[arg]
            if lead is None:
                value = ref[:, first : first + columns]
            elif ref.shape[0] == out.shape[0]:
                value = ref[:, lead, first : first + columns]
            else:
                value = ref[lead, :, first : first + columns]
            out[:, at : at + columns] = value

    return kernel


def pack_plan(args, in_count, in_split, rest_split):
    plan, sizes, at, group = [], [0, 0], 0, 0
    entries = []
    for arg, value in enumerate(args):
        if arg == in_count:
            group, at = 1, 0
        for lead in range(min(value.shape[:2])) if len(value.shape) == 3 else (None,):
            for first in range(0, value.shape[-1], LANES):
                columns = min(LANES, value.shape[-1] - first)
                entries.append((group, at, arg, lead, first, columns))
                at += LANES
        sizes[group] = at
    splits = (in_split, rest_split)
    for group, at, arg, lead, first, columns in entries:
        if at < splits[group]:
            to = at + (in_split if group else 0)
        else:
            to = in_split + rest_split + at - splits[group] + (sizes[0] - in_split if group else 0)
        plan.append((arg, lead, first, columns, to))
    return plan, sum(sizes)


def input_rows(quarter):
    def kernel(here, rows_in, ids_in, gain, normed_out, own_out, tail_out):
        rank = here[4] * 2 + here[3]
        rows, width = rows_in.shape
        value = rows_in[...].astype(f32)
        scale = lax.rsqrt(jnp.mean(value * value, -1, keepdims=True) + eps)
        normed = (value * scale * gain[...]).astype(bf16)
        normed_out[...] = normed
        own_out[...] = normed_out[rows_at(rank, quarter), :]
        tail_out[:, :width] = normed[rows - EDGE :, :]
        tail_out[:, width:] = ids_in[rows - EDGE :, :].astype(bf16)

    return kernel


def scan_front(heads, inner, state, shard, ranges):
    pairs = heads // 2
    tiles = (inner + 2 * state) // LANES

    def kernel(here, normed, tail, taps, ids_in, bias, alog, skip, *refs):
        pieces, refs = refs[: 2 * len(HALVED)], refs[2 * len(HALVED) :]
        proj, lags, y_out, conv_out, cum_out, steps_out, state_out, act, sums, weights_in, ids_ext, done = refs
        copies = load_blocks(pieces, weights_in, done, here, ranges, shard, HALVED)
        columns = weights_in.shape[1]
        wide = 3 * LANES
        rows, depth = normed.shape
        ids_ext[0:EDGE, :] = tail[:, depth:].astype(f32)
        ids_ext[EDGE:, :] = ids_in[...]
        lane = ids((rows, LANES), 1)
        row = ids((rows, LANES), 0)
        no_row_before = here[0] + here[1] + here[2] == 0
        lags[...] = jnp.zeros_like(lags)
        for back in range(taps.shape[0] // 2):
            same = ids_ext[EDGE - back : EDGE - back + rows, :] == ids_in[...]
            same = same & ((row >= back) | jnp.logical_not(no_row_before))
            lags[...] = jnp.where((lane == back) & same, 1.0, lags[...])
        first = len(copies) // 2
        wait_all(copies[:first])
        for at in range(0, columns, wide):
            if at + wide > ranges[0][3] and first:
                wait_all(copies[first:])
                first = 0
            part = weights_in[:, at : at + wide]
            proj[0:EDGE, at : at + wide] = dot(tail[:, :depth], part)
            proj[EDGE:, at : at + wide] = dot(normed[...], part)
        count = taps.shape[0] // 2
        for tile in range(tiles):
            at = tile * LANES
            total = jnp.zeros((rows, LANES), f32)
            for back in range(count):
                source = proj[EDGE - back : EDGE - back + rows, inner + at : inner + at + LANES]
                weight = taps[count - 1 - back : count - back, at : at + LANES]
                total = total + weight * source * lags[:, back : back + 1]
            conv_out[:, at : at + LANES] = total
            act[:, at : at + LANES] = total * jax.nn.sigmoid(total)
        b_rows = act[:, inner : inner + state]
        c_rows = act[:, inner + state : inner + 2 * state]
        raw = proj[EDGE : EDGE + rows, 2 * inner + 2 * state :] + bias[...]
        steps = jnp.maximum(raw, 0.0) + jnp.log1p(jnp.exp(-jnp.abs(raw)))
        reset = 1.0 - lags[:, 1:2]
        logs = jnp.where(lane < heads, -steps * jnp.exp(alog[...]), jnp.where(lane == heads, reset, 0.0))
        lower = (ids((rows, rows), 0) >= ids((rows, rows), 1)).astype(f32)
        cum = dot_exact(lower, logs)
        steps_out[...] = steps
        cum_out[...] = cum
        turned, run_col, last_run, keep = run_info(cum, heads)
        inner_cb = dot_exact(c_rows, b_rows, NT)
        closing = jnp.where(run_col == last_run, jnp.exp(cum[rows - 1 : rows, :] - cum), 0.0)
        left = ids((rows, LANES), 1) < LANES // 2
        for pair in range(pairs):
            at = pair * LANES
            x_pair = act[:, at : at + LANES]
            scaled = x_pair * per_head(steps, pair, rows)
            parts = []
            for head in (2 * pair, 2 * pair + 1):
                gaps = cum[:, head : head + 1] - turned[head : head + 1, :]
                weights = jnp.exp(jnp.where(keep, gaps, -jnp.inf)) * inner_cb
                parts.append(dot_left(weights, scaled))
            y_out[:, at : at + LANES] = (
                jnp.where(left, parts[0], parts[1]) + skip[:, at : at + LANES] * x_pair
            )
            sums[at : at + LANES, :] = dot_both(scaled * per_head(closing, pair, rows), b_rows, TN)
        last = cum[rows - 1 : rows, :]
        fill_states(state_out, sums, jnp.where(last_run == 0.0, jnp.exp(last), 0.0), heads)

    return kernel


def fill_states(out, sums, keep, heads):
    blocks, size = out.shape[0], sums.shape[0] // out.shape[0]
    head_rows = sums.shape[0] // heads
    row_head = (ids((blocks, LANES), 0) * size + ids((blocks, LANES), 1)) // head_rows
    table = jnp.zeros((blocks, LANES), f32)
    for head in range(heads):
        table = jnp.where(row_head == head, keep[:, head : head + 1], table)
    for block in range(blocks):
        out[block, 0:size, :] = sums[block * size : (block + 1) * size, :]
        out[block, size : size + SUB, :] = jnp.broadcast_to(table[block : block + 1, :], (SUB, LANES))


def gate_front(heads, inner, state, shard, ranges):
    pairs = heads // 2

    def kernel(here, y_in, proj, conv, cum_in, entering, gain, *refs):
        pieces, refs = refs[: 2 * len(HALVED)], refs[2 * len(HALVED) :]
        w_back, y_out, mixed_out, mine_out, theirs_out, mixed_low, partial, done = refs
        copies = load_blocks(pieces, w_back, done, here, ranges, shard, HALVED)
        rows = y_in.shape[0]
        quarter = rows // 4
        width = partial.shape[1] - LANES
        core = here[3]
        cum = cum_in[...]
        opening = jnp.where(cum[:, heads : heads + 1] == 0.0, jnp.exp(cum), 0.0)
        c_conv = conv[:, inner + state : inner + 2 * state]
        c_rows = c_conv * jax.nn.sigmoid(c_conv)
        squares = jnp.zeros((rows, LANES), f32)
        for pair in range(pairs):
            at = pair * LANES
            y_pair = y_in[:, at : at + LANES] + per_head(opening, pair, rows) * dot_both(
                c_rows, entering[at : at + LANES, :], NT
            )
            z_pair = proj[EDGE : EDGE + rows, at : at + LANES]
            gated = y_pair * z_pair * jax.nn.sigmoid(z_pair)
            y_out[:, at : at + LANES] = y_pair
            high, low = halves(gated * gain[:, at : at + LANES])
            mixed_out[:, at : at + LANES] = high
            mixed_low[:, at : at + LANES] = low
            squares = squares + gated * gated
        total = jnp.sum(squares, 1, keepdims=True)
        partial[:, width:] = jnp.broadcast_to(total, (rows, LANES))
        wait_all(copies)
        wide = 2 * LANES
        for at in range(0, width, wide):
            part = w_back[at : at + wide, :]
            partial[:, at : at + wide] = dot(mixed_out[...], part, NT) + dot(mixed_low[...], part, NT)
        for half in range(2):
            to = slice(half * quarter, (half + 1) * quarter)
            mine_out[to, :] = partial[rows_at(2 * half + core, quarter), :]
            theirs_out[to, :] = partial[rows_at(2 * half + 1 - core, quarter), :]

    return kernel


def core_sum(width):
    def kernel(mine, theirs, sum_out, sent_out):
        total = mine[...] + theirs[...]
        sum_out[...] = total[:, :width]
        sent_out[:, :width] = total[:, :width].astype(bf16)
        squares = total[:, width : width + 1]
        high = squares.astype(bf16).astype(f32)
        lane = ids((total.shape[0], LANES), 1)
        sent_out[:, width:] = jnp.where(lane == 0, high, jnp.where(lane == 1, squares - high, 0.0)).astype(bf16)

    return kernel


def middle_rows(quarter, width, inner_total):
    def kernel(here, sent, got, rows_in, gain, middle_out, post_out, scales_out):
        core = here[3]
        total = sent[...].astype(f32) + got[...].astype(f32)
        squares = total[:, width : width + 1] + total[:, width + 1 : width + 2]
        scale_mix = lax.rsqrt(squares / inner_total + eps)
        for half in range(2):
            to = slice(half * quarter, (half + 1) * quarter)
            middle_out[to, :] = rows_in[rows_at(2 * half + core, quarter), :].astype(f32)
        middle = middle_out[...] + scale_mix * total[:, :width]
        middle_out[...] = middle
        scale = lax.rsqrt(jnp.mean(middle * middle, -1, keepdims=True) + eps)
        post_out[...] = (middle * scale * gain[...]).astype(bf16)
        lane = ids((2 * quarter, LANES), 1)
        scales_out[...] = jnp.where(lane == 0, scale_mix, scale)

    return kernel


def experts_both(quarter, hidden, ffe, experts, shard, ranges):
    def kernel(here, post_mine, post_theirs, cot_in, share, *refs):
        pieces, refs = refs[: 2 * len(HALVED)], refs[2 * len(HALVED) :]
        (
            post, cot, act_out, dpre_out, out_mine, out_theirs, dpost_mine, dpost_theirs,
            weights, shares, gates, ups, done,
        ) = refs
        copies = load_blocks(pieces, weights, done, here, ranges, shard, HALVED)
        core = here[3]
        half = 2 * quarter
        width = post.shape[1]
        post[0:half, :] = post_mine[...]
        post[half:, :] = post_theirs[...]
        for index in range(2):
            to = slice(index * quarter, (index + 1) * quarter)
            cot[to, :] = cot_in[rows_at(2 * index + core, quarter), :]
            to = slice(half + index * quarter, half + (index + 1) * quarter)
            cot[to, :] = cot_in[rows_at(2 * index + 1 - core, quarter), :]
            shares[index * quarter : (index + 1) * quarter, :] = share[rows_at(2 * index + core, quarter), :]
            shares[half + index * quarter : half + (index + 1) * quarter, :] = share[
                rows_at(2 * index + 1 - core, quarter), :
            ]
        wide = 2 * LANES
        left = ids((2 * half, wide), 1) < ffe
        first = ranges[0][3]
        wait_all(copies[: len(copies) // 2])
        for at in range(0, hidden, wide):
            gates[:, at : at + wide] = dot(post[...], weights[:, at : at + wide])
        for at in range(0, hidden, wide):
            if hidden + at + wide <= first:
                ups[:, at : at + wide] = dot(post[...], weights[:, hidden + at : hidden + at + wide])
        wait_all(copies[len(copies) // 2 :])
        for at in range(0, hidden, wide):
            gate = gates[:, at : at + wide]
            if hidden + at + wide <= first:
                up = ups[:, at : at + wide]
            else:
                up = dot(post[...], weights[:, hidden + at : hidden + at + wide])
            d_act = dot(cot[...], weights[:, 2 * hidden + at : 2 * hidden + at + wide])
            sigma = jax.nn.sigmoid(gate)
            silu = gate * sigma
            act = silu * up
            expert = at // ffe
            if expert < experts:
                by = jnp.where(left, shares[:, expert : expert + 1], shares[:, expert + 1 : expert + 2])
                act = act * by
                d_act = d_act * by
            act_out[:, at : at + wide] = act.astype(bf16)
            dpre_out[:, at : at + wide] = (d_act * up * silu_slope(gate, sigma)).astype(bf16)
            dpre_out[:, hidden + at : hidden + at + wide] = (d_act * silu).astype(bf16)
        for at in range(0, width, wide):
            d_post = dot(dpre_out[...], weights[at : at + wide, : 2 * hidden], NT)
            dpost_mine[:, at : at + wide] = d_post[:half]
            dpost_theirs[:, at : at + wide] = d_post[half:].astype(bf16)
        for at in range(0, width, wide):
            out = dot(act_out[...], weights[at : at + wide, 2 * hidden :], NT)
            out_mine[:, at : at + wide] = out[:half]
            out_theirs[:, at : at + wide] = out[half:].astype(bf16)

    return kernel


def add_round():
    def kernel(mine, theirs, sent_out):
        sent_out[...] = (mine[...] + theirs[...].astype(f32)).astype(bf16)

    return kernel


def add_split(quarter):
    def kernel(here, mine, theirs, own_out, sent_out):
        pair = here[4]
        own = rows_at(pair, quarter)
        away = rows_at(1 - pair, quarter)
        own_out[...] = mine[own, :] + theirs[own, :].astype(f32)
        sent_out[...] = (mine[away, :] + theirs[away, :].astype(f32)).astype(sent_out.dtype)

    return kernel


def middle_back(quarter, width, inner_total):
    def kernel(
        here, sent, got, cot_in, middle_in, scales, core_total, pair_sent, gain,
        dmiddle_out, back_out, gain_out,
    ):
        core = here[3]
        d_post = sent[...].astype(f32) + got[...].astype(f32)
        middle = middle_in[...]
        scale_mix, scale = scales[:, 0:1], scales[:, 1:2]
        gain_out[...] = 0.5 * jnp.sum(d_post * middle * scale, 0, keepdims=True)
        scaled = d_post * gain[...]
        for half in range(2):
            to = slice(half * quarter, (half + 1) * quarter)
            dmiddle_out[to, :] = cot_in[rows_at(2 * half + core, quarter), :].astype(f32)
        d_middle = (
            dmiddle_out[...]
            + scale * scaled
            - middle * (scale * scale * scale) * jnp.mean(scaled * middle, -1, keepdims=True)
        )
        dmiddle_out[...] = d_middle
        d_proj = (scale_mix * d_middle.astype(bf16).astype(f32)).astype(bf16)
        back_out[:, :width] = d_proj
        projected = core_total[...] + pair_sent[:, :width].astype(f32)
        d_scale = jnp.sum(d_proj.astype(f32) * projected, -1, keepdims=True)
        coeff = -d_scale * scale_mix * scale_mix / inner_total
        high = coeff.astype(bf16).astype(f32)
        lane = ids((2 * quarter, LANES), 1)
        back_out[:, width:] = jnp.where(lane == 0, high, jnp.where(lane == 1, coeff - high, 0.0)).astype(bf16)

    return kernel


def gate_back(heads, inner, state):
    pairs = heads // 2

    def kernel(
        here, back_mine, back_theirs, w_back, y_in, proj, conv, cum_in, gain,
        dproj_out, dy_out, dz_out, gain_out, enter_out, sums, factors, d_mixed,
    ):
        rows = y_in.shape[0]
        quarter = rows // 4
        width = dproj_out.shape[1]
        core = here[3]
        for index in range(2):
            part = slice(index * quarter, (index + 1) * quarter)
            for ref, at in ((back_mine, 2 * index + core), (back_theirs, 2 * index + 1 - core)):
                dproj_out[rows_at(at, quarter), :] = ref[part, :width]
                factors[rows_at(at, quarter), :] = ref[part, width:].astype(f32)
        d_mixed[...] = dot(dproj_out[...], w_back[...])
        cum = cum_in[...]
        opening = jnp.where(cum[:, heads : heads + 1] == 0.0, jnp.exp(cum), 0.0)
        c_conv = conv[:, inner + state : inner + 2 * state]
        c_rows = c_conv * jax.nn.sigmoid(c_conv)
        factor = factors[:, 0:1] + factors[:, 1:2]
        for pair in range(pairs):
            at = pair * LANES
            y_pair = y_in[:, at : at + LANES]
            z_pair = proj[EDGE : EDGE + rows, at : at + LANES]
            sigma = jax.nn.sigmoid(z_pair)
            silu = z_pair * sigma
            gated = y_pair * silu
            d_mix = d_mixed[:, at : at + LANES]
            gain_out[:, at : at + LANES] = jnp.sum(d_mix * gated, 0, keepdims=True)
            d_gated = d_mix * gain[:, at : at + LANES] + factor * gated
            dz_out[:, at : at + LANES] = (d_gated * y_pair * silu_slope(z_pair, sigma)).astype(bf16)
            d_y = d_gated * silu
            dy_out[:, at : at + LANES] = d_y
            sums[at : at + LANES, :] = dot_both(d_y * per_head(opening, pair, rows), c_rows, TN)
        last = cum[rows - 1 : rows, :]
        last_run = last[:, heads : heads + 1]
        fill_states(enter_out, sums, jnp.where(last_run == 0.0, jnp.exp(last), 0.0), heads)

    return kernel


def bc_split(state, inner):
    def kernel(here, d_bc, tail, mine_out, theirs_out, whole):
        core = here[3]
        last = d_bc.shape[0] - EDGE
        whole[0:last, :] = d_bc[0:last, :]
        whole[last:, :] = d_bc[last:, :] + tail[:, inner:]
        first, second = whole[:, :state], whole[:, state:]
        mine_out[...] = jnp.where(core == 0, first, second)
        theirs_out[...] = jnp.where(core == 0, second, first)

    return kernel


def add_exact():
    def kernel(mine, theirs, out):
        out[...] = mine[...] + theirs[...]

    return kernel


def join_grads(inner):
    def prepare(arrays, out):
        d_z, d_x, tail, d_dt, bc_mine, bc_theirs = arrays
        rows = out.shape[0]
        out[:, :inner] = d_z[...]
        out[:, inner : 2 * inner] = d_x[...].astype(bf16)
        out[rows - EDGE :, inner : 2 * inner] = (d_x[rows - EDGE :, :] + tail[:, :inner]).astype(bf16)
        out[:, 2 * inner : 2 * inner + LANES] = d_dt[...]
        out[:, 2 * inner + LANES :] = (bc_mine[...] + bc_theirs[...]).astype(bf16)

    return prepare


def input_back(quarter, inner, state, shard, ranges):
    def kernel(here, d_all, rows_in, *refs):
        pieces, refs = refs[: 2 * len(HALVED)], refs[2 * len(HALVED) :]
        mine_out, theirs_out, gain_out, d_in, win, done = refs
        wait_all(load_blocks(pieces, win, done, here, ranges, shard, HALVED))
        core = here[3]
        rows, width = rows_in.shape
        wide = 2 * LANES
        bc_at = 2 * inner + 2 * state
        d_bc = 0.5 * d_all[:, 2 * inner + LANES :].astype(f32)
        for at in range(0, width, wide):
            part = win[at : at + wide, :]
            w_bc = jnp.where(
                core == 0,
                part[:, 2 * inner : 2 * inner + state].astype(f32),
                part[:, 2 * inner + state : bc_at].astype(f32),
            )
            d_in[:, at : at + wide] = (
                dot(d_all[:, : 2 * inner], part[:, : 2 * inner], NT)
                + dot(d_all[:, 2 * inner : 2 * inner + LANES], part[:, bc_at:], NT)
                + dot(d_bc, w_bc, NT)
            )
        value = rows_in[...].astype(f32)
        scale = lax.rsqrt(jnp.mean(value * value, -1, keepdims=True) + eps)
        gain_out[...] = jnp.sum(d_in[...] * value * scale, 0, keepdims=True)
        for index in range(2):
            part = slice(index * quarter, (index + 1) * quarter)
            mine_out[part, :] = d_in[rows_at(2 * index + core, quarter), :]
            theirs_out[part, :] = d_in[rows_at(2 * index + 1 - core, quarter), :].astype(bf16)

    return kernel


def input_grad(quarter):
    def kernel(here, own_sum, got, tokens, d_middle, gain, grad_out):
        pair = here[4]
        value = tokens[...].astype(f32)
        scale = lax.rsqrt(jnp.mean(value * value, -1, keepdims=True) + eps)
        scaled = (own_sum[...] + got[...].astype(f32)) * gain[...]
        grad_out[...] = (
            d_middle[rows_at(pair, quarter), :]
            + scale * scaled
            - value * (scale * scale * scale) * jnp.mean(scaled * value, -1, keepdims=True)
        )

    return kernel


def layer_out(quarter):
    def kernel(here, own_sum, got, middle, out):
        out[...] = middle[rows_at(here[4], quarter), :] + own_sum[...] + got[...].astype(f32)

    return kernel


def scan_back(heads, inner, state):
    pairs = heads // 2
    tiles = (inner + 2 * state) // LANES

    def kernel(
        proj, taps, lags, bias, alog, skip, conv, cum_in, steps_in, dy_in, entering, leaving,
        dx_out, dbc_out, tail_out, ddt_out, conv_grad, head_grad, skip_grad, dact, rowsums, dpre_out,
    ):
        rows = dy_in.shape[0]
        count = taps.shape[0] // 2
        cum = cum_in[...]
        steps = steps_in[...]
        lane = ids((rows, LANES), 1)
        left = lane < LANES // 2
        turned, run_col, last_run, keep = run_info(cum, heads)
        b_conv = conv[:, inner : inner + state]
        c_conv = conv[:, inner + state : inner + 2 * state]
        b_rows = b_conv * jax.nn.sigmoid(b_conv)
        c_rows = c_conv * jax.nn.sigmoid(c_conv)
        inner_cb = dot_exact(c_rows, b_rows, NT)
        last_cum = cum[rows - 1 : rows, :]
        closing = jnp.where(run_col == last_run, jnp.exp(last_cum - cum), 0.0)
        opening = jnp.where(run_col == 0.0, jnp.exp(cum), 0.0)
        keep_old = jnp.where(last_run == 0.0, jnp.exp(last_cum), 0.0)
        d_cb = jnp.zeros((rows, rows), f32)
        d_b = jnp.zeros((rows, state), f32)
        d_c = jnp.zeros((rows, state), f32)
        d_cum = jnp.zeros((rows, LANES), f32)
        d_steps = jnp.zeros((rows, LANES), f32)
        d_open = jnp.zeros((rows, LANES), f32)
        d_close = jnp.zeros((rows, LANES), f32)
        d_keep = jnp.zeros((1, LANES), f32)
        lane_row = ids((1, LANES), 1)
        rowsums[...] = jnp.zeros_like(rowsums)
        for pair in range(pairs):
            at = pair * LANES
            x_conv = conv[:, at : at + LANES]
            x_pair = x_conv * jax.nn.sigmoid(x_conv)
            d_y = dy_in[:, at : at + LANES]
            step_pair = per_head(steps, pair, rows)
            scaled = x_pair * step_pair
            enter_pair = entering[at : at + LANES, :]
            leave_pair = leaving[at : at + LANES, :]
            close_pair = per_head(closing, pair, rows)
            b_leave = dot(b_rows, leave_pair, NT)
            c_enter = dot(c_rows, enter_pair, NT)
            d_b = d_b + dot_both(scaled * close_pair, leave_pair)
            d_c = d_c + dot_both(d_y * per_head(opening, pair, rows), enter_pair)
            close_prod = b_leave * scaled
            open_prod = d_y * c_enter
            keep_prod = enter_pair * leave_pair
            parts = []
            for side, head in ((0, 2 * pair), (1, 2 * pair + 1)):
                mine = left if side == 0 else ~left
                gaps = cum[:, head : head + 1] - turned[head : head + 1, :]
                decay = jnp.exp(jnp.where(keep, gaps, -jnp.inf))
                weights = decay * inner_cb
                d_weights = dot_left(jnp.where(mine, d_y, 0.0), scaled, NT)
                d_cb = d_cb + d_weights * decay
                flow = d_weights * weights
                d_cum = d_cum + jnp.where(lane == head, jnp.sum(flow, 1, keepdims=True), 0.0)
                rowsums[head : head + 1, :] = jnp.sum(flow, 0, keepdims=True)
                parts.append(dot(weights, d_y, TN))
                half = LANES // 2
                kept = jnp.sum(
                    jnp.sum(keep_prod[side * half : side * half + half, :], 0, keepdims=True), 1, keepdims=True
                )
                d_keep = d_keep + jnp.where(lane_row == head, kept, 0.0)
                d_open = d_open + jnp.where(
                    lane == head, jnp.sum(jnp.where(mine, open_prod, 0.0), 1, keepdims=True), 0.0
                )
                d_close = d_close + jnp.where(
                    lane == head, jnp.sum(jnp.where(mine, close_prod, 0.0), 1, keepdims=True), 0.0
                )
            d_scaled = jnp.where(left, parts[0], parts[1]) + close_pair * b_leave
            skip_grad[:, at : at + LANES] = jnp.sum(d_y * x_pair, 0, keepdims=True)
            dact[:, at : at + LANES] = step_pair * d_scaled + skip[:, at : at + LANES] * d_y
            step_prod = d_scaled * x_pair
            for side, head in ((0, 2 * pair), (1, 2 * pair + 1)):
                mine = left if side == 0 else ~left
                d_steps = d_steps + jnp.where(
                    lane == head, jnp.sum(jnp.where(mine, step_prod, 0.0), 1, keepdims=True), 0.0
                )
        dact[:, inner : inner + state] = d_b + dot_both(d_cb, c_rows, TN)
        dact[:, inner + state : inner + 2 * state] = d_c + dot_both(d_cb, b_rows)
        ended = closing * d_close
        d_last = jnp.sum(ended, 0, keepdims=True) + keep_old * d_keep
        d_cum = d_cum - rowsums[...].T + opening * d_open - ended
        d_cum = d_cum + jnp.where(ids((rows, LANES), 0) == rows - 1, d_last, 0.0)
        upper = (ids((rows, rows), 0) <= ids((rows, rows), 1)).astype(f32)
        d_logs = jnp.where(lane < heads, dot_exact(upper, d_cum), 0.0)
        rate = jnp.exp(alog[...])
        raw = proj[EDGE : EDGE + rows, 2 * inner + 2 * state :] + bias[...]
        d_raw = (d_steps - rate * d_logs) * jax.nn.sigmoid(raw)
        ddt_out[...] = d_raw.astype(bf16)
        head_grad[...] = jnp.zeros_like(head_grad)
        head_grad[0:1, :] = jnp.sum(d_raw, 0, keepdims=True)
        head_grad[1:2, :] = -jnp.sum(d_logs * steps, 0, keepdims=True) * rate
        dpre_out[...] = jnp.zeros_like(dpre_out)
        conv_grad[...] = jnp.zeros_like(conv_grad)
        for tile in range(tiles):
            at = tile * LANES
            value = conv[:, at : at + LANES]
            sigma = jax.nn.sigmoid(value)
            d_conv = dact[:, at : at + LANES] * (sigma * (1.0 + value * (1.0 - sigma)))
            for back in range(count):
                tap = count - 1 - back
                masked = d_conv * lags[:, back : back + 1]
                source = proj[EDGE - back : EDGE - back + rows, inner + at : inner + at + LANES]
                conv_grad[tap : tap + 1, at : at + LANES] = jnp.sum(masked * source, 0, keepdims=True)
                dpre_out[EDGE - back : EDGE - back + rows, at : at + LANES] += (
                    taps[tap : tap + 1, at : at + LANES] * masked
                )
        dx_out[...] = dpre_out[EDGE:, :inner]
        dbc_out[...] = dpre_out[EDGE:, inner:]
        tail_out[...] = dpre_out[0:EDGE, :]

    return kernel


def chain_states(reverse, blocks, size):
    def kernel(parts, carried_out):
        factors = parts[:, size, :].T
        carried = jnp.zeros((size, LANES), f32)
        for turn in range(blocks):
            k = blocks - 1 - turn if reverse else turn
            carried_out[k] = carried
            carried = factors[0:size, k : k + 1] * carried + parts[k, 0:size, :]

    return kernel


def exchange_states(sent, size, axis, reverse, wait=()):
    blocks = lax.axis_size(axis)
    parts = lax.all_to_all(sent, axis, 0, 0, tiled=True)
    carried = kernel_call(
        chain_states(reverse, blocks, size), [shape_of((blocks, size, LANES))], parts, wait=wait
    )[0]
    back = lax.all_to_all(carried, axis, 0, 0, tiled=True)
    return back.reshape(blocks * size, LANES)


def other(value, bit):
    count = lax.axis_size("tensor")
    return lax.ppermute(value, "tensor", [(rank, rank ^ bit) for rank in range(count)])


def place():
    x_size, z_size, y_size = DP_SHAPE
    index = lax.axis_index("dp")
    return index // (z_size * y_size), index // y_size % z_size, index % y_size


def shift(value, axis, step):
    x_size, z_size, y_size = DP_SHAPE
    pairs = []
    for x in range(x_size):
        for z in range(z_size):
            for y in range(y_size):
                to_x = (x + step) % x_size if axis == "x" else x
                to_z = (z + step) % z_size if axis == "z" else z
                to_y = (y + step) % y_size if axis == "y" else y
                pairs.append(((x * z_size + z) * y_size + y, (to_x * z_size + to_z) * y_size + to_y))
    return lax.ppermute(value, "dp", pairs)


RING = (0, -1, 1, 2)


def spread(pack, near, split):
    mids = []
    for columns, axis in ((slice(0, split), "y"), (slice(split, None), "x")):
        own = jnp.stack([pack[:, columns], near[:, columns]])
        back, ahead = shift(own, axis, 1), shift(own, axis, -1)
        far = [shift(back[:1], axis, 1), shift(ahead[1:], axis, -1)]
        mids.append((own, back, ahead, *far))
    return mids


def finish(mids):
    return [(mid, shift(mid, axis, 1), shift(mid, axis, -1)) for mid, axis in zip(mids, "xy", strict=True)]


def join_mids(cuts):
    def kernel(*refs):
        done = refs[-1]
        copies = []
        for half, cut in enumerate(cuts):
            at = 0
            out = refs[10 + half]
            for ref in refs[5 * half : 5 * half + 5]:
                copy = pltpu.make_async_copy(
                    ref.at[:, :, pl.ds(cut, out.shape[2])], out.at[pl.ds(at, ref.shape[0])], done.at[len(copies)]
                )
                copy.start()
                copies.append(copy)
                at += ref.shape[0]
        wait_all(copies)

    return kernel


def cut_far():
    def kernel(*refs):
        done = refs[-1]
        copies = []
        for index in range(4):
            out = refs[4 + index]
            half = out.shape[0]
            copy = pltpu.make_async_copy(refs[index].at[pl.ds((index % 2) * half, half)], out, done.at[index])
            copy.start()
            copies.append(copy)
        wait_all(copies)

    return kernel


def finish_cut(rings, wait):
    arrived = [part for ring in rings for part in ring[1:]]
    return kernel_call(
        cut_far(), [shape_of((part.shape[0] // 2, *part.shape[1:]), bf16) for part in arrived], *arrived,
        raw=range(4),
        scratch=[pltpu.SemaphoreType.DMA((4,))],
        wait=wait,
    )


def finish_far(rings, cut):
    pieces = []
    for half, axis in enumerate("xy"):
        pieces += [*rings[half], shift(cut[2 * half], axis, 1), shift(cut[2 * half + 1], axis, -1)]
    return pieces


SENT = 5


def cut_chunks(outs, rows_of, part):
    own, to_ahead, to_back, ahead_first, back_second = outs
    own[0:part, :] = rows_of(0, 0)
    own[part:, :] = rows_of(0, 1)
    to_ahead[0:part, :] = rows_of(2, 0)
    to_ahead[part:, :] = rows_of(1, 1)
    to_back[0:part, :] = rows_of(2, 1)
    to_back[part:, :] = rows_of(-1, 0)
    ahead_first[...] = rows_of(1, 0)
    back_second[...] = rows_of(-1, 1)


def chunk_shapes(part, widths):
    shapes = []
    for width in widths:
        shapes += [shape_of((2 * part, width), bf16)] * 3 + [shape_of((part, width), bf16)] * 2
    return shapes


def wrapped(index, step):
    return lax.rem(index + (step + 4), 4)


def term_products(plan, shard, prepare=None, joined=0):
    x_size, z_size, y_size = DP_SHAPE
    part = 4 * shard

    def kernel(here, *refs):
        count = len(refs) - 2 * SENT - 2 - (prepare is not None)
        arrays, outs, scratch = list(refs[:count]), refs[count : count + 2 * SENT], refs[-2:]
        if prepare is not None:
            prepare(arrays[count - joined :], refs[-3])
            arrays = [*arrays[: count - joined], refs[-3]]
        x, y = here[0], here[2]
        for half, terms in enumerate(plan):
            product = scratch[half]
            at = 0
            for lhs, rhs, first, last in terms:
                for start in range(first, last, 2 * LANES):
                    stop = min(start + 2 * LANES, last)
                    product[:, at : at + stop - start] = dot(
                        arrays[lhs][...], arrays[rhs][:, start:stop], TN
                    ).astype(bf16)
                    at += stop - start

            def along_x(step, side, product=product):
                row = (wrapped(x, step) * 2 + side) * part
                return product[pl.ds(pl.multiple_of(row, part), part), :]

            def along_y(step, side, product=product):
                groups = range(side * 4, side * 4 + 4)
                rows = [(group * y_size + wrapped(y, step)) * shard for group in groups]
                return jnp.concatenate([product[pl.ds(pl.multiple_of(row, 16), shard), :] for row in rows], 0)

            cut_chunks(outs[half * SENT : (half + 1) * SENT], along_x if half == 0 else along_y, part)

    return kernel


def ring_add(part):
    def kernel(*refs):
        for half in range(2):
            from_back, from_ahead, ahead_first, back_second = refs[4 * half : 4 * half + 4]
            ahead_out, back_out = refs[8 + 2 * half : 10 + 2 * half]
            ahead_out[...] = (ahead_first[...].astype(f32) + from_back[0:part, :].astype(f32)).astype(bf16)
            back_out[...] = (back_second[...].astype(f32) + from_ahead[0:part, :].astype(f32)).astype(bf16)

    return kernel


def ring_totals(refs, part):
    own, from_back, from_ahead, from_back_last, from_ahead_last = refs
    first = own[0:part, :].astype(f32) + from_ahead[part:, :].astype(f32) + from_back_last[...].astype(f32)
    second = own[part:, :].astype(f32) + from_back[part:, :].astype(f32) + from_ahead_last[...].astype(f32)
    return first, second


def ring_total():
    def kernel(*refs):
        for half in range(2):
            out = refs[2 * SENT + half]
            part = out.shape[0] // 2
            first, second = ring_totals(refs[half * SENT : (half + 1) * SENT], part)
            out[0:part, :] = first.astype(bf16)
            out[part:, :] = second.astype(bf16)

    return kernel


def ring_fold(shard):
    part = 4 * shard

    def kernel(here, *refs):
        x, y = here[0], here[2]
        ended, refs = refs[:2], refs[2:]
        outs, scratch = refs[2 * SENT : 4 * SENT], refs[4 * SENT :]
        for half in range(2):
            total = scratch[half]
            wide = ended[half].shape[1]
            total[:, :wide] = ended[half][...].astype(f32)
            total[0:part, wide:], total[part:, wide:] = ring_totals(refs[half * SENT : (half + 1) * SENT], part)

            def along_y(step, side, total=total):
                row = side * part + wrapped(y, step) * shard
                return total[pl.ds(pl.multiple_of(row, 16), shard), :].astype(bf16)

            def along_x(step, side, total=total):
                row = (wrapped(x, step) * 2 + side) * shard
                return total[pl.ds(pl.multiple_of(row, 16), shard), :].astype(bf16)

            cut_chunks(outs[half * SENT : (half + 1) * SENT], along_y if half == 0 else along_x, shard)

    return kernel


def ring_end(shard, widths):
    def kernel(here, *refs):
        z = here[1]
        mine_out, sent_out = refs[2 * SENT :]
        at = 0
        for half in range(2):
            first, second = ring_totals(refs[half * SENT : (half + 1) * SENT], shard)
            columns = slice(at, at + widths[half])
            mine_out[:, columns] = jnp.where(z == 0, first, second)
            sent_out[:, columns] = jnp.where(z == 0, second, first).astype(bf16)
            at += widths[half]

    return kernel


def ring_send(chunks, axes):
    arrived, stays = [], []
    for half, axis in enumerate(axes):
        own, to_ahead, to_back, ahead_first, back_second = chunks[half * SENT : (half + 1) * SENT]
        arrived += [shift(to_ahead, axis, 1), shift(to_back, axis, -1)]
        stays.append((own, ahead_first, back_second))
    return arrived, stays


def ring_added(arrived, stays, widths, part, wait=()):
    terms = []
    for half in range(2):
        terms += [*arrived[2 * half : 2 * half + 2], *stays[half][1:]]
    shapes = [shape_of((part, width), bf16) for width in widths for _ in range(2)]
    return kernel_call(ring_add(part), shapes, *terms, whole=True, wait=wait)


def ring_passed(arrived, stays, sent, axes):
    results = []
    for half, axis in enumerate(axes):
        last = [shift(sent[2 * half], axis, 1), shift(sent[2 * half + 1], axis, -1)]
        results += [stays[half][0], *arrived[2 * half : 2 * half + 2], *last]
    return results


def ring_pass(arrived, stays, widths, axes, part, wait=()):
    return ring_passed(arrived, stays, ring_added(arrived, stays, widths, part, wait), axes)


def widths_of(plan):
    return [sum(last - first for _, _, first, last in terms) for terms in plan]


def scatter_begin(here, plan, arrays, shard, prepare=None, joined=0, columns=0, wait=()):
    part = 4 * shard
    widths = widths_of(plan)
    shapes = chunk_shapes(part, widths)
    if prepare is not None:
        shapes.append(shape_of((arrays[0].shape[0], columns), bf16))
    return kernel_call(
        term_products(plan, shard, prepare, joined), shapes, here, *arrays,
        flops=sum(2 * arrays[0].shape[0] * 8 * part * width for width in widths),
        small=(0,),
        scratch=[pltpu.VMEM((8 * part, width), bf16) for width in widths],
        whole=True,
        wait=wait,
    )


def grad_blocks(plan, shard):
    def kernel(mine, got, *outs):
        for out, entries in zip(outs, plan, strict=True):
            for lead, first, at, columns in entries:
                value = mine[:, at : at + columns] + got[:, at : at + columns].astype(f32)
                if lead is None and len(out.shape) == 3:
                    side, begin = first // out.shape[2], first % out.shape[2]
                    out[:, side, begin : begin + columns] = value
                elif lead is None:
                    out[:, first : first + columns] = value
                else:
                    out[lead, :, first : first + columns] = value

    return kernel


EACH = 6


def small_rows(model_dim, inner, state, taps, ranks):
    wide, share = model_dim // LANES, inner // LANES
    sizes = {
        "norm": wide,
        "post": wide,
        "taps": taps * ranks * share,
        "bc": taps * 2 * state // LANES,
        "gain": ranks * share,
        "skip": ranks * share,
        "heads": 2 * ranks,
    }
    rows, at = {}, 0
    for name, size in sizes.items():
        rows[name] = at
        at += size
    return rows


def small_table(layout, inner, state, taps, heads):
    share = inner // LANES

    def kernel(here, norm, post, conv, gain, head, skip, out, table):
        rank = here[4] * 2 + here[3]
        ranks = (layout["skip"] - layout["gain"]) // share

        def lanes(i):
            return slice(i * LANES, (i + 1) * LANES)

        table[...] = jnp.zeros_like(table)
        for i in range(layout["post"] - layout["norm"]):
            table[layout["norm"] + i : layout["norm"] + i + 1, :] = norm[:, lanes(i)]
            table[layout["post"] + i : layout["post"] + i + 1, :] = post[:, lanes(i)]
        for i in range(share):
            for tap in range(taps):
                row = layout["taps"] + tap * ranks * share + rank * share + i
                table[pl.ds(row, 1), :] = conv[tap : tap + 1, lanes(i)]
            table[pl.ds(layout["gain"] + rank * share + i, 1), :] = gain[:, lanes(i)]
            table[pl.ds(layout["skip"] + rank * share + i, 1), :] = skip[:, lanes(i)]
        wide = 2 * state // LANES
        for tap in range(taps):
            for i in range(wide):
                row = layout["bc"] + tap * wide + i
                table[row : row + 1, :] = conv[tap : tap + 1, lanes(share + i)]
        for i in range(2):
            table[pl.ds(layout["heads"] + i * ranks + rank, 1), :] = head[i : i + 1, :]
        out[...] = jnp.zeros_like(out)
        for block in range(out.shape[0]):
            out[block, 0:EACH, :] = table[block * EACH : (block + 1) * EACH, :]

    return kernel


def small_sum():
    def kernel(parts, out):
        out[...] = jnp.broadcast_to(jnp.sum(parts[...], 0, keepdims=True), out.shape)

    return kernel


def small_out(layout, ranks, inner, state, taps):
    def kernel(parts, norm, post, conv_x, conv_bc, gain, skip, head, table):
        for block in range(parts.shape[0] // ranks):
            total = jnp.sum(parts[block * ranks : (block + 1) * ranks], 0)
            table[block * EACH : (block + 1) * EACH, :] = total[0:EACH, :]

        def spread_out(ref, line, first):
            for i in range(ref.shape[1] // LANES):
                ref[line : line + 1, i * LANES : (i + 1) * LANES] = table[first + i : first + i + 1, :]

        spread_out(norm, 0, layout["norm"])
        spread_out(post, 0, layout["post"])
        spread_out(gain, 0, layout["gain"])
        spread_out(skip, 0, layout["skip"])
        for tap in range(taps):
            spread_out(conv_x, tap, layout["taps"] + tap * (conv_x.shape[1] // LANES))
            spread_out(conv_bc, tap, layout["bc"] + tap * (conv_bc.shape[1] // LANES))
        head[...] = table[layout["heads"] : layout["heads"] + 2 * ranks, :]

    return kernel


def body(
    tokens,
    cotangent,
    segments,
    routes,
    gate_weights,
    norm_gain,
    w_zx,
    w_bc,
    w_dt,
    conv_x,
    conv_bc,
    dt_bias,
    a_log,
    d_skip,
    mix_gain,
    w_out,
    post_gain,
    exp_gate,
    exp_up,
    exp_down,
    sh_gate,
    sh_up,
    sh_down,
):
    tensor_count = lax.axis_size("tensor")
    tensor_rank = lax.axis_index("tensor")
    pair, core = tensor_rank // 2, tensor_rank % 2
    dp_count = lax.axis_size("dp")
    here = jnp.stack([*place(), core, pair]).astype(jnp.int32)
    quarter = tokens.shape[0]
    block_rows = segments.shape[0]
    model_dim = tokens.shape[1]
    shard = w_zx.shape[0]
    inner = w_zx.shape[2]
    heads = w_dt.shape[1]
    head_dim = inner // heads
    state = w_bc.shape[2]
    conv_taps = conv_x.shape[0]
    inner_total = inner * tensor_count
    head_total = heads * tensor_count
    experts = exp_gate.shape[0]
    ffe = exp_gate.shape[2]
    ffs = sh_gate.shape[1]
    hidden = experts * ffe + ffs
    wide_in = 2 * inner + 2 * state + LANES

    shards = [
        w_zx,
        w_bc,
        w_dt,
        w_out.T,
        exp_gate,
        sh_gate,
        exp_up,
        sh_up,
        exp_down.transpose(0, 2, 1),
        sh_down.T,
    ]
    in_columns, mix_columns, rest_columns = wide_in, wide_in + inner, 3 * hidden
    in_split, rest_split = mix_columns // 256 * LANES, rest_columns // 256 * LANES
    plan, pack_columns = pack_plan(shards, 4, in_split, rest_split)
    pack = kernel_call(pack_blocks(plan, pack_columns), [shape_of((shard, pack_columns), bf16)], *shards, alone=True)[0]
    near = shift(pack, "z", 1)
    mids = spread(pack, near, in_split + rest_split)
    cuts = (in_split, mix_columns - in_split)
    in_mids = [
        jnp.concatenate([part[:, :, :cut] for part in parts], 0) for parts, cut in zip(mids, cuts, strict=True)
    ]
    in_rings = finish(in_mids)
    rows_all = lax.all_gather(tokens, "tensor", axis=0, tiled=True)
    cot_all = lax.all_gather(cotangent, "tensor", axis=0, tiled=True)
    seg_lanes = jnp.broadcast_to(segments.astype(f32)[:, None], (block_rows, LANES))
    normed_in, normed_own, tail_sent = kernel_call(
        input_rows(quarter),
        [
            shape_of((block_rows, model_dim), bf16),
            shape_of((quarter, model_dim), bf16),
            shape_of((EDGE, model_dim + LANES), bf16),
        ],
        here, rows_all, seg_lanes, norm_gain[None, :],
        small=(0,),
    )
    tail_rows = from_behind(tail_sent, "dp", 1)
    head_start = tensor_rank * heads
    chan_start = tensor_rank * inner
    bias_local = lax.dynamic_slice_in_dim(dt_bias, head_start, heads)
    alog_local = lax.dynamic_slice_in_dim(a_log, head_start, heads)
    skip_local = lax.dynamic_slice_in_dim(d_skip, head_start, heads)
    gain_row = lax.dynamic_slice_in_dim(mix_gain, chan_start, inner)[None, :]
    convx_local = lax.dynamic_slice_in_dim(conv_x, chan_start, inner, 1)
    taps = jnp.concatenate([convx_local, conv_bc.reshape(conv_taps, 2 * state)], 1)
    taps = jnp.pad(taps, ((0, conv_taps), (0, 0)))
    bias_row = jnp.pad(bias_local, (0, LANES - heads))[None, :]
    alog_row = jnp.pad(alog_local, (0, LANES - heads))[None, :]
    skip_row = jnp.repeat(skip_local, head_dim)[None, :]

    hot = routes[:, :, None] == jnp.arange(LANES, dtype=jnp.int32)[None, None, :]
    share = jnp.sum(jnp.where(hot, gate_weights[:, :, None], 0.0), 1)
    early = (tail_rows, taps, bias_row, alog_row, skip_row, gain_row, share)
    in_pieces = finish_far(in_rings, finish_cut(in_rings, early))
    rest_mids = kernel_call(
        join_mids(cuts),
        [shape_of((8, shard, parts[0].shape[2] - cut), bf16) for parts, cut in zip(mids, cuts, strict=True)],
        *[part for parts in mids for part in parts],
        raw=range(10),
        alone=True,
        scratch=[pltpu.SemaphoreType.DMA((10,))],
        wait=in_pieces,
    )
    rest_rings = finish(rest_mids)
    rest_cut = finish_cut(rest_rings, ())
    rest_pieces = finish_far(rest_rings, rest_cut)

    scan_flops = 2 * block_rows * block_rows * inner * 2
    size = inner // dp_count
    state_shape = shape_of((dp_count, size + SUB, state))
    proj, lags, y_first, conv, cum, steps, state_sum = kernel_call(
        scan_front(heads, inner, state, shard, column_ranges(in_split, 0, in_columns)),
        [
            shape_of((block_rows + EDGE, in_columns)),
            shape_of((block_rows, LANES)),
            shape_of((block_rows, inner)),
            shape_of((block_rows, inner + 2 * state)),
            shape_of((block_rows, LANES)),
            shape_of((block_rows, LANES)),
            state_shape,
        ],
        here, normed_in, tail_rows, taps, seg_lanes, bias_row, alog_row, skip_row, *in_pieces,
        flops=scan_flops + 2 * block_rows * model_dim * in_columns,
        small=(0,),
        raw=range(8, 8 + len(in_pieces)),
        scratch=[
            pltpu.VMEM((block_rows, inner + 2 * state), f32),
            pltpu.VMEM((inner, state), f32),
            pltpu.VMEM((model_dim, in_columns), bf16),
            pltpu.VMEM((block_rows + EDGE, LANES), f32),
            pltpu.SemaphoreType.DMA((64,)),
        ],
    )
    entering = exchange_states(state_sum, size, "dp", False, rest_mids)
    w_back, y_all, mixer_in, mine, theirs = kernel_call(
        gate_front(heads, inner, state, shard, column_ranges(in_split, in_columns, in_columns + inner)),
        [
            shape_of((model_dim, inner), bf16),
            shape_of((block_rows, inner)),
            shape_of((block_rows, inner), bf16),
            shape_of((2 * quarter, model_dim + LANES)),
            shape_of((2 * quarter, model_dim + LANES)),
        ],
        here, y_first, proj, conv, cum, entering, gain_row, *in_pieces,
        flops=scan_flops,
        small=(0,),
        raw=range(7, 7 + len(in_pieces)),
        scratch=[
            pltpu.VMEM((block_rows, inner), bf16),
            pltpu.VMEM((block_rows, model_dim + LANES), f32),
            pltpu.SemaphoreType.DMA((64,)),
        ],
    )
    core_total, sent = kernel_call(
        core_sum(model_dim),
        [shape_of((2 * quarter, model_dim)), shape_of((2 * quarter, model_dim + LANES), bf16)],
        mine, other(theirs, 1),
        wait=[ring[1:] for ring in rest_rings],
    )
    from_pair = other(sent, 2)
    middle, post_mine, scales = kernel_call(
        middle_rows(quarter, model_dim, inner_total),
        [
            shape_of((2 * quarter, model_dim)),
            shape_of((2 * quarter, model_dim), bf16),
            shape_of((2 * quarter, LANES)),
        ],
        here, sent, from_pair, rows_all, post_gain[None, :],
        small=(0,),
    )
    post_theirs = other(post_mine, 1)
    half_shape = (2 * quarter, model_dim)
    post, cot, act, d_pre, ffn_mine, ffn_theirs, dpost_mine, dpost_theirs = kernel_call(
        experts_both(quarter, hidden, ffe, experts, shard, column_ranges(rest_split, 0, 3 * hidden)),
        [
            shape_of((block_rows, model_dim), bf16),
            shape_of((block_rows, model_dim), bf16),
            shape_of((block_rows, hidden), bf16),
            shape_of((block_rows, 2 * hidden), bf16),
            shape_of(half_shape),
            shape_of(half_shape, bf16),
            shape_of(half_shape),
            shape_of(half_shape, bf16),
        ],
        here, post_mine, post_theirs, cot_all, share, *rest_pieces,
        flops=12 * block_rows * model_dim * hidden,
        small=(0,),
        raw=range(5, 5 + len(rest_pieces)),
        scratch=[
            pltpu.VMEM((model_dim, 3 * hidden), bf16),
            pltpu.VMEM((block_rows, LANES), f32),
            pltpu.VMEM((block_rows, hidden), f32),
            pltpu.VMEM((block_rows, hidden), f32),
            pltpu.SemaphoreType.DMA((64,)),
        ],
    )
    ffn_split = (3 * hidden) // 256 * LANES
    ffn_plan = (((0, 2, 0, ffn_split),), ((0, 2, ffn_split, 2 * hidden), (1, 3, 0, hidden)))
    sent_post = kernel_call(add_round(), [shape_of(half_shape, bf16)], dpost_mine, other(dpost_theirs, 1))[0]
    ffn_chunks = scatter_begin(here, ffn_plan, (post, cot, d_pre, act), shard)
    ffn_sent, ffn_terms = ring_send(ffn_chunks, "xy")
    d_middle, back_mine, grad_post_gain = kernel_call(
        middle_back(quarter, model_dim, inner_total),
        [
            shape_of(half_shape),
            shape_of((2 * quarter, model_dim + LANES), bf16),
            shape_of((1, model_dim)),
        ],
        here, sent_post, other(sent_post, 2), cot_all, middle, scales, core_total, from_pair,
        post_gain[None, :],
        small=(0,),
    )
    back_theirs = other(back_mine, 1)
    d_proj, d_y, d_z, grad_gain, d_enter = kernel_call(
        gate_back(heads, inner, state),
        [
            shape_of((block_rows, model_dim), bf16),
            shape_of((block_rows, inner)),
            shape_of((block_rows, inner), bf16),
            shape_of((1, inner)),
            state_shape,
        ],
        here, back_mine, back_theirs, w_back, y_all, proj, conv, cum, gain_row,
        flops=scan_flops,
        small=(0,),
        scratch=[
            pltpu.VMEM((inner, state), f32),
            pltpu.VMEM((block_rows, LANES), f32),
            pltpu.VMEM((block_rows, inner), f32),
        ],
    )

    ffn_own, ffn_away = kernel_call(
        add_split(quarter),
        [shape_of((quarter, model_dim)), shape_of((quarter, model_dim), bf16)],
        here, ffn_mine, other(ffn_theirs, 1),
        small=(0,),
    )
    block_out = kernel_call(
        layer_out(quarter),
        [shape_of((quarter, model_dim))],
        here, ffn_own, other(ffn_away, 2), middle,
        small=(0,),
    )[0]

    leaving = exchange_states(d_enter, size, "dp", True)
    ffn_widths = widths_of(ffn_plan)
    ffn_added = ring_added(ffn_sent, ffn_terms, ffn_widths, 4 * shard)
    d_x, d_bc, tail, d_dt, grad_taps, grad_heads, grad_skip = kernel_call(
        scan_back(heads, inner, state),
        [
            shape_of((block_rows, inner)),
            shape_of((block_rows, 2 * state)),
            shape_of((EDGE, inner + 2 * state)),
            shape_of((block_rows, LANES), bf16),
            shape_of((SUB, inner + 2 * state)),
            shape_of((SUB, LANES)),
            shape_of((1, inner)),
        ],
        proj, taps, lags, bias_row, alog_row, skip_row, conv, cum, steps, d_y, entering, leaving,
        flops=3 * scan_flops,
        wait=ffn_added,
        scratch=[
            pltpu.VMEM((block_rows, inner + 2 * state), f32),
            pltpu.VMEM((LANES, block_rows), f32),
            pltpu.VMEM((block_rows + EDGE, inner + 2 * state), f32),
        ],
    )
    tail = from_behind(tail, "dp", -1)
    ffn_rings = ring_passed(ffn_sent, ffn_terms, ffn_added, "xy")
    ffn_totals = kernel_call(
        ring_total(), [shape_of((8 * shard, width), bf16) for width in ffn_widths], *ffn_rings, whole=True
    )
    bc_half = shape_of((block_rows, state))
    bc_mine, bc_theirs = kernel_call(
        bc_split(state, inner),
        [bc_half] * 2,
        here, d_bc, tail,
        small=(0,),
        scratch=[pltpu.VMEM((block_rows, 2 * state), f32)],
    )
    bc_sum = kernel_call(add_exact(), [bc_half], bc_mine, other(bc_theirs, 1))[0]
    dt_at = 2 * inner
    bc_at = dt_at + LANES
    out_at = bc_at + state
    mix_split = (out_at + inner) // 256 * LANES
    mix_plan = (((0, 3, 0, mix_split),), ((0, 3, mix_split, out_at), (1, 2, 0, inner)))
    mix_widths = widths_of(mix_plan)
    *mix_chunks, d_all = scatter_begin(
        here, mix_plan,
        (normed_in, d_proj, mixer_in, d_z, d_x, tail, d_dt, bc_sum, other(bc_sum, 2)),
        shard, join_grads(inner), 6, out_at, ffn_totals,
    )
    mix_sent, mix_terms = ring_send(mix_chunks, "xy")
    din_mine, din_theirs, grad_norm = kernel_call(
        input_back(quarter, inner, state, shard, column_ranges(in_split, 0, in_columns)),
        [shape_of(half_shape), shape_of(half_shape, bf16), shape_of((1, model_dim))],
        here, d_all, rows_all, *in_pieces,
        flops=2 * block_rows * model_dim * in_columns,
        small=(0,),
        raw=range(3, 3 + len(in_pieces)),
        scratch=[
            pltpu.VMEM((block_rows, model_dim), f32),
            pltpu.VMEM((model_dim, in_columns), bf16),
            pltpu.SemaphoreType.DMA((64,)),
        ],
    )
    din_own, din_sent = kernel_call(
        add_split(quarter),
        [shape_of((quarter, model_dim)), shape_of((quarter, model_dim), bf16)],
        here, din_mine, other(din_theirs, 1),
        small=(0,),
    )
    grad_tokens = kernel_call(
        input_grad(quarter),
        [shape_of((quarter, model_dim))],
        here, din_own, other(din_sent, 2), tokens, d_middle, norm_gain[None, :],
        small=(0,),
    )[0]
    layout = small_rows(model_dim, inner, state, conv_taps, tensor_count)
    table_shape = shape_of((dp_count, SUB, LANES))
    table = kernel_call(
        small_table(layout, inner, state, conv_taps, heads),
        [table_shape],
        here, grad_norm, grad_post_gain, grad_taps, grad_gain, grad_heads, grad_skip,
        small=(0,),
        scratch=[pltpu.VMEM((dp_count * EACH, LANES), f32)],
    )[0]
    table = lax.all_to_all(table, "dp", 0, 0, tiled=True)
    mix_rings = ring_pass(mix_sent, mix_terms, mix_widths, "xy", 4 * shard, (grad_tokens, block_out))
    devices = dp_count * tensor_count
    table = kernel_call(small_sum(), [shape_of((devices, SUB, LANES))], table)[0]
    table_end = lax.all_to_all(table, ("dp", "tensor"), 0, 0, tiled=True)
    small = kernel_call(
        small_out(layout, tensor_count, inner, state, conv_taps),
        [
            shape_of((1, model_dim)),
            shape_of((1, model_dim)),
            shape_of((conv_taps, inner_total)),
            shape_of((conv_taps, 2 * state)),
            shape_of((1, inner_total)),
            shape_of((1, inner_total)),
            shape_of((2 * tensor_count, LANES)),
        ],
        table_end,
        scratch=[pltpu.VMEM((dp_count * EACH, LANES), f32)],
    )
    norm_sum, post_sum, taps_x, taps_bc, gain_sum, skip_sum, head_sums = small
    head_grads = head_sums.reshape(2, tensor_count, LANES)[:, :, :heads].reshape(2, -1)
    small_outs = (
        norm_sum[0],
        post_sum[0],
        head_grads[0],
        head_grads[1],
        jnp.sum(skip_sum.reshape(head_total, head_dim), 1),
        gain_sum[0],
    )
    widths = [one + two for one, two in zip(ffn_widths, mix_widths, strict=True)]
    chunks = kernel_call(
        ring_fold(shard), chunk_shapes(shard, widths), here, *ffn_totals, *mix_rings,
        small=(0,),
        scratch=[pltpu.VMEM((8 * shard, width), f32) for width in widths],
        whole=True,
        wait=table,
    )
    sent, terms = ring_send(chunks, "yx")
    results = ring_pass(sent, terms, widths, "yx", shard, table_end)
    sum_shape = (shard, sum(widths))
    mine, sent = kernel_call(
        ring_end(shard, widths), [shape_of(sum_shape), shape_of(sum_shape, bf16)], here, *results,
        small=(0,),
        whole=True,
    )
    def found(group, first, columns):
        ffn_wide, mix_wide = ffn_widths[0], mix_widths[0]
        entries = []
        for at in range(first, first + columns, LANES):
            half, shift_by = (0, 0) if at < (ffn_wide, mix_wide)[group] else (1, (ffn_wide, mix_wide)[group])
            begin = half * widths[0] + (ffn_widths[half] if group else 0)
            entries.append((at - first, begin + at - shift_by, LANES))
        return entries

    def plain(group, first, columns):
        return [(None, *entry) for entry in found(group, first, columns)]

    def by_expert(first):
        entries = found(0, first, experts * ffe)
        return [(at // ffe, at % ffe, begin, columns) for at, begin, columns in entries]

    wide_e = experts * ffe
    out_plan = [
        plain(1, 0, 2 * inner),
        plain(1, dt_at, LANES),
        plain(1, bc_at, state),
        plain(1, out_at, inner),
        by_expert(0),
        by_expert(hidden),
        by_expert(2 * hidden),
        plain(0, wide_e, ffs),
        plain(0, hidden + wide_e, ffs),
        plain(0, 2 * hidden + wide_e, ffs),
    ]
    grad_zx, grad_dt, bc_half, grad_out, grad_eg, grad_eu, grad_ed, grad_sg, grad_su, grad_sd = kernel_call(
        grad_blocks(out_plan, shard),
        [
            shape_of((shard, 2, inner)),
            shape_of((shard, LANES)),
            shape_of((shard, state)),
            shape_of((shard, inner)),
            *[shape_of((experts, shard, ffe))] * 3,
            *[shape_of((shard, ffs))] * 3,
        ],
        mine, shift(sent, "z", 1),
        wait=small_outs,
    )
    bc_far = other(bc_half, 1)
    grad_bc = jnp.stack([jnp.where(core == 0, bc_half, bc_far), jnp.where(core == 0, bc_far, bc_half)], 1)
    return (
        block_out,
        grad_tokens,
        small_outs[0],
        grad_zx,
        grad_bc,
        grad_dt[:, :heads],
        taps_x,
        taps_bc.reshape(conv_taps, 2, state),
        small_outs[2],
        small_outs[3],
        small_outs[4],
        small_outs[5],
        grad_out.T,
        small_outs[1],
        grad_eg,
        grad_eu,
        grad_ed.transpose(0, 2, 1),
        grad_sg,
        grad_su,
        grad_sd.T,
    )


def solution(mesh):
    in_specs = (
        P(("dp", "tensor"), None),
        P(("dp", "tensor"), None),
        P("dp"),
        P("dp", None),
        P("dp", None),
        P(),
        P("dp", None, "tensor"),
        P("dp", None, None),
        P("dp", "tensor"),
        P(),
        P(),
        P(),
        P(),
        P(),
        P(),
        P("tensor", "dp"),
        P(),
        P(None, "dp", "tensor"),
        P(None, "dp", "tensor"),
        P(None, "tensor", "dp"),
        P("dp", "tensor"),
        P("dp", "tensor"),
        P("tensor", "dp"),
    )
    out_specs = (
        P(("dp", "tensor"), None),
        P(("dp", "tensor"), None),
        P(),
        P("dp", None, "tensor"),
        P("dp", None, None),
        P("dp", "tensor"),
        P(),
        P(),
        P(),
        P(),
        P(),
        P(),
        P("tensor", "dp"),
        P(),
        P(None, "dp", "tensor"),
        P(None, "dp", "tensor"),
        P(None, "tensor", "dp"),
        P("dp", "tensor"),
        P("dp", "tensor"),
        P("tensor", "dp"),
    )
    return jax.shard_map(body, mesh=mesh, in_specs=in_specs, out_specs=out_specs, check_vma=False)
```

```python
import math

import jax
import jax.numpy as jnp
from jax import lax
from jax.experimental import pallas as pl
from jax.experimental.pallas import tpu as pltpu
from jax.sharding import PartitionSpec as P

f32 = jnp.float32
bf16 = jnp.bfloat16
eps = 1e-05
highest = lax.Precision.HIGHEST
LANES = 128
DP_SHAPE = (4, 2, 4)
EDGE = 16
SUB = 8
RAW_LIMIT = 48 * 1024 * 1024
WHOLE_LIMIT = 62 * 1024 * 1024
RING_SPARE = 4 * 1024 * 1024
VMEM_SPARE = 8 * 1024 * 1024

NN = (((1,), (0,)), ((), ()))
NT = (((1,), (1,)), ((), ()))
TN = (((0,), (0,)), ((), ()))


def dot(a, b, dims=NN):
    return lax.dot_general(a.astype(bf16), b.astype(bf16), dims, preferred_element_type=f32)


def dot_exact(a, b, dims=NN):
    return lax.dot_general(a, b, dims, precision=highest, preferred_element_type=f32)


def halves(value):
    high = value.astype(bf16)
    return high, (value - high.astype(f32)).astype(bf16)


def dot_left(a, b, dims=NN):
    high, low = halves(a)
    return dot(high, b, dims) + dot(low, b, dims)


def dot_both(a, b, dims=NN):
    a_high, a_low = halves(a)
    b_high, b_low = halves(b)
    return dot(a_high, b_high, dims) + (dot(a_low, b_high, dims) + dot(a_high, b_low, dims))


def from_behind(value, axis, steps):
    count = lax.axis_size(axis)
    leading, last = (max(0, -steps), min(count, count - steps))
    return lax.ppermute(value, axis, [(source, source + steps) for source in range(leading, last)])


def kernel_call(kernel, out_shapes, *args, flops=0, scratch=(), small=(), raw=(), whole=False, alone=False, wait=()):
    moved = sum(a.size * a.dtype.itemsize for a in args)
    moved += sum(s.size * s.dtype.itemsize for s in out_shapes)
    kept = [a for i, a in enumerate(args) if i not in raw and i not in small] + list(out_shapes)
    kept += [s for s in scratch if s.dtype in (f32, bf16)]
    held = sum(math.prod(a.shape) * (4 if a.dtype == f32 else 2) for a in kept)
    limit = held + (RING_SPARE if whole else VMEM_SPARE)
    limit = WHOLE_LIMIT if alone else max(limit, RAW_LIMIT if len(raw) > 1 else 0)
    spaces = [
        pltpu.SMEM if i in small else pl.ANY if i in raw else pltpu.VMEM for i in range(len(args))
    ]
    wait = jax.tree.leaves(wait)
    count = len(args)

    def body_of(*refs):
        kernel(*refs[:count], *refs[count + len(wait) :])

    return pl.pallas_call(
        body_of,
        name=kernel.__qualname__.split(".")[0],
        out_shape=out_shapes,
        in_specs=[pl.BlockSpec(memory_space=space) for space in spaces + [pl.ANY] * len(wait)],
        scratch_shapes=scratch,
        compiler_params=pltpu.CompilerParams(vmem_limit_bytes=limit),
        cost_estimate=pl.CostEstimate(flops=flops, bytes_accessed=moved, transcendentals=0),
    )(*args, *wait)


def shape_of(shape, dtype=f32):
    return jax.ShapeDtypeStruct(shape, dtype)


def ids(shape, dim):
    return lax.broadcasted_iota(jnp.int32, shape, dim)


def per_head(columns, pair, rows):
    left = ids((rows, LANES), 1) < LANES // 2
    return jnp.where(left, columns[:, 2 * pair : 2 * pair + 1], columns[:, 2 * pair + 1 : 2 * pair + 2])


def run_info(cum, heads):
    rows = cum.shape[0]
    turned = cum.T
    run_col = cum[:, heads : heads + 1]
    run_row = turned[heads : heads + 1, :]
    keep = (ids((rows, rows), 0) >= ids((rows, rows), 1)) & (run_col == run_row)
    return turned, run_col, run_col[rows - 1 : rows, :], keep


HALVED = ((0, 0, 8), (-1, 0, 8), (1, 0, 8), (2, 0, 4), (2, 4, 4))


def load_blocks(pieces, target, done, here, ranges, shard, form):
    x_size, z_size, y_size = DP_SHAPE
    x, z, y = here[0], here[1], here[2]
    copies = []
    for half, start, at, width in ranges:
        for index, (far, begin, blocks) in enumerate(form):
            for block in range(blocks):
                place_in = begin + block
                near = RING[place_in // 2]
                to_x, to_y = (far, near) if half == 0 else (near, far)
                to_x = lax.rem(x + (to_x + x_size), x_size)
                to_y = lax.rem(y + (to_y + y_size), y_size)
                to_z = lax.rem(z + place_in % 2, z_size)
                row = pl.multiple_of(((to_x * z_size + to_z) * y_size + to_y) * shard, 16)
                copy = pltpu.make_async_copy(
                    pieces[half * len(form) + index].at[block, :, pl.ds(start, width)],
                    target.at[pl.ds(row, shard), pl.ds(at, width)],
                    done.at[len(copies)],
                )
                copy.start()
                copies.append(copy)
    return copies


def wait_all(copies):
    for copy in copies:
        copy.wait()


def column_ranges(split, first, last):
    ranges = []
    if first < split:
        ranges.append((0, first, 0, min(last, split) - first))
    if last > split:
        begin = max(first, split)
        ranges.append((1, begin - split, begin - first, last - begin))
    return ranges


def rows_at(index, quarter):
    return pl.ds(pl.multiple_of(index * quarter, quarter), quarter)


def silu_slope(value, sigma):
    return sigma * (1.0 + value * (1.0 - sigma))


def pack_blocks(plan, width):
    def kernel(*refs):
        ins, out = refs[:-1], refs[-1]
        for arg, lead, first, columns, at in plan:
            if columns % LANES:
                out[:, at : at + LANES] = jnp.zeros((out.shape[0], LANES), bf16)
            ref = ins[arg]
            if lead is None:
                value = ref[:, first : first + columns]
            elif ref.shape[0] == out.shape[0]:
                value = ref[:, lead, first : first + columns]
            else:
                value = ref[lead, :, first : first + columns]
            out[:, at : at + columns] = value

    return kernel


def pack_plan(args, in_count, in_split, rest_split):
    plan, sizes, at, group = [], [0, 0], 0, 0
    entries = []
    for arg, value in enumerate(args):
        if arg == in_count:
            group, at = 1, 0
        for lead in range(min(value.shape[:2])) if len(value.shape) == 3 else (None,):
            for first in range(0, value.shape[-1], LANES):
                columns = min(LANES, value.shape[-1] - first)
                entries.append((group, at, arg, lead, first, columns))
                at += LANES
        sizes[group] = at
    splits = (in_split, rest_split)
    for group, at, arg, lead, first, columns in entries:
        if at < splits[group]:
            to = at + (in_split if group else 0)
        else:
            to = in_split + rest_split + at - splits[group] + (sizes[0] - in_split if group else 0)
        plan.append((arg, lead, first, columns, to))
    return plan, sum(sizes)


def input_rows(quarter):
    def kernel(here, rows_in, ids_in, gain, normed_out, own_out, tail_out):
        rank = here[4] * 2 + here[3]
        rows, width = rows_in.shape
        value = rows_in[...].astype(f32)
        scale = lax.rsqrt(jnp.mean(value * value, -1, keepdims=True) + eps)
        normed = (value * scale * gain[...]).astype(bf16)
        normed_out[...] = normed
        own_out[...] = normed_out[rows_at(rank, quarter), :]
        tail_out[:, :width] = normed[rows - EDGE :, :]
        tail_out[:, width:] = ids_in[rows - EDGE :, :].astype(bf16)

    return kernel


def scan_front(heads, inner, state, shard, ranges):
    pairs = heads // 2
    tiles = (inner + 2 * state) // LANES

    def kernel(here, normed, tail, taps, ids_in, bias, alog, skip, *refs):
        pieces, refs = refs[: 2 * len(HALVED)], refs[2 * len(HALVED) :]
        proj, lags, y_out, conv_out, cum_out, steps_out, state_out, act, sums, weights_in, ids_ext, done = refs
        copies = load_blocks(pieces, weights_in, done, here, ranges, shard, HALVED)
        columns = weights_in.shape[1]
        wide = 3 * LANES
        rows, depth = normed.shape
        ids_ext[0:EDGE, :] = tail[:, depth:].astype(f32)
        ids_ext[EDGE:, :] = ids_in[...]
        lane = ids((rows, LANES), 1)
        row = ids((rows, LANES), 0)
        no_row_before = here[0] + here[1] + here[2] == 0
        lags[...] = jnp.zeros_like(lags)
        for back in range(taps.shape[0] // 2):
            same = ids_ext[EDGE - back : EDGE - back + rows, :] == ids_in[...]
            same = same & ((row >= back) | jnp.logical_not(no_row_before))
            lags[...] = jnp.where((lane == back) & same, 1.0, lags[...])
        first = len(copies) // 2
        wait_all(copies[:first])
        for at in range(0, columns, wide):
            if at + wide > ranges[0][3] and first:
                wait_all(copies[first:])
                first = 0
            part = weights_in[:, at : at + wide]
            proj[0:EDGE, at : at + wide] = dot(tail[:, :depth], part)
            proj[EDGE:, at : at + wide] = dot(normed[...], part)
        count = taps.shape[0] // 2
        for tile in range(tiles):
            at = tile * LANES
            total = jnp.zeros((rows, LANES), f32)
            for back in range(count):
                source = proj[EDGE - back : EDGE - back + rows, inner + at : inner + at + LANES]
                weight = taps[count - 1 - back : count - back, at : at + LANES]
                total = total + weight * source * lags[:, back : back + 1]
            conv_out[:, at : at + LANES] = total
            act[:, at : at + LANES] = total * jax.nn.sigmoid(total)
        b_rows = act[:, inner : inner + state]
        c_rows = act[:, inner + state : inner + 2 * state]
        raw = proj[EDGE : EDGE + rows, 2 * inner + 2 * state :] + bias[...]
        steps = jnp.maximum(raw, 0.0) + jnp.log1p(jnp.exp(-jnp.abs(raw)))
        reset = 1.0 - lags[:, 1:2]
        logs = jnp.where(lane < heads, -steps * jnp.exp(alog[...]), jnp.where(lane == heads, reset, 0.0))
        lower = (ids((rows, rows), 0) >= ids((rows, rows), 1)).astype(f32)
        cum = dot_exact(lower, logs)
        steps_out[...] = steps
        cum_out[...] = cum
        turned, run_col, last_run, keep = run_info(cum, heads)
        inner_cb = dot_exact(c_rows, b_rows, NT)
        closing = jnp.where(run_col == last_run, jnp.exp(cum[rows - 1 : rows, :] - cum), 0.0)
        left = ids((rows, LANES), 1) < LANES // 2
        for pair in range(pairs):
            at = pair * LANES
            x_pair = act[:, at : at + LANES]
            scaled = x_pair * per_head(steps, pair, rows)
            parts = []
            for head in (2 * pair, 2 * pair + 1):
                gaps = cum[:, head : head + 1] - turned[head : head + 1, :]
                weights = jnp.exp(jnp.where(keep, gaps, -jnp.inf)) * inner_cb
                parts.append(dot_left(weights, scaled))
            y_out[:, at : at + LANES] = (
                jnp.where(left, parts[0], parts[1]) + skip[:, at : at + LANES] * x_pair
            )
            sums[at : at + LANES, :] = dot_both(scaled * per_head(closing, pair, rows), b_rows, TN)
        last = cum[rows - 1 : rows, :]
        fill_states(state_out, sums, jnp.where(last_run == 0.0, jnp.exp(last), 0.0), heads)

    return kernel


def fill_states(out, sums, keep, heads):
    blocks, size = out.shape[0], sums.shape[0] // out.shape[0]
    head_rows = sums.shape[0] // heads
    row_head = (ids((blocks, LANES), 0) * size + ids((blocks, LANES), 1)) // head_rows
    table = jnp.zeros((blocks, LANES), f32)
    for head in range(heads):
        table = jnp.where(row_head == head, keep[:, head : head + 1], table)
    for block in range(blocks):
        out[block, 0:size, :] = sums[block * size : (block + 1) * size, :]
        out[block, size : size + SUB, :] = jnp.broadcast_to(table[block : block + 1, :], (SUB, LANES))


def gate_front(heads, inner, state, shard, ranges):
    pairs = heads // 2

    def kernel(here, y_in, proj, conv, cum_in, entering, gain, *refs):
        pieces, refs = refs[: 2 * len(HALVED)], refs[2 * len(HALVED) :]
        w_back, y_out, mixed_out, mine_out, theirs_out, mixed_low, partial, done = refs
        copies = load_blocks(pieces, w_back, done, here, ranges, shard, HALVED)
        rows = y_in.shape[0]
        quarter = rows // 4
        width = partial.shape[1] - LANES
        core = here[3]
        cum = cum_in[...]
        opening = jnp.where(cum[:, heads : heads + 1] == 0.0, jnp.exp(cum), 0.0)
        c_conv = conv[:, inner + state : inner + 2 * state]
        c_rows = c_conv * jax.nn.sigmoid(c_conv)
        squares = jnp.zeros((rows, LANES), f32)
        for pair in range(pairs):
            at = pair * LANES
            y_pair = y_in[:, at : at + LANES] + per_head(opening, pair, rows) * dot_both(
                c_rows, entering[at : at + LANES, :], NT
            )
            z_pair = proj[EDGE : EDGE + rows, at : at + LANES]
            gated = y_pair * z_pair * jax.nn.sigmoid(z_pair)
            y_out[:, at : at + LANES] = y_pair
            high, low = halves(gated * gain[:, at : at + LANES])
            mixed_out[:, at : at + LANES] = high
            mixed_low[:, at : at + LANES] = low
            squares = squares + gated * gated
        total = jnp.sum(squares, 1, keepdims=True)
        partial[:, width:] = jnp.broadcast_to(total, (rows, LANES))
        wait_all(copies)
        wide = 2 * LANES
        for at in range(0, width, wide):
            part = w_back[at : at + wide, :]
            partial[:, at : at + wide] = dot(mixed_out[...], part, NT) + dot(mixed_low[...], part, NT)
        for half in range(2):
            to = slice(half * quarter, (half + 1) * quarter)
            mine_out[to, :] = partial[rows_at(2 * half + core, quarter), :]
            theirs_out[to, :] = partial[rows_at(2 * half + 1 - core, quarter), :]

    return kernel


def core_sum(width):
    def kernel(mine, theirs, sum_out, sent_out):
        total = mine[...] + theirs[...]
        sum_out[...] = total[:, :width]
        sent_out[:, :width] = total[:, :width].astype(bf16)
        squares = total[:, width : width + 1]
        high = squares.astype(bf16).astype(f32)
        lane = ids((total.shape[0], LANES), 1)
        sent_out[:, width:] = jnp.where(lane == 0, high, jnp.where(lane == 1, squares - high, 0.0)).astype(bf16)

    return kernel


def middle_rows(quarter, width, inner_total):
    def kernel(here, sent, got, rows_in, gain, middle_out, post_out, scales_out):
        core = here[3]
        total = sent[...].astype(f32) + got[...].astype(f32)
        squares = total[:, width : width + 1] + total[:, width + 1 : width + 2]
        scale_mix = lax.rsqrt(squares / inner_total + eps)
        for half in range(2):
            to = slice(half * quarter, (half + 1) * quarter)
            middle_out[to, :] = rows_in[rows_at(2 * half + core, quarter), :].astype(f32)
        middle = middle_out[...] + scale_mix * total[:, :width]
        middle_out[...] = middle
        scale = lax.rsqrt(jnp.mean(middle * middle, -1, keepdims=True) + eps)
        post_out[...] = (middle * scale * gain[...]).astype(bf16)
        lane = ids((2 * quarter, LANES), 1)
        scales_out[...] = jnp.where(lane == 0, scale_mix, scale)

    return kernel


def experts_both(quarter, hidden, ffe, experts, shard, ranges):
    def kernel(here, post_mine, post_theirs, cot_in, share, *refs):
        pieces, refs = refs[: 2 * len(HALVED)], refs[2 * len(HALVED) :]
        (
            post, cot, act_out, dpre_out, out_mine, out_theirs, dpost_mine, dpost_theirs,
            weights, shares, gates, ups, done,
        ) = refs
        copies = load_blocks(pieces, weights, done, here, ranges, shard, HALVED)
        core = here[3]
        half = 2 * quarter
        width = post.shape[1]
        post[0:half, :] = post_mine[...]
        post[half:, :] = post_theirs[...]
        for index in range(2):
            to = slice(index * quarter, (index + 1) * quarter)
            cot[to, :] = cot_in[rows_at(2 * index + core, quarter), :]
            to = slice(half + index * quarter, half + (index + 1) * quarter)
            cot[to, :] = cot_in[rows_at(2 * index + 1 - core, quarter), :]
            shares[index * quarter : (index + 1) * quarter, :] = share[rows_at(2 * index + core, quarter), :]
            shares[half + index * quarter : half + (index + 1) * quarter, :] = share[
                rows_at(2 * index + 1 - core, quarter), :
            ]
        wide = 2 * LANES
        left = ids((2 * half, wide), 1) < ffe
        first = ranges[0][3]
        wait_all(copies[: len(copies) // 2])
        for at in range(0, hidden, wide):
            gates[:, at : at + wide] = dot(post[...], weights[:, at : at + wide])
        for at in range(0, hidden, wide):
            if hidden + at + wide <= first:
                ups[:, at : at + wide] = dot(post[...], weights[:, hidden + at : hidden + at + wide])
        wait_all(copies[len(copies) // 2 :])
        for at in range(0, hidden, wide):
            gate = gates[:, at : at + wide]
            if hidden + at + wide <= first:
                up = ups[:, at : at + wide]
            else:
                up = dot(post[...], weights[:, hidden + at : hidden + at + wide])
            d_act = dot(cot[...], weights[:, 2 * hidden + at : 2 * hidden + at + wide])
            sigma = jax.nn.sigmoid(gate)
            silu = gate * sigma
            act = silu * up
            expert = at // ffe
            if expert < experts:
                by = jnp.where(left, shares[:, expert : expert + 1], shares[:, expert + 1 : expert + 2])
                act = act * by
                d_act = d_act * by
            act_out[:, at : at + wide] = act.astype(bf16)
            dpre_out[:, at : at + wide] = (d_act * up * silu_slope(gate, sigma)).astype(bf16)
            dpre_out[:, hidden + at : hidden + at + wide] = (d_act * silu).astype(bf16)
        for at in range(0, width, wide):
            d_post = dot(dpre_out[...], weights[at : at + wide, : 2 * hidden], NT)
            dpost_mine[:, at : at + wide] = d_post[:half]
            dpost_theirs[:, at : at + wide] = d_post[half:].astype(bf16)
        for at in range(0, width, wide):
            out = dot(act_out[...], weights[at : at + wide, 2 * hidden :], NT)
            out_mine[:, at : at + wide] = out[:half]
            out_theirs[:, at : at + wide] = out[half:].astype(bf16)

    return kernel


def add_round():
    def kernel(mine, theirs, sent_out):
        sent_out[...] = (mine[...] + theirs[...].astype(f32)).astype(bf16)

    return kernel


def add_split(quarter):
    def kernel(here, mine, theirs, own_out, sent_out):
        pair = here[4]
        own = rows_at(pair, quarter)
        away = rows_at(1 - pair, quarter)
        own_out[...] = mine[own, :] + theirs[own, :].astype(f32)
        sent_out[...] = (mine[away, :] + theirs[away, :].astype(f32)).astype(sent_out.dtype)

    return kernel


def middle_back(quarter, width, inner_total):
    def kernel(
        here, sent, got, cot_in, middle_in, scales, core_total, pair_sent, gain,
        dmiddle_out, back_out, gain_out,
    ):
        core = here[3]
        d_post = sent[...].astype(f32) + got[...].astype(f32)
        middle = middle_in[...]
        scale_mix, scale = scales[:, 0:1], scales[:, 1:2]
        gain_out[...] = 0.5 * jnp.sum(d_post * middle * scale, 0, keepdims=True)
        scaled = d_post * gain[...]
        for half in range(2):
            to = slice(half * quarter, (half + 1) * quarter)
            dmiddle_out[to, :] = cot_in[rows_at(2 * half + core, quarter), :].astype(f32)
        d_middle = (
            dmiddle_out[...]
            + scale * scaled
            - middle * (scale * scale * scale) * jnp.mean(scaled * middle, -1, keepdims=True)
        )
        dmiddle_out[...] = d_middle
        d_proj = (scale_mix * d_middle.astype(bf16).astype(f32)).astype(bf16)
        back_out[:, :width] = d_proj
        projected = core_total[...] + pair_sent[:, :width].astype(f32)
        d_scale = jnp.sum(d_proj.astype(f32) * projected, -1, keepdims=True)
        coeff = -d_scale * scale_mix * scale_mix / inner_total
        high = coeff.astype(bf16).astype(f32)
        lane = ids((2 * quarter, LANES), 1)
        back_out[:, width:] = jnp.where(lane == 0, high, jnp.where(lane == 1, coeff - high, 0.0)).astype(bf16)

    return kernel


def gate_back(heads, inner, state):
    pairs = heads // 2

    def kernel(
        here, back_mine, back_theirs, w_back, y_in, proj, conv, cum_in, gain,
        dproj_out, dy_out, dz_out, gain_out, enter_out, sums, factors, d_mixed,
    ):
        rows = y_in.shape[0]
        quarter = rows // 4
        width = dproj_out.shape[1]
        core = here[3]
        for index in range(2):
            part = slice(index * quarter, (index + 1) * quarter)
            for ref, at in ((back_mine, 2 * index + core), (back_theirs, 2 * index + 1 - core)):
                dproj_out[rows_at(at, quarter), :] = ref[part, :width]
                factors[rows_at(at, quarter), :] = ref[part, width:].astype(f32)
        d_mixed[...] = dot(dproj_out[...], w_back[...])
        cum = cum_in[...]
        opening = jnp.where(cum[:, heads : heads + 1] == 0.0, jnp.exp(cum), 0.0)
        c_conv = conv[:, inner + state : inner + 2 * state]
        c_rows = c_conv * jax.nn.sigmoid(c_conv)
        factor = factors[:, 0:1] + factors[:, 1:2]
        for pair in range(pairs):
            at = pair * LANES
            y_pair = y_in[:, at : at + LANES]
            z_pair = proj[EDGE : EDGE + rows, at : at + LANES]
            sigma = jax.nn.sigmoid(z_pair)
            silu = z_pair * sigma
            gated = y_pair * silu
            d_mix = d_mixed[:, at : at + LANES]
            gain_out[:, at : at + LANES] = jnp.sum(d_mix * gated, 0, keepdims=True)
            d_gated = d_mix * gain[:, at : at + LANES] + factor * gated
            dz_out[:, at : at + LANES] = (d_gated * y_pair * silu_slope(z_pair, sigma)).astype(bf16)
            d_y = d_gated * silu
            dy_out[:, at : at + LANES] = d_y
            sums[at : at + LANES, :] = dot_both(d_y * per_head(opening, pair, rows), c_rows, TN)
        last = cum[rows - 1 : rows, :]
        last_run = last[:, heads : heads + 1]
        fill_states(enter_out, sums, jnp.where(last_run == 0.0, jnp.exp(last), 0.0), heads)

    return kernel


def bc_split(state, inner):
    def kernel(here, d_bc, tail, mine_out, theirs_out, whole):
        core = here[3]
        last = d_bc.shape[0] - EDGE
        whole[0:last, :] = d_bc[0:last, :]
        whole[last:, :] = d_bc[last:, :] + tail[:, inner:]
        first, second = whole[:, :state], whole[:, state:]
        mine_out[...] = jnp.where(core == 0, first, second)
        theirs_out[...] = jnp.where(core == 0, second, first)

    return kernel


def add_exact():
    def kernel(mine, theirs, out):
        out[...] = mine[...] + theirs[...]

    return kernel


def join_grads(inner):
    def prepare(arrays, out):
        d_z, d_x, tail, d_dt, bc_mine, bc_theirs = arrays
        rows = out.shape[0]
        out[:, :inner] = d_z[...]
        out[:, inner : 2 * inner] = d_x[...].astype(bf16)
        out[rows - EDGE :, inner : 2 * inner] = (d_x[rows - EDGE :, :] + tail[:, :inner]).astype(bf16)
        out[:, 2 * inner : 2 * inner + LANES] = d_dt[...]
        out[:, 2 * inner + LANES :] = (bc_mine[...] + bc_theirs[...]).astype(bf16)

    return prepare


def input_back(quarter, inner, state, shard, ranges):
    def kernel(here, d_all, rows_in, *refs):
        pieces, refs = refs[: 2 * len(HALVED)], refs[2 * len(HALVED) :]
        mine_out, theirs_out, gain_out, d_in, win, done = refs
        wait_all(load_blocks(pieces, win, done, here, ranges, shard, HALVED))
        core = here[3]
        rows, width = rows_in.shape
        wide = 2 * LANES
        bc_at = 2 * inner + 2 * state
        d_bc = 0.5 * d_all[:, 2 * inner + LANES :].astype(f32)
        for at in range(0, width, wide):
            part = win[at : at + wide, :]
            w_bc = jnp.where(
                core == 0,
                part[:, 2 * inner : 2 * inner + state].astype(f32),
                part[:, 2 * inner + state : bc_at].astype(f32),
            )
            d_in[:, at : at + wide] = (
                dot(d_all[:, : 2 * inner], part[:, : 2 * inner], NT)
                + dot(d_all[:, 2 * inner : 2 * inner + LANES], part[:, bc_at:], NT)
                + dot(d_bc, w_bc, NT)
            )
        value = rows_in[...].astype(f32)
        scale = lax.rsqrt(jnp.mean(value * value, -1, keepdims=True) + eps)
        gain_out[...] = jnp.sum(d_in[...] * value * scale, 0, keepdims=True)
        for index in range(2):
            part = slice(index * quarter, (index + 1) * quarter)
            mine_out[part, :] = d_in[rows_at(2 * index + core, quarter), :]
            theirs_out[part, :] = d_in[rows_at(2 * index + 1 - core, quarter), :].astype(bf16)

    return kernel


def input_grad(quarter):
    def kernel(here, own_sum, got, tokens, d_middle, gain, grad_out):
        pair = here[4]
        value = tokens[...].astype(f32)
        scale = lax.rsqrt(jnp.mean(value * value, -1, keepdims=True) + eps)
        scaled = (own_sum[...] + got[...].astype(f32)) * gain[...]
        grad_out[...] = (
            d_middle[rows_at(pair, quarter), :]
            + scale * scaled
            - value * (scale * scale * scale) * jnp.mean(scaled * value, -1, keepdims=True)
        )

    return kernel


def layer_out(quarter):
    def kernel(here, own_sum, got, middle, out):
        out[...] = middle[rows_at(here[4], quarter), :] + own_sum[...] + got[...].astype(f32)

    return kernel


def scan_back(heads, inner, state):
    pairs = heads // 2
    tiles = (inner + 2 * state) // LANES

    def kernel(
        proj, taps, lags, bias, alog, skip, conv, cum_in, steps_in, dy_in, entering, leaving,
        dx_out, dbc_out, tail_out, ddt_out, conv_grad, head_grad, skip_grad, dact, rowsums, dpre_out,
    ):
        rows = dy_in.shape[0]
        count = taps.shape[0] // 2
        cum = cum_in[...]
        steps = steps_in[...]
        lane = ids((rows, LANES), 1)
        left = lane < LANES // 2
        turned, run_col, last_run, keep = run_info(cum, heads)
        b_conv = conv[:, inner : inner + state]
        c_conv = conv[:, inner + state : inner + 2 * state]
        b_rows = b_conv * jax.nn.sigmoid(b_conv)
        c_rows = c_conv * jax.nn.sigmoid(c_conv)
        inner_cb = dot_exact(c_rows, b_rows, NT)
        last_cum = cum[rows - 1 : rows, :]
        closing = jnp.where(run_col == last_run, jnp.exp(last_cum - cum), 0.0)
        opening = jnp.where(run_col == 0.0, jnp.exp(cum), 0.0)
        keep_old = jnp.where(last_run == 0.0, jnp.exp(last_cum), 0.0)
        d_cb = jnp.zeros((rows, rows), f32)
        d_b = jnp.zeros((rows, state), f32)
        d_c = jnp.zeros((rows, state), f32)
        d_cum = jnp.zeros((rows, LANES), f32)
        d_steps = jnp.zeros((rows, LANES), f32)
        d_open = jnp.zeros((rows, LANES), f32)
        d_close = jnp.zeros((rows, LANES), f32)
        d_keep = jnp.zeros((1, LANES), f32)
        lane_row = ids((1, LANES), 1)
        rowsums[...] = jnp.zeros_like(rowsums)
        for pair in range(pairs):
            at = pair * LANES
            x_conv = conv[:, at : at + LANES]
            x_pair = x_conv * jax.nn.sigmoid(x_conv)
            d_y = dy_in[:, at : at + LANES]
            step_pair = per_head(steps, pair, rows)
            scaled = x_pair * step_pair
            enter_pair = entering[at : at + LANES, :]
            leave_pair = leaving[at : at + LANES, :]
            close_pair = per_head(closing, pair, rows)
            b_leave = dot(b_rows, leave_pair, NT)
            c_enter = dot(c_rows, enter_pair, NT)
            d_b = d_b + dot_both(scaled * close_pair, leave_pair)
            d_c = d_c + dot_both(d_y * per_head(opening, pair, rows), enter_pair)
            close_prod = b_leave * scaled
            open_prod = d_y * c_enter
            keep_prod = enter_pair * leave_pair
            parts = []
            for side, head in ((0, 2 * pair), (1, 2 * pair + 1)):
                mine = left if side == 0 else ~left
                gaps = cum[:, head : head + 1] - turned[head : head + 1, :]
                decay = jnp.exp(jnp.where(keep, gaps, -jnp.inf))
                weights = decay * inner_cb
                d_weights = dot_left(jnp.where(mine, d_y, 0.0), scaled, NT)
                d_cb = d_cb + d_weights * decay
                flow = d_weights * weights
                d_cum = d_cum + jnp.where(lane == head, jnp.sum(flow, 1, keepdims=True), 0.0)
                rowsums[head : head + 1, :] = jnp.sum(flow, 0, keepdims=True)
                parts.append(dot(weights, d_y, TN))
                half = LANES // 2
                kept = jnp.sum(
                    jnp.sum(keep_prod[side * half : side * half + half, :], 0, keepdims=True), 1, keepdims=True
                )
                d_keep = d_keep + jnp.where(lane_row == head, kept, 0.0)
                d_open = d_open + jnp.where(
                    lane == head, jnp.sum(jnp.where(mine, open_prod, 0.0), 1, keepdims=True), 0.0
                )
                d_close = d_close + jnp.where(
                    lane == head, jnp.sum(jnp.where(mine, close_prod, 0.0), 1, keepdims=True), 0.0
                )
            d_scaled = jnp.where(left, parts[0], parts[1]) + close_pair * b_leave
            skip_grad[:, at : at + LANES] = jnp.sum(d_y * x_pair, 0, keepdims=True)
            dact[:, at : at + LANES] = step_pair * d_scaled + skip[:, at : at + LANES] * d_y
            step_prod = d_scaled * x_pair
            for side, head in ((0, 2 * pair), (1, 2 * pair + 1)):
                mine = left if side == 0 else ~left
                d_steps = d_steps + jnp.where(
                    lane == head, jnp.sum(jnp.where(mine, step_prod, 0.0), 1, keepdims=True), 0.0
                )
        dact[:, inner : inner + state] = d_b + dot_both(d_cb, c_rows, TN)
        dact[:, inner + state : inner + 2 * state] = d_c + dot_both(d_cb, b_rows)
        ended = closing * d_close
        d_last = jnp.sum(ended, 0, keepdims=True) + keep_old * d_keep
        d_cum = d_cum - rowsums[...].T + opening * d_open - ended
        d_cum = d_cum + jnp.where(ids((rows, LANES), 0) == rows - 1, d_last, 0.0)
        upper = (ids((rows, rows), 0) <= ids((rows, rows), 1)).astype(f32)
        d_logs = jnp.where(lane < heads, dot_exact(upper, d_cum), 0.0)
        rate = jnp.exp(alog[...])
        raw = proj[EDGE : EDGE + rows, 2 * inner + 2 * state :] + bias[...]
        d_raw = (d_steps - rate * d_logs) * jax.nn.sigmoid(raw)
        ddt_out[...] = d_raw.astype(bf16)
        head_grad[...] = jnp.zeros_like(head_grad)
        head_grad[0:1, :] = jnp.sum(d_raw, 0, keepdims=True)
        head_grad[1:2, :] = -jnp.sum(d_logs * steps, 0, keepdims=True) * rate
        dpre_out[...] = jnp.zeros_like(dpre_out)
        conv_grad[...] = jnp.zeros_like(conv_grad)
        for tile in range(tiles):
            at = tile * LANES
            value = conv[:, at : at + LANES]
            sigma = jax.nn.sigmoid(value)
            d_conv = dact[:, at : at + LANES] * (sigma * (1.0 + value * (1.0 - sigma)))
            for back in range(count):
                tap = count - 1 - back
                masked = d_conv * lags[:, back : back + 1]
                source = proj[EDGE - back : EDGE - back + rows, inner + at : inner + at + LANES]
                conv_grad[tap : tap + 1, at : at + LANES] = jnp.sum(masked * source, 0, keepdims=True)
                dpre_out[EDGE - back : EDGE - back + rows, at : at + LANES] += (
                    taps[tap : tap + 1, at : at + LANES] * masked
                )
        dx_out[...] = dpre_out[EDGE:, :inner]
        dbc_out[...] = dpre_out[EDGE:, inner:]
        tail_out[...] = dpre_out[0:EDGE, :]

    return kernel


def chain_states(reverse, blocks, size):
    def kernel(parts, carried_out):
        factors = parts[:, size, :].T
        carried = jnp.zeros((size, LANES), f32)
        for turn in range(blocks):
            k = blocks - 1 - turn if reverse else turn
            carried_out[k] = carried.astype(carried_out.dtype)
            carried = factors[0:size, k : k + 1] * carried + parts[k, 0:size, :]

    return kernel


def exchange_states(sent, size, axis, reverse, wait=()):
    blocks = lax.axis_size(axis)
    parts = lax.all_to_all(sent, axis, 0, 0, tiled=True)
    carried = kernel_call(
        chain_states(reverse, blocks, size), [shape_of((blocks, size, LANES), bf16)], parts, wait=wait
    )[0]
    back = lax.all_to_all(carried, axis, 0, 0, tiled=True)
    return back.astype(f32).reshape(blocks * size, LANES)


def other(value, bit):
    count = lax.axis_size("tensor")
    return lax.ppermute(value, "tensor", [(rank, rank ^ bit) for rank in range(count)])


def place():
    x_size, z_size, y_size = DP_SHAPE
    index = lax.axis_index("dp")
    return index // (z_size * y_size), index // y_size % z_size, index % y_size


def shift(value, axis, step):
    x_size, z_size, y_size = DP_SHAPE
    pairs = []
    for x in range(x_size):
        for z in range(z_size):
            for y in range(y_size):
                to_x = (x + step) % x_size if axis == "x" else x
                to_z = (z + step) % z_size if axis == "z" else z
                to_y = (y + step) % y_size if axis == "y" else y
                pairs.append(((x * z_size + z) * y_size + y, (to_x * z_size + to_z) * y_size + to_y))
    return lax.ppermute(value, "dp", pairs)


RING = (0, -1, 1, 2)


def spread(pack, near, split):
    mids = []
    for columns, axis in ((slice(0, split), "y"), (slice(split, None), "x")):
        own = jnp.stack([pack[:, columns], near[:, columns]])
        back, ahead = shift(own, axis, 1), shift(own, axis, -1)
        far = [shift(back[:1], axis, 1), shift(ahead[1:], axis, -1)]
        mids.append((own, back, ahead, *far))
    return mids


def finish(mids):
    return [(mid, shift(mid, axis, 1), shift(mid, axis, -1)) for mid, axis in zip(mids, "xy", strict=True)]


def join_mids(cuts):
    def kernel(*refs):
        done = refs[-1]
        copies = []
        for half, cut in enumerate(cuts):
            at = 0
            out = refs[10 + half]
            for ref in refs[5 * half : 5 * half + 5]:
                copy = pltpu.make_async_copy(
                    ref.at[:, :, pl.ds(cut, out.shape[2])], out.at[pl.ds(at, ref.shape[0])], done.at[len(copies)]
                )
                copy.start()
                copies.append(copy)
                at += ref.shape[0]
        wait_all(copies)

    return kernel


def cut_far():
    def kernel(*refs):
        done = refs[-1]
        copies = []
        for index in range(4):
            out = refs[4 + index]
            half = out.shape[0]
            copy = pltpu.make_async_copy(refs[index].at[pl.ds((index % 2) * half, half)], out, done.at[index])
            copy.start()
            copies.append(copy)
        wait_all(copies)

    return kernel


def finish_cut(rings, wait):
    arrived = [part for ring in rings for part in ring[1:]]
    return kernel_call(
        cut_far(), [shape_of((part.shape[0] // 2, *part.shape[1:]), bf16) for part in arrived], *arrived,
        raw=range(4),
        scratch=[pltpu.SemaphoreType.DMA((4,))],
        wait=wait,
    )


def finish_far(rings, cut):
    pieces = []
    for half, axis in enumerate("xy"):
        pieces += [*rings[half], shift(cut[2 * half], axis, 1), shift(cut[2 * half + 1], axis, -1)]
    return pieces


SENT = 5


def cut_chunks(outs, rows_of, part):
    own, to_ahead, to_back, ahead_first, back_second = outs
    own[0:part, :] = rows_of(0, 0)
    own[part:, :] = rows_of(0, 1)
    to_ahead[0:part, :] = rows_of(2, 0)
    to_ahead[part:, :] = rows_of(1, 1)
    to_back[0:part, :] = rows_of(2, 1)
    to_back[part:, :] = rows_of(-1, 0)
    ahead_first[...] = rows_of(1, 0)
    back_second[...] = rows_of(-1, 1)


def chunk_shapes(part, widths):
    shapes = []
    for width in widths:
        shapes += [shape_of((2 * part, width), bf16)] * 3 + [shape_of((part, width), bf16)] * 2
    return shapes


def wrapped(index, step):
    return lax.rem(index + (step + 4), 4)


def term_products(plan, shard, prepare=None, joined=0):
    x_size, z_size, y_size = DP_SHAPE
    part = 4 * shard

    def kernel(here, *refs):
        count = len(refs) - 2 * SENT - 2 - (prepare is not None)
        arrays, outs, scratch = list(refs[:count]), refs[count : count + 2 * SENT], refs[-2:]
        if prepare is not None:
            prepare(arrays[count - joined :], refs[-3])
            arrays = [*arrays[: count - joined], refs[-3]]
        x, y = here[0], here[2]
        for half, terms in enumerate(plan):
            product = scratch[half]
            at = 0
            for lhs, rhs, first, last in terms:
                for start in range(first, last, 2 * LANES):
                    stop = min(start + 2 * LANES, last)
                    product[:, at : at + stop - start] = dot(
                        arrays[lhs][...], arrays[rhs][:, start:stop], TN
                    ).astype(bf16)
                    at += stop - start

            def along_x(step, side, product=product):
                row = (wrapped(x, step) * 2 + side) * part
                return product[pl.ds(pl.multiple_of(row, part), part), :]

            def along_y(step, side, product=product):
                groups = range(side * 4, side * 4 + 4)
                rows = [(group * y_size + wrapped(y, step)) * shard for group in groups]
                return jnp.concatenate([product[pl.ds(pl.multiple_of(row, 16), shard), :] for row in rows], 0)

            cut_chunks(outs[half * SENT : (half + 1) * SENT], along_x if half == 0 else along_y, part)

    return kernel


def ring_add(part):
    def kernel(*refs):
        for half in range(2):
            from_back, from_ahead, ahead_first, back_second = refs[4 * half : 4 * half + 4]
            ahead_out, back_out = refs[8 + 2 * half : 10 + 2 * half]
            ahead_out[...] = (ahead_first[...].astype(f32) + from_back[0:part, :].astype(f32)).astype(bf16)
            back_out[...] = (back_second[...].astype(f32) + from_ahead[0:part, :].astype(f32)).astype(bf16)

    return kernel


def ring_totals(refs, part):
    own, from_back, from_ahead, from_back_last, from_ahead_last = refs
    first = own[0:part, :].astype(f32) + from_ahead[part:, :].astype(f32) + from_back_last[...].astype(f32)
    second = own[part:, :].astype(f32) + from_back[part:, :].astype(f32) + from_ahead_last[...].astype(f32)
    return first, second


def ring_total():
    def kernel(*refs):
        for half in range(2):
            out = refs[2 * SENT + half]
            part = out.shape[0] // 2
            first, second = ring_totals(refs[half * SENT : (half + 1) * SENT], part)
            out[0:part, :] = first.astype(bf16)
            out[part:, :] = second.astype(bf16)

    return kernel


def ring_fold(shard):
    part = 4 * shard

    def kernel(here, *refs):
        x, y = here[0], here[2]
        ended, refs = refs[:2], refs[2:]
        outs, scratch = refs[2 * SENT : 4 * SENT], refs[4 * SENT :]
        for half in range(2):
            total = scratch[half]
            wide = ended[half].shape[1]
            total[:, :wide] = ended[half][...].astype(f32)
            total[0:part, wide:], total[part:, wide:] = ring_totals(refs[half * SENT : (half + 1) * SENT], part)

            def along_y(step, side, total=total):
                row = side * part + wrapped(y, step) * shard
                return total[pl.ds(pl.multiple_of(row, 16), shard), :].astype(bf16)

            def along_x(step, side, total=total):
                row = (wrapped(x, step) * 2 + side) * shard
                return total[pl.ds(pl.multiple_of(row, 16), shard), :].astype(bf16)

            cut_chunks(outs[half * SENT : (half + 1) * SENT], along_y if half == 0 else along_x, shard)

    return kernel


def ring_end(shard, widths):
    def kernel(here, *refs):
        z = here[1]
        mine_out, sent_out = refs[2 * SENT :]
        at = 0
        for half in range(2):
            first, second = ring_totals(refs[half * SENT : (half + 1) * SENT], shard)
            columns = slice(at, at + widths[half])
            mine_out[:, columns] = jnp.where(z == 0, first, second)
            sent_out[:, columns] = jnp.where(z == 0, second, first).astype(bf16)
            at += widths[half]

    return kernel


def ring_send(chunks, axes):
    arrived, stays = [], []
    for half, axis in enumerate(axes):
        own, to_ahead, to_back, ahead_first, back_second = chunks[half * SENT : (half + 1) * SENT]
        arrived += [shift(to_ahead, axis, 1), shift(to_back, axis, -1)]
        stays.append((own, ahead_first, back_second))
    return arrived, stays


def ring_added(arrived, stays, widths, part, wait=()):
    terms = []
    for half in range(2):
        terms += [*arrived[2 * half : 2 * half + 2], *stays[half][1:]]
    shapes = [shape_of((part, width), bf16) for width in widths for _ in range(2)]
    return kernel_call(ring_add(part), shapes, *terms, whole=True, wait=wait)


def ring_passed(arrived, stays, sent, axes):
    results = []
    for half, axis in enumerate(axes):
        last = [shift(sent[2 * half], axis, 1), shift(sent[2 * half + 1], axis, -1)]
        results += [stays[half][0], *arrived[2 * half : 2 * half + 2], *last]
    return results


def ring_pass(arrived, stays, widths, axes, part, wait=()):
    return ring_passed(arrived, stays, ring_added(arrived, stays, widths, part, wait), axes)


def widths_of(plan):
    return [sum(last - first for _, _, first, last in terms) for terms in plan]


def scatter_begin(here, plan, arrays, shard, prepare=None, joined=0, columns=0, wait=()):
    part = 4 * shard
    widths = widths_of(plan)
    shapes = chunk_shapes(part, widths)
    if prepare is not None:
        shapes.append(shape_of((arrays[0].shape[0], columns), bf16))
    return kernel_call(
        term_products(plan, shard, prepare, joined), shapes, here, *arrays,
        flops=sum(2 * arrays[0].shape[0] * 8 * part * width for width in widths),
        small=(0,),
        scratch=[pltpu.VMEM((8 * part, width), bf16) for width in widths],
        whole=True,
        wait=wait,
    )


def grad_blocks(plan, shard):
    def kernel(mine, got, *outs):
        for out, entries in zip(outs, plan, strict=True):
            for lead, first, at, columns in entries:
                value = mine[:, at : at + columns] + got[:, at : at + columns].astype(f32)
                if lead is None and len(out.shape) == 3:
                    side, begin = first // out.shape[2], first % out.shape[2]
                    out[:, side, begin : begin + columns] = value
                elif lead is None:
                    out[:, first : first + columns] = value
                else:
                    out[lead, :, first : first + columns] = value

    return kernel


EACH = 6


def small_rows(model_dim, inner, state, taps, ranks):
    wide, share = model_dim // LANES, inner // LANES
    sizes = {
        "norm": wide,
        "post": wide,
        "taps": taps * ranks * share,
        "bc": taps * 2 * state // LANES,
        "gain": ranks * share,
        "skip": ranks * share,
        "heads": 2 * ranks,
    }
    rows, at = {}, 0
    for name, size in sizes.items():
        rows[name] = at
        at += size
    return rows


def small_table(layout, inner, state, taps, heads):
    share = inner // LANES

    def kernel(here, norm, post, conv, gain, head, skip, out, table):
        rank = here[4] * 2 + here[3]
        ranks = (layout["skip"] - layout["gain"]) // share

        def lanes(i):
            return slice(i * LANES, (i + 1) * LANES)

        table[...] = jnp.zeros_like(table)
        for i in range(layout["post"] - layout["norm"]):
            table[layout["norm"] + i : layout["norm"] + i + 1, :] = norm[:, lanes(i)]
            table[layout["post"] + i : layout["post"] + i + 1, :] = post[:, lanes(i)]
        for i in range(share):
            for tap in range(taps):
                row = layout["taps"] + tap * ranks * share + rank * share + i
                table[pl.ds(row, 1), :] = conv[tap : tap + 1, lanes(i)]
            table[pl.ds(layout["gain"] + rank * share + i, 1), :] = gain[:, lanes(i)]
            table[pl.ds(layout["skip"] + rank * share + i, 1), :] = skip[:, lanes(i)]
        wide = 2 * state // LANES
        for tap in range(taps):
            for i in range(wide):
                row = layout["bc"] + tap * wide + i
                table[row : row + 1, :] = conv[tap : tap + 1, lanes(share + i)]
        for i in range(2):
            table[pl.ds(layout["heads"] + i * ranks + rank, 1), :] = head[i : i + 1, :]
        out[...] = jnp.zeros_like(out)
        for block in range(out.shape[0]):
            out[block, 0:EACH, :] = table[block * EACH : (block + 1) * EACH, :]

    return kernel


def small_sum():
    def kernel(parts, out):
        out[...] = jnp.broadcast_to(jnp.sum(parts[...], 0, keepdims=True), out.shape)

    return kernel


def small_out(layout, ranks, inner, state, taps):
    def kernel(parts, norm, post, conv_x, conv_bc, gain, skip, head, table):
        for block in range(parts.shape[0] // ranks):
            total = jnp.sum(parts[block * ranks : (block + 1) * ranks], 0)
            table[block * EACH : (block + 1) * EACH, :] = total[0:EACH, :]

        def spread_out(ref, line, first):
            for i in range(ref.shape[1] // LANES):
                ref[line : line + 1, i * LANES : (i + 1) * LANES] = table[first + i : first + i + 1, :]

        spread_out(norm, 0, layout["norm"])
        spread_out(post, 0, layout["post"])
        spread_out(gain, 0, layout["gain"])
        spread_out(skip, 0, layout["skip"])
        for tap in range(taps):
            spread_out(conv_x, tap, layout["taps"] + tap * (conv_x.shape[1] // LANES))
            spread_out(conv_bc, tap, layout["bc"] + tap * (conv_bc.shape[1] // LANES))
        head[...] = table[layout["heads"] : layout["heads"] + 2 * ranks, :]

    return kernel


def body(
    tokens,
    cotangent,
    segments,
    routes,
    gate_weights,
    norm_gain,
    w_zx,
    w_bc,
    w_dt,
    conv_x,
    conv_bc,
    dt_bias,
    a_log,
    d_skip,
    mix_gain,
    w_out,
    post_gain,
    exp_gate,
    exp_up,
    exp_down,
    sh_gate,
    sh_up,
    sh_down,
):
    tensor_count = lax.axis_size("tensor")
    tensor_rank = lax.axis_index("tensor")
    pair, core = tensor_rank // 2, tensor_rank % 2
    dp_count = lax.axis_size("dp")
    here = jnp.stack([*place(), core, pair]).astype(jnp.int32)
    quarter = tokens.shape[0]
    block_rows = segments.shape[0]
    model_dim = tokens.shape[1]
    shard = w_zx.shape[0]
    inner = w_zx.shape[2]
    heads = w_dt.shape[1]
    head_dim = inner // heads
    state = w_bc.shape[2]
    conv_taps = conv_x.shape[0]
    inner_total = inner * tensor_count
    head_total = heads * tensor_count
    experts = exp_gate.shape[0]
    ffe = exp_gate.shape[2]
    ffs = sh_gate.shape[1]
    hidden = experts * ffe + ffs
    wide_in = 2 * inner + 2 * state + LANES

    shards = [
        w_zx,
        w_bc,
        w_dt,
        w_out.T,
        exp_gate,
        sh_gate,
        exp_up,
        sh_up,
        exp_down.transpose(0, 2, 1),
        sh_down.T,
    ]
    in_columns, mix_columns, rest_columns = wide_in, wide_in + inner, 3 * hidden
    in_split, rest_split = mix_columns // 256 * LANES, rest_columns // 256 * LANES
    plan, pack_columns = pack_plan(shards, 4, in_split, rest_split)
    pack = kernel_call(pack_blocks(plan, pack_columns), [shape_of((shard, pack_columns), bf16)], *shards, alone=True)[0]
    near = shift(pack, "z", 1)
    mids = spread(pack, near, in_split + rest_split)
    cuts = (in_split, mix_columns - in_split)
    in_mids = [
        jnp.concatenate([part[:, :, :cut] for part in parts], 0) for parts, cut in zip(mids, cuts, strict=True)
    ]
    in_rings = finish(in_mids)
    rows_all = lax.all_gather(tokens, "tensor", axis=0, tiled=True)
    cot_all = lax.all_gather(cotangent, "tensor", axis=0, tiled=True)
    seg_lanes = jnp.broadcast_to(segments.astype(f32)[:, None], (block_rows, LANES))
    normed_in, normed_own, tail_sent = kernel_call(
        input_rows(quarter),
        [
            shape_of((block_rows, model_dim), bf16),
            shape_of((quarter, model_dim), bf16),
            shape_of((EDGE, model_dim + LANES), bf16),
        ],
        here, rows_all, seg_lanes, norm_gain[None, :],
        small=(0,),
    )
    tail_rows = from_behind(tail_sent, "dp", 1)
    head_start = tensor_rank * heads
    chan_start = tensor_rank * inner
    bias_local = lax.dynamic_slice_in_dim(dt_bias, head_start, heads)
    alog_local = lax.dynamic_slice_in_dim(a_log, head_start, heads)
    skip_local = lax.dynamic_slice_in_dim(d_skip, head_start, heads)
    gain_row = lax.dynamic_slice_in_dim(mix_gain, chan_start, inner)[None, :]
    convx_local = lax.dynamic_slice_in_dim(conv_x, chan_start, inner, 1)
    taps = jnp.concatenate([convx_local, conv_bc.reshape(conv_taps, 2 * state)], 1)
    taps = jnp.pad(taps, ((0, conv_taps), (0, 0)))
    bias_row = jnp.pad(bias_local, (0, LANES - heads))[None, :]
    alog_row = jnp.pad(alog_local, (0, LANES - heads))[None, :]
    skip_row = jnp.repeat(skip_local, head_dim)[None, :]

    hot = routes[:, :, None] == jnp.arange(LANES, dtype=jnp.int32)[None, None, :]
    share = jnp.sum(jnp.where(hot, gate_weights[:, :, None], 0.0), 1)
    early = (tail_rows, taps, bias_row, alog_row, skip_row, gain_row, share)
    in_pieces = finish_far(in_rings, finish_cut(in_rings, early))
    rest_mids = kernel_call(
        join_mids(cuts),
        [shape_of((8, shard, parts[0].shape[2] - cut), bf16) for parts, cut in zip(mids, cuts, strict=True)],
        *[part for parts in mids for part in parts],
        raw=range(10),
        alone=True,
        scratch=[pltpu.SemaphoreType.DMA((10,))],
        wait=in_pieces,
    )
    rest_rings = finish(rest_mids)
    rest_cut = finish_cut(rest_rings, ())
    rest_pieces = finish_far(rest_rings, rest_cut)

    scan_flops = 2 * block_rows * block_rows * inner * 2
    size = inner // dp_count
    state_shape = shape_of((dp_count, size + SUB, state))
    proj, lags, y_first, conv, cum, steps, state_sum = kernel_call(
        scan_front(heads, inner, state, shard, column_ranges(in_split, 0, in_columns)),
        [
            shape_of((block_rows + EDGE, in_columns)),
            shape_of((block_rows, LANES)),
            shape_of((block_rows, inner)),
            shape_of((block_rows, inner + 2 * state)),
            shape_of((block_rows, LANES)),
            shape_of((block_rows, LANES)),
            state_shape,
        ],
        here, normed_in, tail_rows, taps, seg_lanes, bias_row, alog_row, skip_row, *in_pieces,
        flops=scan_flops + 2 * block_rows * model_dim * in_columns,
        small=(0,),
        raw=range(8, 8 + len(in_pieces)),
        scratch=[
            pltpu.VMEM((block_rows, inner + 2 * state), f32),
            pltpu.VMEM((inner, state), f32),
            pltpu.VMEM((model_dim, in_columns), bf16),
            pltpu.VMEM((block_rows + EDGE, LANES), f32),
            pltpu.SemaphoreType.DMA((64,)),
        ],
    )
    entering = exchange_states(state_sum, size, "dp", False, rest_mids)
    w_back, y_all, mixer_in, mine, theirs = kernel_call(
        gate_front(heads, inner, state, shard, column_ranges(in_split, in_columns, in_columns + inner)),
        [
            shape_of((model_dim, inner), bf16),
            shape_of((block_rows, inner)),
            shape_of((block_rows, inner), bf16),
            shape_of((2 * quarter, model_dim + LANES)),
            shape_of((2 * quarter, model_dim + LANES)),
        ],
        here, y_first, proj, conv, cum, entering, gain_row, *in_pieces,
        flops=scan_flops,
        small=(0,),
        raw=range(7, 7 + len(in_pieces)),
        scratch=[
            pltpu.VMEM((block_rows, inner), bf16),
            pltpu.VMEM((block_rows, model_dim + LANES), f32),
            pltpu.SemaphoreType.DMA((64,)),
        ],
    )
    core_total, sent = kernel_call(
        core_sum(model_dim),
        [shape_of((2 * quarter, model_dim)), shape_of((2 * quarter, model_dim + LANES), bf16)],
        mine, other(theirs, 1),
        wait=[ring[1:] for ring in rest_rings],
    )
    from_pair = other(sent, 2)
    middle, post_mine, scales = kernel_call(
        middle_rows(quarter, model_dim, inner_total),
        [
            shape_of((2 * quarter, model_dim)),
            shape_of((2 * quarter, model_dim), bf16),
            shape_of((2 * quarter, LANES)),
        ],
        here, sent, from_pair, rows_all, post_gain[None, :],
        small=(0,),
    )
    post_theirs = other(post_mine, 1)
    half_shape = (2 * quarter, model_dim)
    post, cot, act, d_pre, ffn_mine, ffn_theirs, dpost_mine, dpost_theirs = kernel_call(
        experts_both(quarter, hidden, ffe, experts, shard, column_ranges(rest_split, 0, 3 * hidden)),
        [
            shape_of((block_rows, model_dim), bf16),
            shape_of((block_rows, model_dim), bf16),
            shape_of((block_rows, hidden), bf16),
            shape_of((block_rows, 2 * hidden), bf16),
            shape_of(half_shape),
            shape_of(half_shape, bf16),
            shape_of(half_shape),
            shape_of(half_shape, bf16),
        ],
        here, post_mine, post_theirs, cot_all, share, *rest_pieces,
        flops=12 * block_rows * model_dim * hidden,
        small=(0,),
        raw=range(5, 5 + len(rest_pieces)),
        scratch=[
            pltpu.VMEM((model_dim, 3 * hidden), bf16),
            pltpu.VMEM((block_rows, LANES), f32),
            pltpu.VMEM((block_rows, hidden), f32),
            pltpu.VMEM((block_rows, hidden), f32),
            pltpu.SemaphoreType.DMA((64,)),
        ],
    )
    ffn_split = (3 * hidden) // 256 * LANES
    ffn_plan = (((0, 2, 0, ffn_split),), ((0, 2, ffn_split, 2 * hidden), (1, 3, 0, hidden)))
    sent_post = kernel_call(add_round(), [shape_of(half_shape, bf16)], dpost_mine, other(dpost_theirs, 1))[0]
    ffn_chunks = scatter_begin(here, ffn_plan, (post, cot, d_pre, act), shard)
    ffn_sent, ffn_terms = ring_send(ffn_chunks, "xy")
    d_middle, back_mine, grad_post_gain = kernel_call(
        middle_back(quarter, model_dim, inner_total),
        [
            shape_of(half_shape),
            shape_of((2 * quarter, model_dim + LANES), bf16),
            shape_of((1, model_dim)),
        ],
        here, sent_post, other(sent_post, 2), cot_all, middle, scales, core_total, from_pair,
        post_gain[None, :],
        small=(0,),
    )
    back_theirs = other(back_mine, 1)
    d_proj, d_y, d_z, grad_gain, d_enter = kernel_call(
        gate_back(heads, inner, state),
        [
            shape_of((block_rows, model_dim), bf16),
            shape_of((block_rows, inner)),
            shape_of((block_rows, inner), bf16),
            shape_of((1, inner)),
            state_shape,
        ],
        here, back_mine, back_theirs, w_back, y_all, proj, conv, cum, gain_row,
        flops=scan_flops,
        small=(0,),
        scratch=[
            pltpu.VMEM((inner, state), f32),
            pltpu.VMEM((block_rows, LANES), f32),
            pltpu.VMEM((block_rows, inner), f32),
        ],
    )

    ffn_own, ffn_away = kernel_call(
        add_split(quarter),
        [shape_of((quarter, model_dim)), shape_of((quarter, model_dim), bf16)],
        here, ffn_mine, other(ffn_theirs, 1),
        small=(0,),
    )
    block_out = kernel_call(
        layer_out(quarter),
        [shape_of((quarter, model_dim))],
        here, ffn_own, other(ffn_away, 2), middle,
        small=(0,),
    )[0]

    leaving = exchange_states(d_enter, size, "dp", True)
    ffn_widths = widths_of(ffn_plan)
    ffn_added = ring_added(ffn_sent, ffn_terms, ffn_widths, 4 * shard)
    d_x, d_bc, tail, d_dt, grad_taps, grad_heads, grad_skip = kernel_call(
        scan_back(heads, inner, state),
        [
            shape_of((block_rows, inner)),
            shape_of((block_rows, 2 * state)),
            shape_of((EDGE, inner + 2 * state)),
            shape_of((block_rows, LANES), bf16),
            shape_of((SUB, inner + 2 * state)),
            shape_of((SUB, LANES)),
            shape_of((1, inner)),
        ],
        proj, taps, lags, bias_row, alog_row, skip_row, conv, cum, steps, d_y, entering, leaving,
        flops=3 * scan_flops,
        wait=ffn_added,
        scratch=[
            pltpu.VMEM((block_rows, inner + 2 * state), f32),
            pltpu.VMEM((LANES, block_rows), f32),
            pltpu.VMEM((block_rows + EDGE, inner + 2 * state), f32),
        ],
    )
    tail = from_behind(tail, "dp", -1)
    ffn_rings = ring_passed(ffn_sent, ffn_terms, ffn_added, "xy")
    ffn_totals = kernel_call(
        ring_total(), [shape_of((8 * shard, width), bf16) for width in ffn_widths], *ffn_rings, whole=True
    )
    bc_half = shape_of((block_rows, state))
    bc_mine, bc_theirs = kernel_call(
        bc_split(state, inner),
        [bc_half] * 2,
        here, d_bc, tail,
        small=(0,),
        scratch=[pltpu.VMEM((block_rows, 2 * state), f32)],
    )
    bc_sum = kernel_call(add_exact(), [bc_half], bc_mine, other(bc_theirs, 1))[0]
    dt_at = 2 * inner
    bc_at = dt_at + LANES
    out_at = bc_at + state
    mix_split = (out_at + inner) // 256 * LANES
    mix_plan = (((0, 3, 0, mix_split),), ((0, 3, mix_split, out_at), (1, 2, 0, inner)))
    mix_widths = widths_of(mix_plan)
    *mix_chunks, d_all = scatter_begin(
        here, mix_plan,
        (normed_in, d_proj, mixer_in, d_z, d_x, tail, d_dt, bc_sum, other(bc_sum, 2)),
        shard, join_grads(inner), 6, out_at, ffn_totals,
    )
    mix_sent, mix_terms = ring_send(mix_chunks, "xy")
    din_mine, din_theirs, grad_norm = kernel_call(
        input_back(quarter, inner, state, shard, column_ranges(in_split, 0, in_columns)),
        [shape_of(half_shape), shape_of(half_shape, bf16), shape_of((1, model_dim))],
        here, d_all, rows_all, *in_pieces,
        flops=2 * block_rows * model_dim * in_columns,
        small=(0,),
        raw=range(3, 3 + len(in_pieces)),
        scratch=[
            pltpu.VMEM((block_rows, model_dim), f32),
            pltpu.VMEM((model_dim, in_columns), bf16),
            pltpu.SemaphoreType.DMA((64,)),
        ],
    )
    din_own, din_sent = kernel_call(
        add_split(quarter),
        [shape_of((quarter, model_dim)), shape_of((quarter, model_dim), bf16)],
        here, din_mine, other(din_theirs, 1),
        small=(0,),
    )
    grad_tokens = kernel_call(
        input_grad(quarter),
        [shape_of((quarter, model_dim))],
        here, din_own, other(din_sent, 2), tokens, d_middle, norm_gain[None, :],
        small=(0,),
    )[0]
    layout = small_rows(model_dim, inner, state, conv_taps, tensor_count)
    table_shape = shape_of((dp_count, SUB, LANES))
    table = kernel_call(
        small_table(layout, inner, state, conv_taps, heads),
        [table_shape],
        here, grad_norm, grad_post_gain, grad_taps, grad_gain, grad_heads, grad_skip,
        small=(0,),
        scratch=[pltpu.VMEM((dp_count * EACH, LANES), f32)],
    )[0]
    table = lax.all_to_all(table, "dp", 0, 0, tiled=True)
    mix_rings = ring_pass(mix_sent, mix_terms, mix_widths, "xy", 4 * shard, (grad_tokens, block_out))
    devices = dp_count * tensor_count
    table = kernel_call(small_sum(), [shape_of((devices, SUB, LANES))], table)[0]
    table_end = lax.all_to_all(table, ("dp", "tensor"), 0, 0, tiled=True)
    small = kernel_call(
        small_out(layout, tensor_count, inner, state, conv_taps),
        [
            shape_of((1, model_dim)),
            shape_of((1, model_dim)),
            shape_of((conv_taps, inner_total)),
            shape_of((conv_taps, 2 * state)),
            shape_of((1, inner_total)),
            shape_of((1, inner_total)),
            shape_of((2 * tensor_count, LANES)),
        ],
        table_end,
        scratch=[pltpu.VMEM((dp_count * EACH, LANES), f32)],
    )
    norm_sum, post_sum, taps_x, taps_bc, gain_sum, skip_sum, head_sums = small
    head_grads = head_sums.reshape(2, tensor_count, LANES)[:, :, :heads].reshape(2, -1)
    small_outs = (
        norm_sum[0],
        post_sum[0],
        head_grads[0],
        head_grads[1],
        jnp.sum(skip_sum.reshape(head_total, head_dim), 1),
        gain_sum[0],
    )
    widths = [one + two for one, two in zip(ffn_widths, mix_widths, strict=True)]
    chunks = kernel_call(
        ring_fold(shard), chunk_shapes(shard, widths), here, *ffn_totals, *mix_rings,
        small=(0,),
        scratch=[pltpu.VMEM((8 * shard, width), f32) for width in widths],
        whole=True,
        wait=table,
    )
    sent, terms = ring_send(chunks, "yx")
    results = ring_pass(sent, terms, widths, "yx", shard, table_end)
    sum_shape = (shard, sum(widths))
    mine, sent = kernel_call(
        ring_end(shard, widths), [shape_of(sum_shape), shape_of(sum_shape, bf16)], here, *results,
        small=(0,),
        whole=True,
    )
    def found(group, first, columns):
        ffn_wide, mix_wide = ffn_widths[0], mix_widths[0]
        entries = []
        for at in range(first, first + columns, LANES):
            half, shift_by = (0, 0) if at < (ffn_wide, mix_wide)[group] else (1, (ffn_wide, mix_wide)[group])
            begin = half * widths[0] + (ffn_widths[half] if group else 0)
            entries.append((at - first, begin + at - shift_by, LANES))
        return entries

    def plain(group, first, columns):
        return [(None, *entry) for entry in found(group, first, columns)]

    def by_expert(first):
        entries = found(0, first, experts * ffe)
        return [(at // ffe, at % ffe, begin, columns) for at, begin, columns in entries]

    wide_e = experts * ffe
    out_plan = [
        plain(1, 0, 2 * inner),
        plain(1, dt_at, LANES),
        plain(1, bc_at, state),
        plain(1, out_at, inner),
        by_expert(0),
        by_expert(hidden),
        by_expert(2 * hidden),
        plain(0, wide_e, ffs),
        plain(0, hidden + wide_e, ffs),
        plain(0, 2 * hidden + wide_e, ffs),
    ]
    grad_zx, grad_dt, bc_half, grad_out, grad_eg, grad_eu, grad_ed, grad_sg, grad_su, grad_sd = kernel_call(
        grad_blocks(out_plan, shard),
        [
            shape_of((shard, 2, inner)),
            shape_of((shard, LANES)),
            shape_of((shard, state)),
            shape_of((shard, inner)),
            *[shape_of((experts, shard, ffe))] * 3,
            *[shape_of((shard, ffs))] * 3,
        ],
        mine, shift(sent, "z", 1),
        wait=small_outs,
    )
    bc_far = other(bc_half, 1)
    grad_bc = jnp.stack([jnp.where(core == 0, bc_half, bc_far), jnp.where(core == 0, bc_far, bc_half)], 1)
    return (
        block_out,
        grad_tokens,
        small_outs[0],
        grad_zx,
        grad_bc,
        grad_dt[:, :heads],
        taps_x,
        taps_bc.reshape(conv_taps, 2, state),
        small_outs[2],
        small_outs[3],
        small_outs[4],
        small_outs[5],
        grad_out.T,
        small_outs[1],
        grad_eg,
        grad_eu,
        grad_ed.transpose(0, 2, 1),
        grad_sg,
        grad_su,
        grad_sd.T,
    )


def solution(mesh):
    in_specs = (
        P(("dp", "tensor"), None),
        P(("dp", "tensor"), None),
        P("dp"),
        P("dp", None),
        P("dp", None),
        P(),
        P("dp", None, "tensor"),
        P("dp", None, None),
        P("dp", "tensor"),
        P(),
        P(),
        P(),
        P(),
        P(),
        P(),
        P("tensor", "dp"),
        P(),
        P(None, "dp", "tensor"),
        P(None, "dp", "tensor"),
        P(None, "tensor", "dp"),
        P("dp", "tensor"),
        P("dp", "tensor"),
        P("tensor", "dp"),
    )
    out_specs = (
        P(("dp", "tensor"), None),
        P(("dp", "tensor"), None),
        P(),
        P("dp", None, "tensor"),
        P("dp", None, None),
        P("dp", "tensor"),
        P(),
        P(),
        P(),
        P(),
        P(),
        P(),
        P("tensor", "dp"),
        P(),
        P(None, "dp", "tensor"),
        P(None, "dp", "tensor"),
        P(None, "tensor", "dp"),
        P("dp", "tensor"),
        P("dp", "tensor"),
        P("tensor", "dp"),
    )
    return jax.shard_map(body, mesh=mesh, in_specs=in_specs, out_specs=out_specs, check_vma=False)
```
